32 devices in a mesh: seq: 8 (over y, x, core), fsdp: 4 (over z).
Axes of the slice: x: 2, y: 2, z: 4, core: 2. Of those that a mesh axis runs over, the one named last changes fastest.
Arguments:
- inputs: bfloat16 [2, 4, 512, 2048], P(None, 'fsdp', 'seq'), may hold values from -6 to 6
- cotangent: bfloat16 [2, 4, 512, 2048], P(None, 'fsdp', 'seq'), may hold values from -6 to 6
- block_ids: int32 [2, 4, 512], P(None, 'fsdp'), may hold values from 0 to 3, never falling along the last dimension, each value on 1 to 256 neighbouring positions
- ln1_gain: bfloat16 [2048], P(('seq', 'fsdp')), may hold values from 0.5 to 1.5
- ln1_bias: bfloat16 [2048], P(('seq', 'fsdp')), may hold values from -1 to 1
- qkv_weight: bfloat16 [2048, 6144], P(('seq', 'fsdp')), may hold values from -0.125 to 0.125
- qkv_bias: bfloat16 [6144], P(('seq', 'fsdp')), may hold values from -0.5 to 0.5
- out_weight: bfloat16 [2048, 2048], P(('seq', 'fsdp')), may hold values from -1 to 1
- ln2_gain: bfloat16 [2048], P(('seq', 'fsdp')), may hold values from 0.5 to 1.5
- ln2_bias: bfloat16 [2048], P(('seq', 'fsdp')), may hold values from -1 to 1
- gate_weight: bfloat16 [2048, 5632], P(('seq', 'fsdp')), may hold values from -0.125 to 0.125
- up_weight: bfloat16 [2048, 5632], P(('seq', 'fsdp')), may hold values from -0.125 to 0.125
- down_weight: bfloat16 [5632, 2048], P(('seq', 'fsdp')), may hold values from -0.078125 to 0.078125
Outputs:
- layer_out: bfloat16 [2, 4, 512, 2048], P(None, 'fsdp', 'seq')
- input_grad: bfloat16 [2, 4, 512, 2048], P(None, 'fsdp', 'seq')
- ln1_gain_grad: float32 [2048], P(('seq', 'fsdp'))
- ln1_bias_grad: float32 [2048], P(('seq', 'fsdp'))
- qkv_weight_grad: float32 [2048, 6144], P(('seq', 'fsdp'))
- qkv_bias_grad: float32 [6144], P(('seq', 'fsdp'))
- out_weight_grad: float32 [2048, 2048], P(('seq', 'fsdp'))
- ln2_gain_grad: float32 [2048], P(('seq', 'fsdp'))
- ln2_bias_grad: float32 [2048], P(('seq', 'fsdp'))
- gate_weight_grad: float32 [2048, 5632], P(('seq', 'fsdp'))
- up_weight_grad: float32 [2048, 5632], P(('seq', 'fsdp'))
- down_weight_grad: float32 [5632, 2048], P(('seq', 'fsdp'))
The draws below stay inside these ranges and needn't reach their ends.
Inputs may be any that keep to these rules, and one draw needn't show every extreme that they name: `block_ids`: along each sequence the block ids never fall; each block holds 1 to 256 tokens.
All inputs are finite; a program needn't handle non-finite values.
Results may differ from the reference program's by a relative error of at most 0.014.
Values may be sent and summed in bfloat16 or wider, within the bound.
No kernel may reach another device: no remote copies, remote signals or barrier semaphores. Data moves between devices by JAX's collectives and lax.ppermute only.
A program may use at most 448 MiB of HBM per device.

```python
import math
import jax
import jax.numpy as jnp
import numpy as np
from jax import lax

D = 2048
H = 32
HD = 64
FF = 5632
ROT = 16
BLK = 256
MICRO = 2
SEQS = 4
LENGTH = 512


def level_of(key, dims, cuts, least, high):
    level, own = 1.0, jax.random.fold_in(key, 6)
    for dim, blocks in cuts:
        steps = jnp.exp(jax.random.uniform(jax.random.fold_in(own, dim), (blocks,), jnp.float32, least / len(cuts), high / len(cuts)))
        level = level * jnp.repeat(steps, dims[dim] // blocks).reshape([-1 if axis == dim else 1 for axis in range(len(dims))])
    return level


def split_up(count, total, limit, skew):
    portions = [(1 << 20) // math.isqrt(rank ** skew) + 1 for rank in range(2, count + 1)]
    surplus, given = total - limit - (count - 1), [1] * (count - 1)
    while surplus > 0:
        candidates = [i for i in range(count - 1) if given[i] < limit]
        whole, budget = sum([portions[i] for i in candidates]), surplus
        for i in candidates:
            addition = min(limit - given[i], max(1, budget * portions[i] // whole), surplus)
            given[i] = given[i] + addition
            surplus = surplus - addition
    return np.array([limit] + given)


def uneven_parts(rng, number_of, total, bound, lean):
    if number_of == 2:
        one = jax.random.randint(rng, (), max(1, total - bound), min(bound, total - 1) + 1)
        return jnp.stack([one, total - one])
    lengths = jnp.asarray(split_up(number_of, total, bound, lean), jnp.int32)
    twos = (number_of - 1) // 2
    donor, taker = lengths[1:1 + 2 * twos:2], lengths[2:2 + 2 * twos:2]
    margin = jnp.minimum(donor - 1, bound - taker)
    shifted = jax.random.randint(jax.random.fold_in(rng, 1), (twos,), 0, 1 << 20) % (margin + 1)
    lengths = lengths.at[1:1 + 2 * twos:2].set(donor - shifted).at[2:2 + 2 * twos:2].set(taker + shifted)
    return lengths[jax.random.permutation(jax.random.fold_in(rng, 2), number_of)]


def normal_values(rng, extent, deviation, most, shards=(), held_as=jnp.bfloat16):
    drawn = jax.random.normal(rng, extent, jnp.float32) * deviation
    if len(shards) > 0:
        drawn = level_of(rng, extent, shards, -0.22, 0.18) * drawn
    return jnp.clip(drawn, min=-most, max=most).astype(held_as)


def setup_inputs(seed: int = 0) -> dict:
    splits = jax.random.split(jax.random.key(seed), 14)
    return {
        "inputs": normal_values(splits[0], (MICRO, SEQS, LENGTH, D), 1.0, 6.0, ((1, 4), (2, 8))),
        "cotangent": normal_values(splits[1], (MICRO, SEQS, LENGTH, D), 1.0, 6.0, ((1, 4), (2, 8))),
        "block_ids": jax.vmap(lambda own: jnp.searchsorted(jnp.cumsum(uneven_parts(own, 2 * LENGTH // BLK, LENGTH, BLK, 0)), jnp.arange(LENGTH), side="right"))(jax.random.split(splits[2], MICRO * SEQS)).reshape((MICRO, SEQS, LENGTH)).astype(jnp.int32),
        "ln1_gain": jnp.clip(1.0 + 0.1 * jax.random.normal(splits[3], (D,), jnp.float32), 0.5, 1.5).astype(jnp.bfloat16),
        "ln1_bias": normal_values(splits[4], (D,), 0.2, 1.0, ((0, 32),)),
        "qkv_weight": normal_values(splits[5], (D, 3 * D), D ** -0.5, 0.125, ((0, 32),)),
        "qkv_bias": normal_values(splits[6], (3 * D,), 0.1, 0.5, ((0, 32),)),
        "out_weight": normal_values(splits[7], (D, D), (D // 64) ** -0.5, 1.0, ((0, 32),)),
        "ln2_gain": jnp.clip(1.0 + 0.1 * jax.random.normal(splits[8], (D,), jnp.float32), 0.5, 1.5).astype(jnp.bfloat16),
        "ln2_bias": normal_values(splits[9], (D,), 0.2, 1.0, ((0, 32),)),
        "gate_weight": normal_values(splits[10], (D, FF), D ** -0.5, 0.125, ((0, 32),)),
        "up_weight": normal_values(splits[11], (D, FF), D ** -0.5, 0.125, ((0, 32),)),
        "down_weight": normal_values(splits[12], (FF, D), FF ** -0.5, 0.078125, ((0, 32),)),
    }


@jax.custom_vjp
def low(v):
    return lax.optimization_barrier(v.astype(jnp.bfloat16)).astype(jnp.float32)

@jax.custom_vjp
def low_back(v):
    return v

def low_keep(v):
    return (low(v), None)

def low_pass(kept, grad):
    return (grad,)

def back_keep(v):
    return (v, None)

def back_low(kept, grad):
    return (low(grad),)
low.defvjp(low_keep, low_pass)
low_back.defvjp(back_keep, back_low)
eps_norm = 1e-05
rope_base = 10000.0
masked_score = -1e+30
highest = lax.Precision.HIGHEST

def layer_norm(values, scale_gain, offset):
    average = lax.optimization_barrier(jnp.mean(values, axis=-1, keepdims=True))
    centered = values - average
    spread = lax.optimization_barrier(jnp.mean(centered * centered, axis=-1, keepdims=True))
    return centered * lax.rsqrt(spread + eps_norm) * scale_gain + offset

def rotary(values, positions):
    half_rot = ROT // 2
    frequency = rope_base ** (-2.0 * jnp.arange(half_rot).astype(jnp.float32) / ROT)
    angles = positions.astype(jnp.float32)[:, None] * frequency[None, :]
    cosine = jnp.cos(angles)[:, None, :]
    sine_part = jnp.sin(angles)[:, None, :]
    front_part = values[..., :half_rot]
    back_part = values[..., half_rot:ROT]
    return jnp.concatenate([front_part * cosine - back_part * sine_part, back_part * cosine + front_part * sine_part, values[..., ROT:]], axis=-1)

def attend(queries, keys_all, values, blocks):
    length_all = queries.shape[0]
    block_rows = min(512, length_all)
    block_count = length_all // block_rows
    query_blocks = queries.reshape(block_count, block_rows, H, HD)
    id_blocks = blocks.reshape(block_count, block_rows)
    scaling = HD ** (-0.5)

    def one_block(pieces):
        query_rows, row_ids = pieces
        scores = low_back(jnp.einsum('qhd,khd->hqk', query_rows, keys_all, precision=highest) * scaling)
        allowed = row_ids[None, :, None] >= blocks[None, None, :]
        weights = jax.nn.softmax(jnp.where(allowed, scores, masked_score), axis=-1)
        return jnp.einsum('hqk,khd->qhd', low(weights), values, precision=highest)
    outputs = lax.map(jax.checkpoint(one_block), (query_blocks, id_blocks))
    return outputs.reshape(length_all, H, HD)

def layer(tokens, blocks, params):
    gain_one, offset_one, weight_qkv, bias_qkv, weight_out, gain_two, offset_two, weight_gate, weight_up, weight_down = params
    length_all = tokens.shape[0]
    hidden = low(layer_norm(tokens, gain_one, offset_one))
    linear = low_back(jnp.dot(hidden, weight_qkv, precision=highest) + bias_qkv).reshape(length_all, H, 3, HD)
    positions = jnp.arange(length_all).astype(jnp.int32)
    queries = low(rotary(linear[:, :, 0], positions))
    keys_all = low(rotary(linear[:, :, 1], positions))
    values = low(linear[:, :, 2])
    attended = low_back(low(attend(queries, keys_all, values, blocks))).reshape(length_all, D)
    mixed_sum = tokens + low_back(jnp.dot(attended, weight_out, precision=highest))
    hidden_two = low(layer_norm(mixed_sum, gain_two, offset_two))
    gate_value = low_back(jnp.dot(hidden_two, weight_gate, precision=highest))
    up_value = low_back(jnp.dot(hidden_two, weight_up, precision=highest))
    active = low(jax.nn.silu(gate_value) * up_value)
    return mixed_sum + jnp.dot(active, weight_down, precision=highest)

def reference(inputs, cotangent, block_ids, ln1_gain, ln1_bias, qkv_weight, qkv_bias, out_weight, ln2_gain, ln2_bias, gate_weight, up_weight, down_weight):
    params = tuple((weight_array.astype(jnp.float32) for weight_array in (ln1_gain, ln1_bias, qkv_weight, qkv_bias, out_weight, ln2_gain, ln2_bias, gate_weight, up_weight, down_weight)))
    sequences = inputs.astype(jnp.float32).reshape(MICRO * SEQS, LENGTH, D)
    seq_blocks = block_ids.reshape(MICRO * SEQS, LENGTH)

    def forward(all_tokens, all_params):
        return lax.map(lambda pieces: layer(pieces[0], pieces[1], all_params), (all_tokens, seq_blocks))
    results, pullback = jax.vjp(forward, sequences, params)
    token_grads, param_grads = pullback(cotangent.astype(jnp.float32).reshape(MICRO * SEQS, LENGTH, D))
    shape_all = inputs.shape
    return (results.reshape(shape_all).astype(jnp.bfloat16), token_grads.reshape(shape_all).astype(jnp.bfloat16), param_grads[0], param_grads[1], param_grads[2], param_grads[3], param_grads[4], param_grads[5], param_grads[6], param_grads[7], param_grads[8], param_grads[9])
```

```python
import jax
import jax.numpy as jnp
import numpy as np
from jax import lax
from jax.sharding import Mesh
from jax.sharding import PartitionSpec as P

H = 32
HD = 64
ROT = 16

eps_norm = 1e-05
rope_base = 10000.0
masked_score = -1e30

F32 = jnp.float32
BF16 = jnp.bfloat16

SWAP = [(0, 1), (1, 0)]
EVERY = ("sb", "sr", "fh", "fl")
MEMBERS = ("sr", "fl")


def swap_sb(v):
    return lax.ppermute(v, "sb", SWAP)


def swap_fh(v):
    return lax.ppermute(v, "fh", SWAP)


def swap_fl(v):
    return lax.ppermute(v, "fl", SWAP)


def swap_sr(v, bit):
    n = lax.axis_size("sr")
    return lax.ppermute(v, "sr", [(i, i ^ bit) for i in range(n)])


def norm_stats(values):
    average = jnp.mean(values, axis=-1, keepdims=True)
    centered = values - average
    inv_std = lax.rsqrt(jnp.mean(centered * centered, axis=-1, keepdims=True) + eps_norm)
    return (centered * inv_std, inv_std)


def norm_back(grad_normed, normed, inv_std):
    first_mean = jnp.mean(grad_normed, axis=-1, keepdims=True)
    second_mean = jnp.mean(grad_normed * normed, axis=-1, keepdims=True)
    return inv_std * (grad_normed - first_mean - normed * second_mean)


def gather_tokens(x):
    m = x.shape[0]
    h = m // 2
    a = swap_sr(x, 2)
    b = swap_fl(x)
    xo = swap_sr(x, 1)
    d1 = swap_fl(a[:h])
    d2 = swap_sr(b[h:], 2)
    ao = swap_sr(a, 1)
    bo = swap_sr(b, 1)
    d = jnp.concatenate([d1, d2], 0)
    do = swap_sr(d, 1)
    got = jnp.stack([x, xo, a, ao, b, bo, d, do]).reshape((2, 4) + x.shape)
    bit = 4
    while bit < lax.axis_size("sr"):
        got = jnp.concatenate([got, swap_sr(got, bit)], axis=1)
        bit *= 2
    return got


def scatter_tokens(p):
    bit = lax.axis_size("sr") // 2
    while bit >= 4:
        p = (p[:, :bit].astype(F32) + swap_sr(p[:, bit:], bit).astype(F32)).astype(BF16)
        bit //= 2
    m, width = p.shape[2:]
    h = m // 2
    p = p.reshape(2, 2, 2, m, width)
    q = p[:, :, 0].astype(F32) + swap_sr(p[:, :, 1], 1).astype(F32)
    qb = q.astype(BF16)
    u = q[:, 0, :h] + swap_sr(qb[:, 1, :h], 2).astype(F32)
    w = q[0, :, h:] + swap_fl(qb[1, :, h:]).astype(F32)
    top = u[0] + swap_fl(u[1].astype(BF16)).astype(F32)
    bottom = w[0] + swap_sr(w[1].astype(BF16), 2).astype(F32)
    return jnp.concatenate([top, bottom], 0)


def flip_if(bit, v, axis):
    return jnp.where(bit == 1, lax.rev(v, (axis,)), v)


def gather_groups(w):
    sb, fh = lax.axis_index("sb"), lax.axis_index("fh")
    z = swap_fh(w)
    yw = swap_sb(w)
    yz = swap_sb(z)
    low = jnp.where(fh == 1, z, w)
    high = jnp.where(fh == 1, w, z)
    ylow = jnp.where(fh == 1, yz, yw)
    yhigh = jnp.where(fh == 1, yw, yz)
    return jnp.stack(
        [
            jnp.stack([jnp.where(sb == 1, ylow, low), jnp.where(sb == 1, yhigh, high)]),
            jnp.stack([jnp.where(sb == 1, low, ylow), jnp.where(sb == 1, high, yhigh)]),
        ]
    )


def scatter_groups(part):
    fh = lax.axis_index("fh")
    got = swap_sb(part(1).astype(BF16))
    mine = part(0) + got.astype(F32)
    send = lax.dynamic_index_in_dim(mine, 1 - fh, 0, keepdims=False).astype(BF16)
    keep = lax.dynamic_index_in_dim(mine, fh, 0, keepdims=False)
    return keep + swap_fh(send).astype(F32)


def xor_order(v, axis, index, n):
    shape = v.shape
    bit = 1
    while bit < n:
        r = v.reshape(shape[:axis] + (n // (2 * bit), 2, bit) + shape[axis + 1 :])
        v = flip_if((index // bit) % 2, r, axis + 1).reshape(shape)
        bit *= 2
    return v


def attend(q, k, v, ids):
    s = jnp.einsum("qhd,khd->hqk", q, k, preferred_element_type=F32) * (HD**-0.5)
    s = jnp.where(ids[None, :, None] >= ids[None, None, :], s, masked_score)
    peak = jnp.max(s, axis=-1, keepdims=True)
    e = jnp.exp(s - peak)
    p = e / jnp.sum(e, axis=-1, keepdims=True)
    o = jnp.einsum("hqk,khd->qhd", p.astype(BF16), v, preferred_element_type=F32)
    return o.astype(BF16), p


def attend_back(q, k, v, p, do):
    dp = jnp.einsum("qhd,khd->hqk", do, v, preferred_element_type=F32)
    ds = (p * (dp - jnp.sum(p * dp, axis=-1, keepdims=True))).astype(BF16)
    dq = jnp.einsum("hqk,khd->qhd", ds, k, preferred_element_type=F32) * (HD**-0.5)
    dk = jnp.einsum("hqk,qhd->khd", ds, q, preferred_element_type=F32) * (HD**-0.5)
    dv = jnp.einsum("hqk,qhd->khd", p.astype(BF16), do, preferred_element_type=F32)
    return dq, dk, dv


def rotate(values, cosine, sine, direction):
    half = ROT // 2
    a = values[..., :half]
    b = values[..., half:ROT]
    return jnp.concatenate(
        [a * cosine - direction * b * sine, b * cosine + direction * a * sine, values[..., ROT:]],
        axis=-1,
    )


def shards(
    inputs,
    cotangent,
    block_ids,
    ln1_gain,
    ln1_bias,
    qkv_weight,
    qkv_bias,
    out_weight,
    ln2_gain,
    ln2_bias,
    gate_weight,
    up_weight,
    down_weight,
):
    sb, sr, fh, fl = (lax.axis_index(a) for a in EVERY)
    n_sr = lax.axis_size("sr")
    n_dev = 8 * n_sr
    members = 2 * n_sr
    tok = inputs.shape[2]
    D = inputs.shape[3]
    length = block_ids.shape[2]
    rows = qkv_weight.shape[0]
    ff_rows = down_weight.shape[0]
    FF = ff_rows * n_dev
    heads = H // members
    natural = H % n_dev == 0

    def pick(v, i):
        return lax.dynamic_index_in_dim(v, i, 0, keepdims=False)

    def whole_vector(v):
        return lax.all_gather(v, EVERY, axis=0, tiled=True).astype(F32)

    gain1, bias1, gain2, bias2, bias_qkv = (
        whole_vector(v) for v in (ln1_gain, ln1_bias, ln2_gain, ln2_bias, qkv_bias)
    )

    def by_member(v):
        lead = v.shape[:-1]
        nl = len(lead)
        if natural:
            v = v.reshape(lead + (2, n_sr, 2, 2, -1))
            v = v.transpose((nl + 1, nl + 3) + tuple(range(nl)) + (nl, nl + 2, nl + 4))
        else:
            v = v.reshape(lead + (n_sr, 2, -1))
            v = v.transpose((nl, nl + 1) + tuple(range(nl)) + (nl + 2,))
        return v.reshape((members,) + lead + (-1,))

    def from_members(v):
        lead = v.shape[1:-1]
        nl = len(lead)
        if natural:
            v = v.reshape((n_sr, 2) + lead + (2, 2, -1))
            back = tuple(range(2, 2 + nl)) + (2 + nl, 0, 3 + nl, 1, 4 + nl)
        else:
            v = v.reshape((n_sr, 2) + lead + (-1,))
            back = tuple(range(2, 2 + nl)) + (0, 1, 2 + nl)
        return v.transpose(back).reshape(lead + (-1,))

    def ff_by_member(v):
        lead = v.shape[0]
        v = v.reshape(lead, 2, n_sr, 2, 2, ff_rows).transpose(2, 4, 0, 1, 3, 5)
        return v.reshape(members, lead, 4 * ff_rows)

    def ff_from_members(v):
        lead = v.shape[1]
        v = v.reshape(n_sr, 2, lead, 2, 2, ff_rows).transpose(2, 3, 0, 4, 1, 5)
        return v.reshape(lead, FF)

    def exchange(v):
        return lax.all_to_all(v, MEMBERS, split_axis=0, concat_axis=0, tiled=True)

    def full_rows(w):
        w = gather_groups(w)
        x = w.shape[-1]
        w = w.reshape(2, 2, n_sr, 2, rows, x).transpose(0, 2, 1, 3, 4, 5)
        return w.reshape(D, x)

    own_x = pick(inputs, sb)[0]
    own_x = jnp.concatenate([own_x, swap_sb(pick(inputs, 1 - sb)[0])], 0)
    m = 2 * tok
    xg = gather_tokens(own_x).reshape(members * m, D)
    own_dy = pick(cotangent, sb)[0]
    own_dy = jnp.concatenate([own_dy, swap_sb(pick(cotangent, 1 - sb)[0])], 0)
    dyg = gather_tokens(own_dy).reshape(members * m, D)

    my_ids = pick(block_ids, sb)
    ids = jnp.concatenate([my_ids, swap_fl(my_ids)], 0)
    ids = xor_order(ids.reshape(2, 2, n_sr, tok), 1, sb, 2)
    ids = xor_order(ids, 2, sr, n_sr).transpose(0, 2, 1, 3).reshape(2, length)
    sr_of = (jnp.arange(n_sr, dtype=jnp.int32) ^ sr)[:, None, None]
    sb_of = (jnp.arange(2, dtype=jnp.int32) ^ sb)[None, :, None]
    pos = ((sb_of * n_sr + sr_of) * tok + jnp.arange(tok, dtype=jnp.int32)[None, None, :]).reshape(-1)
    frequency = rope_base ** (-2.0 * jnp.arange(ROT // 2).astype(F32) / ROT)
    angles = pos.astype(F32)[:, None] * frequency[None, :]
    cosine, sine = jnp.cos(angles)[:, None, :], jnp.sin(angles)[:, None, :]

    w_qkv = full_rows(exchange(by_member(qkv_weight)))
    my_bias = lax.dynamic_index_in_dim(by_member(bias_qkv), sr * 2 + fl, 0, keepdims=False)
    if natural:
        w_out_own = gather_groups(out_weight).reshape(heads * HD, D)
        w_out = gather_tokens(w_out_own)
    else:
        w_out_all = lax.all_gather(out_weight, EVERY, axis=0, tiled=True)
        w_out = by_member(w_out_all.T.reshape(D, H * HD)).transpose(0, 2, 1)
        w_out_own = pick(w_out, sr * 2 + fl)
        w_out = xor_order(xor_order(w_out.reshape(n_sr, 2, -1, D), 0, sr, n_sr), 1, fl, 2)
        w_out = w_out.transpose(1, 0, 2, 3)
    w_gu = full_rows(
        exchange(jnp.concatenate([ff_by_member(gate_weight), ff_by_member(up_weight)], -1))
    )
    w_gate, w_up = w_gu[:, : 4 * ff_rows], w_gu[:, 4 * ff_rows :]
    w_down = gather_groups(down_weight).reshape(4 * ff_rows, D)

    n1, _ = norm_stats(xg.astype(F32))
    h1 = (n1 * gain1 + bias1).astype(BF16)
    lin = (jnp.dot(h1, w_qkv, preferred_element_type=F32) + my_bias).reshape(2, length, heads, 3, HD)
    kept = []
    outs = []
    for i in range(2):
        q = rotate(lin[i, :, :, 0], cosine, sine, 1.0).astype(BF16)
        k = rotate(lin[i, :, :, 1], cosine, sine, 1.0).astype(BF16)
        v = lin[i, :, :, 2].astype(BF16)
        o, p = attend(q, k, v, ids[i])
        outs.append(o.reshape(length, heads * HD))
        kept.append((q, k, v, p))
    o_own = jnp.concatenate(outs, 0)
    o_all = gather_tokens(o_own)

    o_rel = o_all.reshape(2, n_sr, 2, n_sr, m, heads * HD)
    pieces = []
    for a in range(2):
        row = []
        for b in range(n_sr):
            block = o_rel[a, b]
            row.append(
                jnp.stack([jnp.stack([block[a ^ c, b ^ d] for d in range(n_sr)]) for c in range(2)])
            )
        pieces.append(jnp.stack(row))
    o_rel = jnp.stack(pieces)
    o_mat = o_rel.transpose(2, 3, 4, 0, 1, 5).reshape(members * m, D)
    x2 = xg.astype(F32) + jnp.dot(o_mat, w_out.reshape(D, D), preferred_element_type=F32)

    n2, r2 = norm_stats(x2)
    h2 = (n2 * gain2 + bias2).astype(BF16)
    g = jnp.dot(h2, w_gate, preferred_element_type=F32)
    u = jnp.dot(h2, w_up, preferred_element_type=F32)
    d_act = lax.dot_general(dyg, w_down, (((1,), (1,)), ((), ())), preferred_element_type=F32)
    s = jax.nn.sigmoid(g)
    act = (g * s * u).astype(BF16)
    d_g = (d_act * u * s * (1.0 + g * (1.0 - s))).astype(BF16)
    d_u = (d_act * (g * s)).astype(BF16)
    d_h2 = lax.dot_general(
        d_g, w_gate, (((1,), (1,)), ((), ())), preferred_element_type=F32
    ) + lax.dot_general(d_u, w_up, (((1,), (1,)), ((), ())), preferred_element_type=F32)
    d_h2 = scatter_tokens(d_h2.astype(BF16).reshape(2, n_sr, m, D))
    n2_own, r2_own, x2_own = n2[:m], r2[:m], x2[:m]
    gain2_grad = jnp.sum(d_h2 * n2_own, axis=0)
    bias2_grad = jnp.sum(d_h2, axis=0)
    d_x2 = own_dy.astype(F32) + norm_back(d_h2 * gain2, n2_own, r2_own)
    d_att = gather_tokens(d_x2.astype(BF16)).reshape(members * m, D)

    y = jnp.dot(act, w_down, preferred_element_type=F32).astype(BF16)
    y = x2_own + scatter_tokens(y.reshape(2, n_sr, m, D))

    def give_back(v):
        v = v.astype(BF16)
        other = swap_sb(v[tok:])
        first = jnp.where(sb == 0, v[:tok], other)
        second = jnp.where(sb == 0, other, v[:tok])
        return jnp.stack([first, second])[:, None]

    layer_out = give_back(y)

    d_o = lax.dot_general(d_att, w_out_own, (((1,), (1,)), ((), ())), preferred_element_type=F32)
    d_o = d_o.astype(BF16).reshape(2, length, heads, HD)
    d_lins = []
    for i in range(2):
        dq, dk, dv = attend_back(*kept[i], d_o[i])
        dq = rotate(dq, cosine, sine, -1.0)
        dk = rotate(dk, cosine, sine, -1.0)
        d_lins.append(jnp.stack([dq, dk, dv], 2).astype(BF16).reshape(length, heads * 3 * HD))
    d_lin = jnp.concatenate(d_lins, 0)
    d_h1 = lax.dot_general(d_lin, w_qkv, (((1,), (1,)), ((), ())), preferred_element_type=F32)
    d_h1 = scatter_tokens(d_h1.astype(BF16).reshape(2, n_sr, m, D))
    n1_own, r1_own = norm_stats(own_x.astype(F32))
    gain1_grad = jnp.sum(d_h1 * n1_own, axis=0)
    bias1_grad = jnp.sum(d_h1, axis=0)
    input_grad = give_back(d_x2 + norm_back(d_h1 * gain1, n1_own, r1_own))

    def grad_rows(h, d, width):
        def part(k):
            side = lax.dynamic_index_in_dim(h.reshape(-1, 2, D // 2), sb ^ k, 1, keepdims=False)
            t = lax.dot_general(side, d, (((0,), (0,)), ((), ())), preferred_element_type=F32)
            return t.reshape(n_sr, 2, 2 * rows, width).transpose(1, 0, 2, 3)

        total = scatter_groups(part).reshape(members, rows, width)
        return exchange(total.astype(BF16)).astype(F32)

    def down_part(k):
        side = lax.dynamic_index_in_dim(act.reshape(-1, 2, 2 * ff_rows), sb ^ k, 1, keepdims=False)
        t = lax.dot_general(side, dyg, (((0,), (0,)), ((), ())), preferred_element_type=F32)
        return t.reshape(2, ff_rows, D)

    down_grad = scatter_groups(down_part)
    gu = grad_rows(h2, jnp.concatenate([d_g, d_u], -1), 8 * ff_rows)
    gate_grad = ff_from_members(gu[..., : 4 * ff_rows])
    up_grad = ff_from_members(gu[..., 4 * ff_rows :])
    if natural:

        def out_part(k):
            side = lax.dynamic_index_in_dim(
                o_own.reshape(-1, 2, heads * HD // 2), sb ^ k, 1, keepdims=False
            )
            t = lax.dot_general(side, d_att, (((0,), (0,)), ((), ())), preferred_element_type=F32)
            return t.reshape(2, heads * HD // 4, D)

        out_grad = scatter_groups(out_part)
    else:
        t = lax.dot_general(o_own, d_att, (((0,), (0,)), ((), ())), preferred_element_type=F32)
        spread = jnp.where(
            jnp.arange(members)[:, None, None] == sr * 2 + fl, t[None], jnp.zeros((), F32)
        )
        spread = spread.reshape(H * HD, D)
        out_grad = lax.psum_scatter(spread, EVERY, scatter_dimension=0, tiled=True)
    qkv_grad = from_members(grad_rows(h1, d_lin, heads * 3 * HD))

    bias_term = jnp.sum(d_lin.astype(F32), axis=0)
    bias_term = jnp.where(jnp.arange(members)[:, None] == sr * 2 + fl, bias_term[None], 0.0)
    bias_term = from_members(bias_term)
    gain1_grad, bias1_grad, bias_grad, gain2_grad, bias2_grad = (
        lax.psum_scatter(v, EVERY, scatter_dimension=0, tiled=True)
        for v in (gain1_grad, bias1_grad, bias_term, gain2_grad, bias2_grad)
    )
    return (
        layer_out,
        input_grad,
        gain1_grad,
        bias1_grad,
        qkv_grad,
        bias_grad,
        out_grad,
        gain2_grad,
        bias2_grad,
        gate_grad,
        up_grad,
        down_grad,
    )


def solution(mesh):
    names = dict(mesh.shape)
    n_seq, n_fsdp = names["seq"], names["fsdp"]
    fine = Mesh(mesh.devices.reshape(2, n_seq // 2, 2, n_fsdp // 2), EVERY)
    tokens = P(None, ("fh", "fl"), ("sb", "sr"), None)
    vector = P(EVERY)
    matrix = P(EVERY, None)
    in_specs = (
        tokens,
        tokens,
        P(None, ("fh", "fl"), None),
        vector,
        vector,
        matrix,
        vector,
        matrix,
        vector,
        vector,
        matrix,
        matrix,
        matrix,
    )
    out_specs = (
        tokens,
        tokens,
        vector,
        vector,
        matrix,
        vector,
        matrix,
        vector,
        vector,
        matrix,
        matrix,
        matrix,
    )
    return jax.shard_map(shards, mesh=fine, in_specs=in_specs, out_specs=out_specs, check_vma=False)
```

```python
import functools

import jax
import jax.numpy as jnp
import numpy as np
from jax import lax
from jax.experimental import pallas as pl
from jax.experimental.pallas import tpu as pltpu
from jax.sharding import Mesh
from jax.sharding import PartitionSpec as P

H = 32
HD = 64
ROT = 16

eps_norm = 1e-05
rope_base = 10000.0
masked_score = -1e30

F32 = jnp.float32
BF16 = jnp.bfloat16

SWAP = [(0, 1), (1, 0)]
EVERY = ("sb", "sx", "c", "fh", "fl")
MEMBERS = ("sx", "c", "fl")
QUAD = ("fl", "sx")
ANY = pl.BlockSpec(memory_space=pl.ANY)
SMEM = pl.BlockSpec(memory_space=pltpu.SMEM)
VMEM = pl.BlockSpec(memory_space=pltpu.VMEM)
NT = (((1,), (1,)), ((), ()))
TN = (((0,), (0,)), ((), ()))
LIMIT = 60 * 1024 * 1024


def params():
    return pltpu.CompilerParams(vmem_limit_bytes=LIMIT)


def cost(microseconds):
    return pl.CostEstimate(flops=int(microseconds * 1e9), bytes_accessed=1024, transcendentals=0)


def dot(a, b, dims=(((1,), (0,)), ((), ()))):
    return lax.dot_general(a, b, dims, preferred_element_type=F32)


def swap_sb(v):
    return lax.ppermute(v, "sb", SWAP)


def swap_fh(v):
    return lax.ppermute(v, "fh", SWAP)


def swap_fl(v):
    return lax.ppermute(v, "fl", SWAP)


def swap_c(v):
    return lax.ppermute(v, "c", SWAP)


def over_quad(v):
    return lax.all_to_all(v, QUAD, split_axis=0, concat_axis=0, tiled=True)


class Live(dict):
    def __getattr__(self, name):
        return self[name]

    def done(self, **new):
        self.update(new)
        self.update(lax.optimization_barrier(dict(self)))

    def drop(self, *names):
        for name in names:
            del self[name]


def normalize(values):
    average = jnp.mean(values, axis=-1, keepdims=True)
    centered = values - average
    inv_std = lax.rsqrt(jnp.mean(centered * centered, axis=-1, keepdims=True) + eps_norm)
    return centered * inv_std, inv_std


def normalize_back(grad_normed, normed, inv_std):
    first_mean = jnp.mean(grad_normed, axis=-1, keepdims=True)
    second_mean = jnp.mean(grad_normed * normed, axis=-1, keepdims=True)
    return inv_std * (grad_normed - first_mean - normed * second_mean)


def in_order(pieces, sb, fh):
    w, z, y, yz = pieces
    a, b = jnp.where(fh == 1, z, w), jnp.where(fh == 1, w, z)
    c, d = jnp.where(fh == 1, yz, y), jnp.where(fh == 1, y, yz)
    first = jnp.stack([jnp.where(sb == 1, c, a), jnp.where(sb == 1, d, b)])
    second = jnp.stack([jnp.where(sb == 1, a, c), jnp.where(sb == 1, b, d)])
    return jnp.stack([first, second])


def flip_if(bit, v, axis):
    return jnp.where(bit == 1, lax.rev(v, (axis,)), v)


def xor_order(v, axis, index, n):
    shape = v.shape
    bit = 1
    while bit < n:
        r = v.reshape(shape[:axis] + (n // (2 * bit), 2, bit) + shape[axis + 1 :])
        v = flip_if((index // bit) % 2, r, axis + 1).reshape(shape)
        bit *= 2
    return v


def load_groups(sc, pieces, places, buf, sems):
    copies = []
    rows = buf.shape[4]
    for n, (piece, (k, r)) in enumerate(zip(pieces, places)):
        where = buf.at[sc[0] ^ (k // 2), pl.ds(r, piece.shape[0]), sc[1] ^ (k % 2)]
        copies.append(pltpu.make_async_copy(piece.at[:, :, pl.ds(0, rows)], where, sems.at[n]))
    for c in copies:
        c.start()
    return copies


def load_down(sc, pieces, places, buf, sems):
    copies = []
    for n, (piece, (k, r)) in enumerate(zip(pieces, places)):
        where = buf
        if len(places) > 1:
            where = buf.at[sc[0] ^ (k // 2), sc[1] ^ (k % 2), pl.ds(r, piece.shape[0])]
        copies.append(pltpu.make_async_copy(piece, where, sems.at[n]))
    for c in copies:
        c.start()
    return copies


class Rows:
    def __init__(self, mine, other):
        self.arrays = [mine, other]
        self.N, self.D = 2 * mine.shape[0], mine.shape[1]

    def scratch(self):
        return [pltpu.VMEM((self.N, self.D), BF16), pltpu.SemaphoreType.DMA((4,))]

    def load(self, refs, buf, sems):
        n = self.N // 4
        copies = [
            pltpu.make_async_copy(
                refs[k].at[pl.ds(f * n, n)], buf.at[pl.ds((2 * f + k) * n, n)], sems.at[2 * f + k]
            )
            for f in range(2)
            for k in range(2)
        ]
        for c in copies:
            c.start()
        return copies


def sides(nb):
    def keep(i):
        f, k, b = i // (2 * nb), lax.rem(i // nb, 2), lax.rem(i, nb)
        return f * nb + jnp.where(k == 0, b, nb - 1)

    def send(i):
        f, k, b = i // (2 * nb), lax.rem(i // nb, 2), lax.rem(i, nb)
        return f * nb + jnp.where(k == 0, 0, b)

    return keep, send


def columns_kernel(plan, n_in, *refs):
    ins, out = refs[:n_in], refs[-1]
    rows = ins[0].shape[0]
    for t, ranges in enumerate(plan):
        out[t, :rows] = jnp.concatenate([ins[i][:, a : a + n] for i, a, n in ranges], axis=-1)
        if len(refs) == n_in + 2:
            out[t, rows:] = refs[n_in][...]


def columns(arrays, plan, extra=None):
    width = sum(n for _, _, n in plan[0])
    more = [] if extra is None else [extra]
    rows = sum(v.shape[0] for v in [arrays[0]] + more)
    return pl.pallas_call(
        functools.partial(columns_kernel, plan, len(arrays)),
        out_shape=jax.ShapeDtypeStruct((len(plan), rows, width), arrays[0].dtype),
        in_specs=[VMEM] * (len(arrays) + len(more)),
        out_specs=VMEM,
        compiler_params=params(),
        cost_estimate=cost(3),
    )(*arrays, *more)


def uncolumns_kernel(plan, *refs):
    ins, out = refs[:-1], refs[-1]
    width = ins[0].shape[2]
    if True:
        at, group, size = 0, [], 0
        for t, b, n in plan:
            group.append(ins[b // width][t, :, b % width : b % width + n].astype(F32))
            size += n
            if size % 128 == 0:
                out[:, at : at + size] = jnp.concatenate(group, axis=-1)
                at, group, size = at + size, [], 0
        if group:
            out[:, at : at + size] = jnp.concatenate(group, axis=-1)


def uncolumns(arrays, plan):
    rows = arrays[0].shape[1]
    return pl.pallas_call(
        functools.partial(uncolumns_kernel, plan),
        out_shape=jax.ShapeDtypeStruct((rows, sum(n for _, _, n in plan)), F32),
        in_specs=[VMEM] * len(arrays),
        out_specs=VMEM,
        compiler_params=params(),
        cost_estimate=cost(3),
    )(*arrays)


def turn(v, c_ref_value, sa, sb_, direction):
    width = v.shape[1]
    back = pltpu.roll(v, ROT // 2, 1)
    front = pltpu.roll(v, width - ROT // 2, 1)
    return v * c_ref_value + direction * (back * sa + front * sb_)


def attention_kernel(dims, places, x_rows, sc, gain, bias, bias_q, tables, id_row, id_col, w_out, x0, x1, *refs):
    heads, length, block, D = dims
    w_refs, (h1, q, k, v, o, lse, keep, send, w, sems, x_buf, x_sems) = refs[: len(places)], refs[len(places) :]
    wide = heads * HD
    per = length // block
    i = pl.program_id(0)

    @pl.when(i == 0)
    def _():
        copies = x_rows.load((x0, x1), x_buf, x_sems)
        for c in load_groups(sc, w_refs, places, w, sems) + copies:
            c.wait()

    rows = pl.ds(pl.multiple_of(i * block, block), block)
    normed, _ = normalize(x_buf[rows, :].astype(F32))
    h = (normed * gain[...] + bias[...]).astype(BF16)
    h1[...] = h
    lin = dot(h, w[...].reshape(D, 3 * wide)) + bias_q[...]
    qk = turn(lin[:, : 2 * wide], tables[0], tables[1], tables[2], 1.0)
    q[rows, :] = qk[:, :wide].astype(BF16)
    k[rows, :] = qk[:, wide:].astype(BF16)
    v[rows, :] = lin[:, 2 * wide :].astype(BF16)

    @pl.when(lax.rem(i, per) == per - 1)
    def _():
        s = i // per
        start = pl.multiple_of(s * length, length)
        step = min(512, length)
        for r in range(length // step):
            part = pl.ds(pl.multiple_of(start + r * step, step), step)
            allowed = id_col[part, 0:1] >= id_row[pl.ds(s, 1), :]
            for hd in range(heads):
                lanes = slice(hd * HD, (hd + 1) * HD)
                kh = k[pl.ds(start, length), lanes]
                vh = v[pl.ds(start, length), lanes]
                score = dot(q[part, lanes], kh, NT) * (HD**-0.5)
                score = jnp.where(allowed, score, masked_score)
                peak = jnp.max(score, axis=-1, keepdims=True)
                e = jnp.exp(score - peak)
                total = jnp.sum(e, axis=-1, keepdims=True)
                p = (e * (1.0 / total)).astype(BF16)
                o[part, lanes] = dot(p, vh).astype(BF16)
                lse[part, hd : hd + 1] = peak + jnp.log(total)
        for side, out in enumerate((keep, send)):
            for b in range(per // 2):
                part = pl.ds(pl.multiple_of(start + (side * (per // 2) + b) * block, block), block)
                out[0, b * block : (b + 1) * block] = dot(o[part, :], w_out[...]).astype(BF16)


def attention(sc, x_rows, gain, bias, bias_q, tables, id_row, id_col, w_out, weight, heads, rows):
    N, D = x_rows.N, x_rows.D
    length = N // 2
    block = 256
    per = length // block
    wide = heads * HD
    n_sr, _, _, f = weight[0][0].shape
    places = [p[1:] for p in weight]
    whole = lambda shape: pl.BlockSpec(shape, lambda i, sc: (0,) * len(shape))
    side = pl.BlockSpec((1, length // 2, D), lambda i, sc: (i // per, 0, 0))
    spec = pltpu.PrefetchScalarGridSpec(
        num_scalar_prefetch=1,
        grid=(N // block,),
        in_specs=[
            whole((1, D)),
            whole((1, D)),
            whole((1, 3 * wide)),
            pl.BlockSpec((3, block, 2 * wide), lambda i, sc: (0, lax.rem(i, per), 0)),
            whole((2, length)),
            whole((N, 1)),
            whole((wide, D)),
            ANY,
            ANY,
        ]
        + [ANY] * len(places),
        out_specs=[pl.BlockSpec((block, D), lambda i, sc: (i, 0))]
        + [whole((N, wide))] * 4
        + [whole((N, heads)), side, side],
        scratch_shapes=[
            pltpu.VMEM((2, n_sr, 2, 2, rows, f), BF16),
            pltpu.SemaphoreType.DMA((len(places),)),
        ]
        + x_rows.scratch(),
    )
    return pl.pallas_call(
        functools.partial(attention_kernel, (heads, length, block, D), places, x_rows),
        grid_spec=spec,
        out_shape=[jax.ShapeDtypeStruct((N, D), BF16)]
        + [jax.ShapeDtypeStruct((N, wide), BF16)] * 4
        + [jax.ShapeDtypeStruct((N, heads), F32)]
        + [jax.ShapeDtypeStruct((2, length // 2, D), BF16)] * 2,
        compiler_params=params(),
        cost_estimate=cost(25),
    )(sc, gain, bias, bias_q, tables, id_row, id_col, w_out, *x_rows.arrays, *[p[0] for p in weight])


def ffn_kernel(dims, h_rows, dy_rows, sc, h0, h1, dy0, dy1, *refs):
    g_list, d_list, block, nb, D, ff = dims
    g_refs, refs = refs[: len(g_list)], refs[len(g_list) :]
    d_refs, refs = refs[: len(d_list)], refs[len(d_list) :]
    h2, act, d_gu, keep, send, g_buf, d_buf, sem_g, sem_d, h_buf, h_sems, dy_buf, dy_sems = refs
    i = pl.program_id(0)
    rows = pl.ds(pl.multiple_of(i * block, block), block)
    copies = []

    @pl.when(i == 0)
    def _():
        first = h_rows.load((h0, h1), h_buf, h_sems) + load_groups(sc, g_refs, g_list, g_buf, sem_g)
        second = dy_rows.load((dy0, dy1), dy_buf, dy_sems) + load_down(sc, d_refs, d_list, d_buf, sem_d)
        for c in first + second:
            c.wait()

    h = h_buf[rows, :]
    h2[...] = h
    w_gu = g_buf[...].reshape(D, 2 * ff)
    gu = dot(h, w_gu)
    g, u = gu[:, :ff], gu[:, ff:]
    s = jax.nn.sigmoid(g)
    silu = g * s
    act[...] = (silu * u).astype(BF16)
    d_act = dot(dy_buf[rows, :], d_buf[...].reshape(ff, D), NT)
    d_g = (d_act * u * s * (1.0 + g * (1.0 - s))).astype(BF16)
    d_u = (d_act * silu).astype(BF16)
    d = jnp.concatenate([d_g, d_u], axis=-1)
    d_gu[...] = d
    d_h = dot(d, w_gu, NT).astype(BF16)
    side = lax.rem(i // nb, 2)

    @pl.when(side == 0)
    def _():
        keep[...] = d_h

    @pl.when(side == 1)
    def _():
        send[...] = d_h


def ffn(sc, h_rows, dy_rows, gu, down, down_places, rows_):
    N, D = h_rows.N, h_rows.D
    block = 256
    nb = N // 4 // block
    n_sr, _, _, two_ff = gu[0][0].shape
    ff = two_ff // 2
    rows = lambda width: pl.BlockSpec((block, width), lambda i, sc: (i, 0))
    d_shape = (2, 2, ff // 4, D) if len(down) > 1 else (ff, D)
    keep, send = sides(nb)
    spec = pltpu.PrefetchScalarGridSpec(
        num_scalar_prefetch=1,
        grid=(N // block,),
        in_specs=[ANY] * (4 + len(gu) + len(down)),
        out_specs=[
            rows(D),
            rows(ff),
            rows(2 * ff),
            pl.BlockSpec((block, D), lambda i, sc: (keep(i), 0)),
            pl.BlockSpec((block, D), lambda i, sc: (send(i), 0)),
        ],
        scratch_shapes=[
            pltpu.VMEM((2, n_sr, 2, 2, rows_, two_ff), BF16),
            pltpu.VMEM(d_shape, BF16),
            pltpu.SemaphoreType.DMA((len(gu),)),
            pltpu.SemaphoreType.DMA((len(down),)),
        ]
        + h_rows.scratch()
        + dy_rows.scratch(),
    )
    dims = ([p[1:] for p in gu], down_places, block, nb, D, ff)
    return pl.pallas_call(
        functools.partial(ffn_kernel, dims, h_rows, dy_rows),
        grid_spec=spec,
        out_shape=[
            jax.ShapeDtypeStruct((N, D), BF16),
            jax.ShapeDtypeStruct((N, ff), BF16),
            jax.ShapeDtypeStruct((N, 2 * ff), BF16),
            jax.ShapeDtypeStruct((N // 2, D), BF16),
            jax.ShapeDtypeStruct((N // 2, D), BF16),
        ],
        compiler_params=params(),
        cost_estimate=cost(30),
    )(sc, *h_rows.arrays, *dy_rows.arrays, *[p[0] for p in gu], *down)


def down_kernel(d_list, nb, ff, D, sc, act, *refs):
    n_d = len(d_list)
    d_refs, (keep, send, d_buf, sem) = refs[:n_d], refs[n_d:]
    i = pl.program_id(0)

    @pl.when(i == 0)
    def _():
        for c in load_down(sc, d_refs, d_list, d_buf, sem):
            c.wait()

    y = dot(act[...], d_buf[...].reshape(ff, D)).astype(BF16)
    side = lax.rem(i // nb, 2)

    @pl.when(side == 0)
    def _():
        keep[...] = y

    @pl.when(side == 1)
    def _():
        send[...] = y


def down_product(sc, act, down, places):
    N, ff = act.shape
    D = down[0].shape[-1]
    block = 256
    nb = N // 4 // block
    d_shape = (2, 2, ff // 4, D) if len(down) > 1 else (ff, D)
    keep, send = sides(nb)
    spec = pltpu.PrefetchScalarGridSpec(
        num_scalar_prefetch=1,
        grid=(N // block,),
        in_specs=[pl.BlockSpec((block, ff), lambda i, sc: (i, 0))] + [ANY] * len(down),
        out_specs=[
            pl.BlockSpec((block, D), lambda i, sc: (keep(i), 0)),
            pl.BlockSpec((block, D), lambda i, sc: (send(i), 0)),
        ],
        scratch_shapes=[pltpu.VMEM(d_shape, BF16), pltpu.SemaphoreType.DMA((len(down),))],
    )
    return pl.pallas_call(
        functools.partial(down_kernel, places, nb, ff, D),
        grid_spec=spec,
        out_shape=[jax.ShapeDtypeStruct((N // 2, D), BF16)] * 2,
        compiler_params=params(),
        cost_estimate=cost(9),
    )(sc, act, *down)


def attention_back_kernel(dims, d_rows, sc, tables, id_row, id_col, q, k, v, lse, w_out, d0, d1, *refs):
    heads, length, N, D, w_list = dims
    w_refs, refs = refs[: len(w_list)], refs[len(w_list) :]
    d_lin, bias_grad, keep, send, w, d_o, d_qk, sem_w, d_att, sem_d = refs
    wide = heads * HD
    copies = d_rows.load((d0, d1), d_att, sem_d)
    loads = load_groups(sc, w_refs, w_list, w, sem_w)
    for c in copies:
        c.wait()
    step = min(512, length)
    scale = HD**-0.5
    bias_grad[...] = jnp.zeros_like(bias_grad)
    for s in range(2):
        start = s * length
        for r in range(length // step):
            at = pl.ds(start + r * step, step)
            d_o[pl.ds(r * step, step), :] = dot(d_att[at, :], w_out[...], NT).astype(BF16)
        d_qk[:, wide:] = jnp.zeros_like(d_qk[:, wide:])
        for hd in range(heads):
            lanes = slice(hd * HD, (hd + 1) * HD)
            k_lanes = slice(wide + hd * HD, wide + (hd + 1) * HD)
            v_lanes = slice(2 * wide + hd * HD, 2 * wide + (hd + 1) * HD)
            kh = k[pl.ds(start, length), lanes]
            vh = v[pl.ds(start, length), lanes]
            for r in range(length // step):
                part = pl.ds(start + r * step, step)
                local = pl.ds(r * step, step)
                allowed = id_col[part, 0:1] >= id_row[s : s + 1, :]
                qh = q[part, lanes]
                score = dot(qh, kh, NT) * scale
                p = jnp.where(allowed, jnp.exp(score - lse[part, hd : hd + 1]), 0.0)
                doh = d_o[local, lanes]
                dp = dot(doh, vh, NT)
                inner = jnp.sum(p * dp, axis=-1, keepdims=True)
                ds = (p * (dp - inner)).astype(BF16)
                d_qk[local, lanes] = dot(ds, kh) * scale
                dk = dot(ds, qh, TN) * scale
                dv = dot(p.astype(BF16), doh, TN)
                if length == step:
                    d_qk[:, k_lanes] = dk
                    d_qk[:, v_lanes] = dv
                else:
                    d_qk[:, k_lanes] += dk
                    d_qk[:, v_lanes] += dv
        if s == 0:
            for c in loads:
                c.wait()
        block = 256
        half = length // 2
        for b in range(length // block):
            local = pl.ds(b * block, block)
            at = pl.ds(start + b * block, block)
            qk = turn(d_qk[local, : 2 * wide], tables[0, local], tables[1, local], tables[2, local], -1.0)
            lin = jnp.concatenate([qk, d_qk[local, 2 * wide :]], axis=-1).astype(BF16)
            d_lin[at, :] = lin
            bias_grad[...] += jnp.sum(lin.astype(F32), axis=0, keepdims=True)
            d_h = dot(lin, w[...].reshape(D, 3 * wide), NT).astype(BF16)
            out = keep if b * block < half else send
            out[pl.ds(s * half + (b * block) % half, block), :] = d_h


def attention_back(sc, tables, id_row, id_col, q, k, v, lse, w_out, d_rows, weight):
    N, wide = q.shape
    D = w_out.shape[1]
    heads = wide // HD
    length = N // 2
    n_sr, _, _, f = weight[0][0].shape
    rows = D // (8 * n_sr)
    dims = (heads, length, N, D, [p[1:] for p in weight])
    return pl.pallas_call(
        functools.partial(attention_back_kernel, dims, d_rows),
        out_shape=[
            jax.ShapeDtypeStruct((N, 3 * wide), BF16),
            jax.ShapeDtypeStruct((1, 3 * wide), F32),
            jax.ShapeDtypeStruct((N // 2, D), BF16),
            jax.ShapeDtypeStruct((N // 2, D), BF16),
        ],
        in_specs=[SMEM] + [VMEM] * 8 + [ANY] * (2 + len(weight)),
        out_specs=[VMEM] * 4,
        scratch_shapes=[
            pltpu.VMEM((2, n_sr, 2, 2, rows, f), BF16),
            pltpu.VMEM((length, wide), BF16),
            pltpu.VMEM((length, 3 * wide), F32),
            pltpu.SemaphoreType.DMA((len(weight),)),
        ]
        + d_rows.scratch(),
        compiler_params=params(),
        cost_estimate=cost(23),
    )(sc, tables, id_row, id_col, q, k, v, lse, w_out, *d_rows.arrays, *[p[0] for p in weight])


def rows_kernel(dims, sc, h, d, other0, other1, same0, same1):
    n, two_rows = dims
    t = dot(h[...], d[...], TN).astype(BF16)
    i = pl.program_id(0)
    for f in range(2):
        for step_, other, same in ((0, other0, same0), (1, other1, same1)):
            for out, here in ((same, sc[1] == f), (other, sc[1] != f)):

                @pl.when(here & (i == step_))
                def _():
                    for j in range(n):
                        r = (2 * j + f) * two_rows
                        out[j * two_rows : (j + 1) * two_rows, :] = t[r : r + two_rows]


def grad_rows(sc, h, d, side, n_sr, rows):
    N, D = h.shape
    f = d.shape[1]
    cut = D // 4
    n = n_sr // 2
    spec = pltpu.PrefetchScalarGridSpec(
        num_scalar_prefetch=1,
        grid=(2,),
        in_specs=[
            pl.BlockSpec((N, cut), lambda i, sc: (0, (sc[0] ^ side) * 2 + i)),
            pl.BlockSpec((N, f), lambda i, sc: (0, 0)),
        ],
        out_specs=[pl.BlockSpec((cut // 2, f), lambda i, sc: (0, 0))] * 4,
    )
    return pl.pallas_call(
        functools.partial(rows_kernel, (n, 2 * rows)),
        grid_spec=spec,
        out_shape=[jax.ShapeDtypeStruct((cut // 2, f), BF16)] * 4,
        compiler_params=params(),
        cost_estimate=cost(7),
    )(sc, h, d)


def slices_kernel(rows, cut, d_rows, sc, a, d0, d1, *refs):
    outs, (buf, sems) = refs[:4], refs[4:]
    i = pl.program_id(0)

    @pl.when(i == 0)
    def _():
        for c in d_rows.load((d0, d1), buf, sems):
            c.wait()

    d = buf[:, pl.ds(pl.multiple_of(i * cut, cut), cut)]
    t = dot(a[...], d, TN).astype(BF16)
    for n in range(4):
        for k in range(4):

            @pl.when((sc[0] == (n // 2) ^ (k // 2)) & (sc[1] == (n % 2) ^ (k % 2)))
            def _():
                outs[k][...] = t[n * rows : (n + 1) * rows]


def grad_slices(sc, a, d_rows):
    N, f = a.shape
    D = d_rows.D
    cut = D // 4
    spec = pltpu.PrefetchScalarGridSpec(
        num_scalar_prefetch=1,
        grid=(D // cut,),
        in_specs=[pl.BlockSpec((N, f), lambda i, sc: (0, 0)), ANY, ANY],
        out_specs=[pl.BlockSpec((f // 4, cut), lambda i, sc: (0, i))] * 4,
        scratch_shapes=d_rows.scratch(),
    )
    return pl.pallas_call(
        functools.partial(slices_kernel, f // 4, cut, d_rows),
        grid_spec=spec,
        out_shape=[jax.ShapeDtypeStruct((f // 4, D), BF16)] * 4,
        compiler_params=params(),
        cost_estimate=cost(9),
    )(sc, a, *d_rows.arrays)


def total_of(terms):
    d = terms[0].astype(F32)
    for n in range(1, terms.shape[0]):
        d += terms[n].astype(F32)
    return d


def forward_kernel(terms, x, gain, bias, x2, copies):
    v = x[...].astype(F32) + total_of(terms)
    x2[...] = v
    normed, _ = normalize(v)
    h = (normed * gain[...] + bias[...]).astype(BF16)
    for n in range(copies.shape[0]):
        copies[n] = h


def norm_step(terms, x, gain, bias):
    n, m, D = terms.shape
    return pl.pallas_call(
        forward_kernel,
        out_shape=[jax.ShapeDtypeStruct((m, D), F32), jax.ShapeDtypeStruct((n, m, D), BF16)],
        in_specs=[VMEM] * 4,
        out_specs=[VMEM] * 2,
        compiler_params=params(),
        cost_estimate=cost(4),
    )(terms, x, gain, bias)


def back_kernel(terms, x, dy, gain, grad, copies, sums):
    d_h = total_of(terms)
    normed, inv_std = normalize(x[...].astype(F32))
    total = dy[...].astype(F32) + normalize_back(d_h * gain[...], normed, inv_std)
    grad[...] = total
    low = total.astype(BF16)
    for n in range(copies.shape[0]):
        copies[n] = low
    sums[0:1, :] = jnp.sum(d_h * normed, axis=0, keepdims=True)
    sums[1:2, :] = jnp.sum(d_h, axis=0, keepdims=True)


def norm_step_back(terms, x, dy, gain, copies):
    n, m, D = terms.shape
    return pl.pallas_call(
        back_kernel,
        out_shape=[
            jax.ShapeDtypeStruct((m, D), F32),
            jax.ShapeDtypeStruct((copies, m, D), BF16),
            jax.ShapeDtypeStruct((2, D), F32),
        ],
        in_specs=[VMEM] * 4,
        out_specs=[VMEM] * 3,
        compiler_params=params(),
        cost_estimate=cost(4),
    )(terms, x, dy, gain)


def shards(
    inputs,
    cotangent,
    block_ids,
    ln1_gain,
    ln1_bias,
    qkv_weight,
    qkv_bias,
    out_weight,
    ln2_gain,
    ln2_bias,
    gate_weight,
    up_weight,
    down_weight,
):
    sb, sx, c, fh, fl = (lax.axis_index(a).astype(jnp.int32) for a in EVERY)
    n_sx = lax.axis_size("sx")
    sr, n_sr = sx * 2 + c, 2 * n_sx
    quad = 2 * n_sx
    n_dev = 8 * n_sr
    members = 2 * n_sr
    tok = inputs.shape[2]
    m = 2 * tok
    D = inputs.shape[3]
    length = block_ids.shape[2]
    N = 2 * length
    rows = qkv_weight.shape[0]
    ff_rows = down_weight.shape[0]
    ff = 4 * ff_rows
    heads = H // members
    wide = heads * HD
    natural = H % n_dev == 0
    sc = jnp.stack([sb, fh])

    def pick(v, i):
        return lax.dynamic_index_in_dim(v, i, 0, keepdims=False)

    def device_of(t, a):
        return (((a // 2) * n_sr + t // 2) * 2 + a % 2) * 2 + t % 2

    def head_of(t, i):
        return device_of(t, i) if natural else t * heads + i

    qkv_plan = [
        [(0, (head_of(t, i) * 3 + part) * HD, HD) for part in range(3) for i in range(heads)]
        for t in range(members)
    ]
    gu_plan = [
        [(w, device_of(t, a) * ff_rows, ff_rows) for w in range(2) for a in range(4)]
        for t in range(members)
    ]
    head_place = {head_of(t, i): (t, i) for t in range(members) for i in range(heads)}
    qkv_back = [
        (head_place[h][0], part * wide + head_place[h][1] * HD, HD) for h in range(H) for part in range(3)
    ]
    ff_place = {device_of(t, a): (t, a) for t in range(members) for a in range(4)}
    gate_back = [(ff_place[d][0], ff_place[d][1] * ff_rows, ff_rows) for d in range(n_dev)]
    up_back = [(t, ff + b, n) for t, b, n in gate_back]

    def exchange(v):
        return lax.all_to_all(v, MEMBERS, split_axis=0, concat_axis=0, tiled=True)

    def of_rows(v):
        return v.reshape((n_sr, 2) + v.shape[1:])

    def both(bit, own, other):
        return jnp.stack([jnp.where(bit == 0, own, other), jnp.where(bit == 0, other, own)])

    my_ids = pick(block_ids, sb)
    c_of = (jnp.arange(2, dtype=jnp.int32) ^ c)[:, None, None, None]
    sx_of = jnp.arange(n_sx, dtype=jnp.int32)[None, :, None, None]
    sb_of = (jnp.arange(2, dtype=jnp.int32) ^ sb)[None, None, :, None]
    pos = ((sb_of * n_sx + sx_of) * 2 + c_of) * tok + jnp.arange(tok, dtype=jnp.int32)[None, None, None, :]
    pos = pos.reshape(-1)
    half = ROT // 2
    lane = np.arange(2 * wide) % HD
    turned = lane < ROT
    frequency = np.where(turned, rope_base ** (-2.0 * (lane % half).astype(np.float32) / ROT), 0.0)
    angles = pos.astype(F32)[:, None] * jnp.asarray(frequency, F32)[None, :]
    sine = jnp.sin(angles)
    to_back = jnp.asarray(np.where(turned & (lane >= half), 1.0, 0.0), F32)
    to_front = jnp.asarray(np.where(lane < half, -1.0, 0.0), F32)
    tables = jnp.stack([jnp.cos(angles), sine * to_back, sine * to_front])

    rep = lambda v_: jnp.broadcast_to(v_[None], (quad,) + v_.shape)
    flat = lambda v_: v_.reshape(-1, v_.shape[-1])
    by_member_of_quad = lambda v_: v_.reshape(quad, m, D)

    small = jnp.concatenate([ln1_gain, ln1_bias, ln2_gain, ln2_bias, qkv_bias])
    n_small = small.shape[0]
    small = jnp.pad(small[None], ((0, 7), (0, 3 * wide - n_small)))
    live = Live(
        sc=sc,
        inputs=inputs,
        cotangent=cotangent,
        my_ids=my_ids,
        out_w=out_weight,
        gate_w=gate_weight,
        up_w=up_weight,
        down_w=down_weight,
    )
    half_rows = ff_rows // 32 * 16 if ff_rows % 16 == 0 else ff_rows // 2
    live.done(qkv_c=columns([qkv_weight], qkv_plan, small))
    down_a, down_b = live.down_w[:half_rows], live.down_w[half_rows:]
    live.drop("down_w")
    give = jnp.concatenate([pick(live.inputs, 1 - sb)[0], pick(live.cotangent, 1 - sb)[0]], 0)
    live.done(
        w_qkv=of_rows(exchange(live.qkv_c)),
        got=swap_sb(give),
        out_1=swap_fh(live.out_w) if natural else live.out_w,
        ids_got=swap_fl(live.my_ids),
        gu_c=columns([live.gate_w, live.up_w], gu_plan),
        down_a=down_a,
        down_b=down_b,
        tables=tables,
    )

    own_x = jnp.concatenate([pick(live.inputs, sb)[0], live.got[:tok]], 0)
    own_dy = jnp.concatenate([pick(live.cotangent, sb)[0], live.got[tok:]], 0)
    ids = both(fl, live.my_ids, live.ids_got).reshape(2, 2, n_sx, 2, tok)
    ids = flip_if(c, flip_if(sb, ids, 1), 3).transpose(0, 3, 2, 1, 4).reshape(2, length)
    live.drop("inputs", "cotangent", "got", "my_ids", "ids_got", "gate_w", "up_w", "qkv_c")
    live.done(
        qkv_1=swap_fh(live.w_qkv),
        qkv_2=swap_sb(live.w_qkv),
        w_gu=of_rows(exchange(live.gu_c)),
        own_x=own_x,
        own_dy=own_dy,
        x_rep=rep(own_x),
        out_2=swap_sb(live.out_w) if natural else live.out_w,
        out_3=swap_sb(live.out_1) if natural else live.out_w,
        ids=ids,
        id_col=ids.reshape(N, 1),
    )

    cut = n_sr // 2
    gu_a, gu_b = live.w_gu[:cut], live.w_gu[cut:]
    live.done(
        qkv_3=swap_sb(live.qkv_1),
        x_mine=flat(over_quad(live.x_rep)),
        dy_rep=rep(live.own_dy),
        gu_1a=swap_fh(gu_a),
        gu_b=gu_b,
    )
    small = [v_[:, :, rows, :n_small] for v_ in (live.w_qkv, live.qkv_1, live.qkv_2, live.qkv_3)]
    small = in_order(small, sb, fh).transpose(0, 2, 1, 3, 4).reshape(n_dev, n_small).astype(F32)
    if natural:
        out_own = in_order((live.out_w, live.out_1, live.out_2, live.out_3), sb, fh)
        out_own = out_own.reshape(wide, D)
    else:
        out_all = lax.all_gather(out_weight, EVERY, axis=0, tiled=True)
        out_own = lax.dynamic_slice_in_dim(out_all, (sr * 2 + fl) * wide, wide, 0)
    gain1, bias1, gain2, bias2 = (
        small[:, n * rows : (n + 1) * rows].reshape(1, D) for n in range(4)
    )
    bias_all = small[:, 4 * rows :].reshape(H, 3, HD)
    if natural:
        my_bias = bias_all.reshape(2, n_sr, 2, 2, 3, HD)
        my_bias = lax.dynamic_index_in_dim(my_bias, sr, 1, keepdims=False)
        my_bias = lax.dynamic_index_in_dim(my_bias, fl, 2, keepdims=False).reshape(heads, 3, HD)
    else:
        my_bias = lax.dynamic_slice_in_dim(bias_all, (sr * 2 + fl) * heads, heads, 0)
    my_bias = my_bias.transpose(1, 0, 2).reshape(1, 3 * wide)

    live.done(
        x_other=swap_c(live.x_mine),
        gain1=gain1,
        bias1=bias1,
        gain2=gain2,
        bias2=bias2,
        my_bias=my_bias,
        out_own=out_own,
    )

    qkv = lambda: [(live.w_qkv, 0, 0), (live.qkv_1, 1, 0), (live.qkv_2, 2, 0), (live.qkv_3, 3, 0)]
    h1, q, k, v, o, lse, keep, send = attention(
        live.sc,
        Rows(live.x_mine, live.x_other),
        live.gain1,
        live.bias1,
        live.my_bias,
        live.tables,
        live.ids,
        live.id_col,
        live.out_own,
        qkv(),
        heads,
        rows,
    )
    live.drop("x_mine", "x_other", "x_rep", "out_w", "out_1", "out_2", "out_3", "gu_c", "bias1", "my_bias")
    live.done(
        h1=h1,
        q=q,
        k=k,
        v=v,
        o=o,
        lse=lse,
        keep=keep,
        send=send,
        gu_1b=swap_fh(live.gu_b),
        down_1a=swap_fh(live.down_a),
        gu_2=swap_sb(live.w_gu),
        down_2a=swap_sb(live.down_a),
        dy_mine=flat(over_quad(live.dy_rep)),
    )
    live.drop("dy_rep", "gu_b")

    def plus(a_, b_, kind=F32):
        return (a_.astype(F32) + b_.astype(F32)).astype(kind)

    live.done(got=swap_c(live.send))
    live.done(
        terms=over_quad(by_member_of_quad(plus(live.keep, live.got, BF16))),
        gu_3=[swap_sb(live.gu_1a), swap_sb(live.gu_1b)],
        dy_other=swap_c(live.dy_mine),
        down_1b=swap_fh(live.down_b),
    )
    x2_own, h2_rep = norm_step(live.terms, live.own_x, live.gain2, live.bias2)
    live.done(
        x2_own=x2_own,
        h2_mine=flat(over_quad(h2_rep)),
        down_2b=swap_sb(live.down_b),
        down_3=[swap_sb(live.down_1a), swap_sb(live.down_1b)],
    )
    live.done(h2_other=swap_c(live.h2_mine))

    down = [live.down_a, live.down_1a, live.down_2a, live.down_3[0], live.down_b, live.down_1b, live.down_2b, live.down_3[1]]
    down_places = [(n, 0) for n in range(4)] + [(n, half_rows) for n in range(4)]
    if ff_rows % 16 != 0:
        down = in_order([jnp.concatenate([down[n], down[n + 4]], 0) for n in range(4)], sb, fh)
        down, down_places = [down.reshape(ff, D)], [(0, 0)]
    gu = [(live.w_gu, 0, 0), (live.gu_1a, 1, 0), (live.gu_1b, 1, cut)]
    gu += [(live.gu_2, 2, 0), (live.gu_3[0], 3, 0), (live.gu_3[1], 3, cut)]
    h2, act, d_gu, keep, send = ffn(
        live.sc,
        Rows(live.h2_mine, live.h2_other),
        Rows(live.dy_mine, live.dy_other),
        gu,
        down,
        down_places,
        rows,
    )
    live.drop("w_gu", "gu_1a", "gu_1b", "gu_2", "gu_3", "down_a", "down_b")
    live.drop("down_1a", "down_1b", "down_2a", "down_2b", "down_3")
    live.drop("h2_mine", "h2_other", "bias2", "got", "terms")

    def give_back(v_):
        other = swap_sb(v_[tok:])
        first = jnp.where(sb == 0, v_[:tok], other)
        second = jnp.where(sb == 0, other, v_[:tok])
        return jnp.stack([first, second])[:, None]

    live.done(
        h2=h2,
        act=act,
        d_gu=d_gu,
        down=down,
        keep=keep,
        got=swap_c(send),
        gu_t=grad_rows(live.sc, h2, d_gu, 1, n_sr, rows),
    )
    live.done(
        terms=over_quad(by_member_of_quad(plus(live.keep, live.got, BF16))),
        gu_got1=[swap_sb(v_) for v_ in live.gu_t[:2]],
        down_t=grad_slices(live.sc, live.act, Rows(live.dy_mine, live.dy_other)),
        gu_m=grad_rows(live.sc, live.h2, live.d_gu, 0, n_sr, rows),
    )
    live.drop("dy_mine", "dy_other", "h2", "d_gu")
    d_x2, att_rep, sums2 = norm_step_back(live.terms, live.x2_own, live.own_dy, live.gain2, quad)
    y_keep, y_send = down_product(live.sc, live.act, live.down, down_places)
    live.drop("act", "down")
    live.done(
        d_x2=d_x2,
        sums2=sums2,
        att_mine=flat(over_quad(att_rep)),
        gu_over=[swap_fh(plus(live.gu_m[0], live.gu_got1[0], BF16))],
        gu_give=plus(live.gu_m[1], live.gu_got1[1], BF16),
        gu_got0=[swap_sb(v_) for v_ in live.gu_t[2:]],
        y_keep=y_keep,
        y_send=y_send,
    )
    live.drop("gu_t", "gu_got1")
    live.done(att_other=swap_c(live.att_mine), y_got=swap_c(live.y_send))
    d_lin, bias_term, keep, send = attention_back(
        live.sc,
        live.tables,
        live.ids,
        live.id_col,
        live.q,
        live.k,
        live.v,
        live.lse,
        live.out_own,
        Rows(live.att_mine, live.att_other),
        qkv(),
    )
    live.drop("q", "k", "v", "lse", "out_own", "w_qkv", "qkv_1", "qkv_2", "qkv_3", "tables", "ids", "id_col", "y_send")
    live.done(
        d_lin=d_lin,
        bias_term=bias_term,
        keep=keep,
        send=send,
        y_terms=over_quad(by_member_of_quad(plus(live.y_keep, live.y_got, BF16))),
        down_got=[swap_sb(v_) for v_ in live.down_t[2:]],
        gu_over=live.gu_over + [swap_fh(live.gu_give)],
    )
    live.drop("y_keep", "y_got", "gu_give")
    live.done(
        got=swap_c(live.send),
        qkv_t=grad_rows(live.sc, live.h1, live.d_lin, 1, n_sr, rows),
        down_give=plus(live.down_t[1], live.down_got[1], BF16),
    )
    live.drop("send")
    gu_sum = [
        (live.gu_m[2 + n].astype(F32) + live.gu_got0[n].astype(F32) + live.gu_over[n].astype(F32)).astype(BF16)
        for n in range(2)
    ]
    live.done(
        terms=over_quad(by_member_of_quad(plus(live.keep, live.got, BF16))),
        qkv_got=[swap_sb(v_) for v_ in live.qkv_t],
        down_over=swap_fh(live.down_give),
        qkv_m=grad_rows(live.sc, live.h1, live.d_lin, 0, n_sr, rows),
        out_t=grad_slices(live.sc, live.o, Rows(live.att_mine, live.att_other)) if natural else (),
        gu_sum=jnp.concatenate(gu_sum, 0),
    )
    live.drop("keep", "got", "h1", "d_lin", "qkv_t", "gu_m", "gu_got0", "gu_over", "down_give")
    _, input_low, sums1 = norm_step_back(live.terms, live.own_x, live.d_x2, live.gain1, 1)
    qkv_give = jnp.concatenate([plus(live.qkv_m[n], live.qkv_got[n], BF16) for n in range(2)], 0)
    y = live.x2_own + jnp.sum(live.y_terms.astype(F32), axis=0)
    live.done(
        input_low=input_low[0],
        sums1=sums1,
        gu_done=exchange(live.gu_sum.reshape(members, rows, -1)),
        qkv_over=swap_fh(qkv_give),
        out_got=[swap_sb(v_) for v_ in live.out_t[2:]],
        layer_out=give_back(y.astype(BF16)),
        down_grad=plus(live.down_t[0], live.down_got[0]) + live.down_over.astype(F32),
    )
    live.drop("down_t", "down_got", "down_over", "y_terms", "gu_sum")
    if natural:
        out_grad = swap_fh(plus(live.out_t[1], live.out_got[1], BF16)).astype(F32)
        out_grad = plus(live.out_t[0], live.out_got[0]) + out_grad
    else:
        d_att = jnp.stack([live.att_mine.reshape(2, N // 4, D), live.att_other.reshape(2, N // 4, D)], 1)
        t = lax.dot_general(live.o, d_att.reshape(N, D), TN, preferred_element_type=F32)
        t = jnp.where(jnp.arange(members)[:, None, None] == sr * 2 + fl, t[None], 0.0)
        out_grad = lax.psum_scatter(t.reshape(H * HD, D), EVERY, scatter_dimension=0, tiled=True)
    qkv_sum = jnp.concatenate([plus(live.qkv_m[2 + n], live.qkv_got[2 + n]) for n in range(2)], 0)
    qkv_sum = plus(qkv_sum, live.qkv_over, BF16)
    qkv_grad = uncolumns([exchange(qkv_sum.reshape(members, rows, -1))], qkv_back)
    input_grad, layer_out, down_grad = give_back(live.input_low), live.layer_out, live.down_grad
    gate_grad = uncolumns([live.gu_done], gate_back)
    up_grad = uncolumns([live.gu_done], up_back)
    sums1, sums2, bias_term = live.sums1, live.sums2, live.bias_term

    bias_term = bias_term.reshape(3, heads, HD).transpose(1, 0, 2)
    if natural:
        bias_term = bias_term.reshape(2, 1, 2, 1, -1)
        here = jnp.arange(n_sr)[None, :, None, None, None] == sr
        here = here & (jnp.arange(2)[None, None, None, :, None] == fl)
    else:
        bias_term = bias_term[None]
        here = jnp.arange(members)[:, None, None, None] == sr * 2 + fl
    bias_term = jnp.where(here, bias_term, 0.0).reshape(n_dev, -1)
    small = jnp.concatenate(
        [sums1[0].reshape(n_dev, -1), sums1[1].reshape(n_dev, -1)]
        + [sums2[0].reshape(n_dev, -1), sums2[1].reshape(n_dev, -1), bias_term],
        axis=1,
    )
    small = small.reshape(2, n_sr, 2, 2, -1).transpose(1, 3, 0, 2, 4).reshape(members, 4, -1)
    small = jnp.sum(exchange(small), axis=0).reshape(2, 2, -1)
    small = pick(small, sb) + swap_sb(pick(small, 1 - sb))
    small = pick(small, fh) + swap_fh(pick(small, 1 - fh))
    gain1_grad, bias1_grad, gain2_grad, bias2_grad = (
        small[n * rows : (n + 1) * rows] for n in range(4)
    )
    bias_grad = small[4 * rows :]
    return (
        layer_out,
        input_grad,
        gain1_grad,
        bias1_grad,
        qkv_grad,
        bias_grad,
        out_grad,
        gain2_grad,
        bias2_grad,
        gate_grad,
        up_grad,
        down_grad,
    )


def solution(mesh):
    names = dict(mesh.shape)
    n_seq, n_fsdp = names["seq"], names["fsdp"]
    fine = Mesh(mesh.devices.reshape(2, n_seq // 4, 2, 2, n_fsdp // 2), EVERY)
    tokens = P(None, ("fh", "fl"), ("sb", "sx", "c"), None)
    vector = P(EVERY)
    matrix = P(EVERY, None)
    in_specs = (tokens, tokens, P(None, ("fh", "fl"), None), vector, vector, matrix, vector, matrix)
    in_specs += (vector, vector, matrix, matrix, matrix)
    out_specs = (tokens, tokens, vector, vector, matrix, vector, matrix, vector, vector)
    out_specs += (matrix, matrix, matrix)
    return jax.shard_map(shards, mesh=fine, in_specs=in_specs, out_specs=out_specs, check_vma=False)
```

```python
import functools

import jax
import jax.numpy as jnp
import numpy as np
from jax import lax
from jax.experimental import pallas as pl
from jax.experimental.pallas import tpu as pltpu
from jax.sharding import Mesh
from jax.sharding import PartitionSpec as P

H = 32
HD = 64
ROT = 16

eps_norm = 1e-05
rope_base = 10000.0
masked_score = -1e30

F32 = jnp.float32
BF16 = jnp.bfloat16

SWAP = [(0, 1), (1, 0)]
EVERY = ("sb", "sx", "c", "fh", "fl")
MEMBERS = ("sx", "c", "fl")
QUAD = ("fl", "sx")
ANY = pl.BlockSpec(memory_space=pl.ANY)
SMEM = pl.BlockSpec(memory_space=pltpu.SMEM)
VMEM = pl.BlockSpec(memory_space=pltpu.VMEM)
NT = (((1,), (1,)), ((), ()))
TN = (((0,), (0,)), ((), ()))
LIMIT = 60 * 1024 * 1024


def params():
    return pltpu.CompilerParams(vmem_limit_bytes=LIMIT)


def cost(microseconds):
    return pl.CostEstimate(flops=int(microseconds * 1e9), bytes_accessed=1024, transcendentals=0)


def dot(a, b, dims=(((1,), (0,)), ((), ()))):
    return lax.dot_general(a, b, dims, preferred_element_type=F32)


def swap_sb(v):
    return lax.ppermute(v, "sb", SWAP)


def swap_fh(v):
    return lax.ppermute(v, "fh", SWAP)


def swap_fl(v):
    return lax.ppermute(v, "fl", SWAP)


def swap_c(v):
    return lax.ppermute(v, "c", SWAP)


def swap_sx(v, bit=1):
    n = lax.axis_size("sx")
    return lax.ppermute(v, "sx", [(i, i ^ bit) for i in range(n)])


def over_quad(v):
    return lax.all_to_all(v, QUAD, split_axis=0, concat_axis=0, tiled=True)


class Live(dict):
    def __getattr__(self, name):
        return self[name]

    def done(self, **new):
        self.update(new)
        self.update(lax.optimization_barrier(dict(self)))

    def drop(self, *names):
        for name in names:
            del self[name]


def normalize(values):
    average = jnp.mean(values, axis=-1, keepdims=True)
    centered = values - average
    inv_std = lax.rsqrt(jnp.mean(centered * centered, axis=-1, keepdims=True) + eps_norm)
    return centered * inv_std, inv_std


def normalize_back(grad_normed, normed, inv_std):
    first_mean = jnp.mean(grad_normed, axis=-1, keepdims=True)
    second_mean = jnp.mean(grad_normed * normed, axis=-1, keepdims=True)
    return inv_std * (grad_normed - first_mean - normed * second_mean)


def gather_first(x):
    return (x, swap_sx(x), swap_fl(x), swap_c(x))


def gather_second(first):
    n_sx = lax.axis_size("sx")
    x, a, b, xo = first
    h = x.shape[0] // 2
    d1 = swap_fl(a[:h])
    d2 = swap_sx(b[h:])
    ao = swap_c(a)
    bo = swap_c(b)
    got = [x, a, b, d1, d2, xo, ao, bo, swap_c(d1), swap_c(d2)]
    bit = 2
    while bit < n_sx:
        got = got + [swap_sx(v, bit) for v in got]
        bit *= 2
    return got


def gather_rows(n_sx, m):
    h = m // 2
    got = []
    for c in range(2):
        at = c * n_sx * m
        over = 2 * n_sx * m + at
        got += [at, at + m, over, over + m, over + m + h]
    bit = 2
    while bit < n_sx:
        got = got + [r + bit * m for r in got]
        bit *= 2
    return got


def add_first_kernel(keep, got, send_x, send_l, keep_x, keep_l):
    h = keep.shape[2] // 2
    for f in range(2):
        for x in range(2):
            q = keep[f, x].astype(F32) + got[f, x].astype(F32)
            if x == 1:
                send_x[f] = q[:h].astype(BF16)
            else:
                keep_x[f] = q[:h]
            if f == 1:
                send_l[x] = q[h:].astype(BF16)
            else:
                keep_l[x] = q[h:]


def add_second_kernel(keep_x, got_x, keep_l, got_l, send_x, send_l, own_x, own_l):
    own_x[...] = keep_x[0] + got_x[0].astype(F32)
    own_l[...] = keep_l[0] + got_l[0].astype(F32)
    send_x[...] = (keep_x[1] + got_x[1].astype(F32)).astype(BF16)
    send_l[...] = (keep_l[1] + got_l[1].astype(F32)).astype(BF16)


def add_first(keep, got):
    bit = keep.shape[1] // 2
    while bit >= 2:
        q = keep.astype(F32) + got.astype(F32)
        keep = q[:, :bit].astype(BF16)
        got = swap_sx(q[:, bit:].astype(BF16), bit)
        bit //= 2
    m, D = keep.shape[2:]
    h = m // 2
    low = jax.ShapeDtypeStruct((2, h, D), BF16)
    high = jax.ShapeDtypeStruct((2, h, D), F32)
    return pl.pallas_call(
        add_first_kernel,
        out_shape=[low, low, high, high],
        in_specs=[VMEM] * 2,
        out_specs=[VMEM] * 4,
        compiler_params=params(),
        cost_estimate=cost(4),
    )(keep, got)


def add_second(keep_x, got_x, keep_l, got_l):
    _, h, D = keep_x.shape
    return pl.pallas_call(
        add_second_kernel,
        out_shape=[jax.ShapeDtypeStruct((h, D), BF16)] * 2 + [jax.ShapeDtypeStruct((h, D), F32)] * 2,
        in_specs=[VMEM] * 4,
        out_specs=[VMEM] * 4,
        compiler_params=params(),
        cost_estimate=cost(3),
    )(keep_x, got_x, keep_l, got_l)


def in_order(pieces, sb, fh):
    w, z, y, yz = pieces
    a, b = jnp.where(fh == 1, z, w), jnp.where(fh == 1, w, z)
    c, d = jnp.where(fh == 1, yz, y), jnp.where(fh == 1, y, yz)
    first = jnp.stack([jnp.where(sb == 1, c, a), jnp.where(sb == 1, d, b)])
    second = jnp.stack([jnp.where(sb == 1, a, c), jnp.where(sb == 1, b, d)])
    return jnp.stack([first, second])


def flip_if(bit, v, axis):
    return jnp.where(bit == 1, lax.rev(v, (axis,)), v)


def xor_order(v, axis, index, n):
    shape = v.shape
    bit = 1
    while bit < n:
        r = v.reshape(shape[:axis] + (n // (2 * bit), 2, bit) + shape[axis + 1 :])
        v = flip_if((index // bit) % 2, r, axis + 1).reshape(shape)
        bit *= 2
    return v


def load_groups(sc, pieces, places, buf, sems, first=0, start=True):
    copies = []
    rows = buf.shape[4]
    for n, (piece, (k, r)) in enumerate(zip(pieces, places)):
        where = buf.at[sc[0] ^ (k // 2), pl.ds(r, piece.shape[0]), sc[1] ^ (k % 2)]
        copies.append(pltpu.make_async_copy(piece.at[:, :, pl.ds(first, rows)], where, sems.at[n]))
    for c in copies if start else ():
        c.start()
    return copies


def load_down(sc, pieces, places, buf, sems, start=True):
    copies = []
    for n, (piece, (k, r)) in enumerate(zip(pieces, places)):
        where = buf
        if len(places) > 1:
            where = buf.at[sc[0] ^ (k // 2), sc[1] ^ (k % 2), pl.ds(r, piece.shape[0])]
        copies.append(pltpu.make_async_copy(piece, where, sems.at[n]))
    for c in copies if start else ():
        c.start()
    return copies


class Rows:
    def __init__(self, arrays, firsts):
        self.arrays, self.firsts = list(arrays), firsts
        self.N, self.D = sum(v.shape[0] for v in arrays), arrays[0].shape[1]

    def scratch(self):
        return [pltpu.VMEM((self.N, self.D), BF16), pltpu.SemaphoreType.DMA((len(self.arrays),))]

    def load(self, sc, refs, buf, sems, start=True):
        copies = [
            pltpu.make_async_copy(ref, buf.at[pl.ds(r, ref.shape[0])], sems.at[n])
            for n, (ref, r) in enumerate(zip(refs, self.firsts))
        ]
        for c in copies if start else ():
            c.start()
        return copies


class Quads:
    def __init__(self, mine, other, m):
        self.arrays, self.m = [mine, other], m
        self.N, self.D = 2 * mine.shape[0], mine.shape[1]
        self.n_sx = mine.shape[0] // (2 * m)

    def scratch(self):
        return [pltpu.VMEM((self.N, self.D), BF16), pltpu.SemaphoreType.DMA((4 * self.n_sx,))]

    def load(self, sc, refs, buf, sems, start=True):
        copies = []
        for k in range(2):
            for f in range(2):
                for x in range(self.n_sx):
                    to = ((2 * (f ^ sc[2]) + k) * self.n_sx + (x ^ sc[3])) * self.m
                    copies.append(
                        pltpu.make_async_copy(
                            refs[k].at[pl.ds((f * self.n_sx + x) * self.m, self.m)],
                            buf.at[pl.ds(pl.multiple_of(to, self.m), self.m)],
                            sems.at[len(copies)],
                        )
                    )
        for c in copies if start else ():
            c.start()
        return copies


def sides(nb, by_index=False):
    def place(f, b, sc):
        if by_index:
            f, b = f ^ sc[2], b ^ (sc[3] // 2)
        return f * nb + b

    def keep(i, sc=None):
        f, k, b = i // (2 * nb), lax.rem(i // nb, 2), lax.rem(i, nb)
        return place(f, jnp.where(k == 0, b, nb - 1), sc)

    def send(i, sc=None):
        f, k, b = i // (2 * nb), lax.rem(i // nb, 2), lax.rem(i, nb)
        return place(f, jnp.where(k == 0, 0, b), sc)

    return keep, send


def columns_kernel(plan, n_in, *refs):
    ins, vectors, out = refs[:n_in], refs[n_in:-1], refs[-1]
    rows = ins[0].shape[0]
    if vectors:
        row = jnp.concatenate([v[...] for v in vectors], axis=-1)
    for t, ranges in enumerate(plan):
        out[t, :rows] = jnp.concatenate([ins[i][:, a : a + n] for i, a, n in ranges], axis=-1)
        if vectors:
            out[t, rows : rows + 1, : row.shape[1]] = row


def columns(arrays, plan, vectors=()):
    width = sum(n for _, _, n in plan[0])
    rows = arrays[0].shape[0] + (8 if vectors else 0)
    return pl.pallas_call(
        functools.partial(columns_kernel, plan, len(arrays)),
        out_shape=jax.ShapeDtypeStruct((len(plan), rows, width), arrays[0].dtype),
        in_specs=[VMEM] * (len(arrays) + len(vectors)),
        out_specs=VMEM,
        compiler_params=params(),
        cost_estimate=cost(3),
    )(*arrays, *vectors)


def uncolumns_kernel(plan, *refs):
    ins, out = refs[:-1], refs[-1]
    width = ins[0].shape[2]
    if True:
        at, group, size = 0, [], 0
        for t, b, n in plan:
            group.append(ins[b // width][t, :, b % width : b % width + n].astype(F32))
            size += n
            if size % 128 == 0:
                out[:, at : at + size] = jnp.concatenate(group, axis=-1)
                at, group, size = at + size, [], 0
        if group:
            out[:, at : at + size] = jnp.concatenate(group, axis=-1)


def uncolumns(arrays, plan):
    rows = arrays[0].shape[1]
    return pl.pallas_call(
        functools.partial(uncolumns_kernel, plan),
        out_shape=jax.ShapeDtypeStruct((rows, sum(n for _, _, n in plan)), F32),
        in_specs=[VMEM] * len(arrays),
        out_specs=VMEM,
        compiler_params=params(),
        cost_estimate=cost(3),
    )(*arrays)


def turn(v, c_ref_value, sa, sb_, direction):
    width = v.shape[1]
    back = pltpu.roll(v, ROT // 2, 1)
    front = pltpu.roll(v, width - ROT // 2, 1)
    return v * c_ref_value + direction * (back * sa + front * sb_)


def attention_kernel(dims, places, x_rows, sc, tables, id_row, id_col, w_out, *refs):
    heads, length, block, D = dims
    x_refs, refs = refs[: len(x_rows.arrays)], refs[len(x_rows.arrays) :]
    w_refs, refs = refs[: len(places)], refs[len(places) :]
    h1, q, k, v, o, lse, keep, send, vectors, w, sems, small, small_sems, bias_q, x_buf, x_sems = refs
    wide = heads * HD
    per = length // block
    i = pl.program_id(0)

    @pl.when(i == 0)
    def _():
        n_sr, rows_ = w.shape[1], w.shape[4]
        copies = x_rows.load(sc, x_refs, x_buf, x_sems)
        copies += load_groups(sc, w_refs, places, small, small_sems, rows_)
        for c in load_groups(sc, w_refs, places, w, sems) + copies:
            c.wait()
        every = [(s, j, f, l) for s in range(2) for j in range(n_sr) for f in range(2) for l in range(2)]
        for n in range(4):
            row = [small[s, j, f, l, 0:1, n * rows_ : (n + 1) * rows_] for s, j, f, l in every]
            vectors[n : n + 1, :] = jnp.concatenate(row, axis=-1).astype(F32)
        first = 4 * rows_
        if 3 * rows_ == 3 * HD:
            row = [
                small[a // 2, sc[4], a % 2, sc[2], 0:1, first + p * HD : first + (p + 1) * HD]
                for p in range(3)
                for a in range(heads)
            ]
        else:
            count = 3 * HD // (3 * rows_)
            row = []
            for a in range(heads):
                for n in range(count):
                    d = ((sc[4] * 2 + sc[2]) * heads + a) * count + n
                    at = (d // (4 * n_sr), lax.rem(d // 4, n_sr), lax.rem(d // 2, 2), lax.rem(d, 2))
                    row.append(small[at[0], at[1], at[2], at[3], 0:1, first : first + 3 * rows_])
        bias_q[...] = jnp.concatenate(row, axis=-1).astype(F32)

    rows = pl.ds(pl.multiple_of(i * block, block), block)
    normed, _ = normalize(x_buf[rows, :].astype(F32))
    h = (normed * vectors[0:1, :] + vectors[1:2, :]).astype(BF16)
    h1[...] = h
    lin = dot(h, w[...].reshape(D, 3 * wide)) + bias_q[...]
    qk = turn(lin[:, : 2 * wide], tables[0], tables[1], tables[2], 1.0)
    q[rows, :] = qk[:, :wide].astype(BF16)
    k[rows, :] = qk[:, wide:].astype(BF16)
    v[rows, :] = lin[:, 2 * wide :].astype(BF16)

    @pl.when(lax.rem(i, per) == per - 1)
    def _():
        s = i // per
        start = pl.multiple_of(s * length, length)
        step = min(length, (1 << 18) // length)
        for r in range(length // step):
            part = pl.ds(pl.multiple_of(start + r * step, step), step)
            allowed = id_col[part, 0:1] >= id_row[pl.ds(s, 1), :]
            for hd in range(heads):
                lanes = slice(hd * HD, (hd + 1) * HD)
                kh = k[pl.ds(start, length), lanes]
                vh = v[pl.ds(start, length), lanes]
                score = dot(q[part, lanes], kh, NT) * (HD**-0.5)
                score = jnp.where(allowed, score, masked_score)
                peak = jnp.max(score, axis=-1, keepdims=True)
                e = jnp.exp(score - peak)
                total = jnp.sum(e, axis=-1, keepdims=True)
                p = (e * (1.0 / total)).astype(BF16)
                o[part, lanes] = dot(p, vh).astype(BF16)
                lse[part, hd : hd + 1] = peak + jnp.log(total)
        for side, out in enumerate((keep, send)):
            for b in range(per // 2):
                part = pl.ds(pl.multiple_of(start + (side * (per // 2) + b) * block, block), block)
                out[0, b * block : (b + 1) * block] = dot(o[part, :], w_out[...]).astype(BF16)


def attention(sc, x_rows, tables, id_row, id_col, w_out, weight, heads, rows):
    N, D = x_rows.N, x_rows.D
    length = N // 2
    block = 256
    per = length // block
    wide = heads * HD
    n_sr, _, _, f = weight[0][0].shape
    places = [p[1:] for p in weight]
    whole = lambda shape: pl.BlockSpec(shape, lambda i, sc: (0,) * len(shape))
    side = pl.BlockSpec((1, length // 2, D), lambda i, sc: (i // per, 0, 0))
    spec = pltpu.PrefetchScalarGridSpec(
        num_scalar_prefetch=1,
        grid=(N // block,),
        in_specs=[
            pl.BlockSpec((3, block, 2 * wide), lambda i, sc: (0, lax.rem(i, per), 0)),
            whole((2, length)),
            whole((N, 1)),
            whole((wide, D)),
        ]
        + [ANY] * (len(x_rows.arrays) + len(places)),
        out_specs=[pl.BlockSpec((block, D), lambda i, sc: (i, 0))]
        + [whole((N, wide))] * 4
        + [whole((N, heads)), side, side, whole((4, D))],
        scratch_shapes=[
            pltpu.VMEM((2, n_sr, 2, 2, rows, f), BF16),
            pltpu.SemaphoreType.DMA((len(places),)),
            pltpu.VMEM((2, n_sr, 2, 2, 8, f), BF16),
            pltpu.SemaphoreType.DMA((len(places),)),
            pltpu.VMEM((1, 3 * wide), F32),
        ]
        + x_rows.scratch(),
    )
    return pl.pallas_call(
        functools.partial(attention_kernel, (heads, length, block, D), places, x_rows),
        grid_spec=spec,
        out_shape=[jax.ShapeDtypeStruct((N, D), BF16)]
        + [jax.ShapeDtypeStruct((N, wide), BF16)] * 4
        + [jax.ShapeDtypeStruct((N, heads), F32)]
        + [jax.ShapeDtypeStruct((2, length // 2, D), BF16)] * 2
        + [jax.ShapeDtypeStruct((4, D), F32)],
        compiler_params=params(),
        cost_estimate=cost(25),
    )(sc, tables, id_row, id_col, w_out, *x_rows.arrays, *[p[0] for p in weight])


def ffn_kernel(dims, h_rows, dy_rows, sc, *refs):
    g_list, d_list, block, nb, D, ff = dims
    h_refs, refs = refs[: len(h_rows.arrays)], refs[len(h_rows.arrays) :]
    dy_refs, refs = refs[: len(dy_rows.arrays)], refs[len(dy_rows.arrays) :]
    g_refs, refs = refs[: len(g_list)], refs[len(g_list) :]
    d_refs, refs = refs[: len(d_list)], refs[len(d_list) :]
    h2, act, d_gu, keep, send, g_buf, d_buf, sem_g, sem_d, h_buf, h_sems, dy_buf, dy_sems = refs
    i = pl.program_id(0)
    rows = pl.ds(pl.multiple_of(i * block, block), block)

    @pl.when(i == 0)
    def _():
        first = h_rows.load(sc, h_refs, h_buf, h_sems) + load_groups(sc, g_refs, g_list, g_buf, sem_g)
        dy_rows.load(sc, dy_refs, dy_buf, dy_sems)
        load_down(sc, d_refs, d_list, d_buf, sem_d)
        for c in first:
            c.wait()

    h = h_buf[rows, :]
    h2[...] = h
    w_gu = g_buf[...].reshape(D, 2 * ff)
    gu = dot(h, w_gu)
    g, u = gu[:, :ff], gu[:, ff:]
    s = jax.nn.sigmoid(g)
    silu = g * s
    act[...] = (silu * u).astype(BF16)

    @pl.when(i == 0)
    def _():
        second = dy_rows.load(sc, dy_refs, dy_buf, dy_sems, False)
        for c in second + load_down(sc, d_refs, d_list, d_buf, sem_d, False):
            c.wait()

    d_act = dot(dy_buf[rows, :], d_buf[...].reshape(ff, D), NT)
    d_g = (d_act * u * s * (1.0 + g * (1.0 - s))).astype(BF16)
    d_u = (d_act * silu).astype(BF16)
    d = jnp.concatenate([d_g, d_u], axis=-1)
    d_gu[...] = d
    d_h = dot(d, w_gu, NT).astype(BF16)
    side = lax.rem(i // nb, 2)

    @pl.when(side == 0)
    def _():
        keep[...] = d_h

    @pl.when(side == 1)
    def _():
        send[...] = d_h


def ffn(sc, h_rows, dy_rows, gu, down, down_places, rows_):
    N, D = h_rows.N, h_rows.D
    block = 256
    nb = N // 4 // block
    n_sr, _, _, two_ff = gu[0][0].shape
    ff = two_ff // 2
    rows = lambda width: pl.BlockSpec((block, width), lambda i, sc: (i, 0))
    d_shape = (2, 2, ff // 4, D) if len(down) > 1 else (ff, D)
    keep, send = sides(nb)
    spec = pltpu.PrefetchScalarGridSpec(
        num_scalar_prefetch=1,
        grid=(N // block,),
        in_specs=[ANY] * (len(h_rows.arrays) + len(dy_rows.arrays) + len(gu) + len(down)),
        out_specs=[
            rows(D),
            rows(ff),
            rows(2 * ff),
            pl.BlockSpec((block, D), lambda i, sc: (keep(i), 0)),
            pl.BlockSpec((block, D), lambda i, sc: (send(i), 0)),
        ],
        scratch_shapes=[
            pltpu.VMEM((2, n_sr, 2, 2, rows_, two_ff), BF16),
            pltpu.VMEM(d_shape, BF16),
            pltpu.SemaphoreType.DMA((len(gu),)),
            pltpu.SemaphoreType.DMA((len(down),)),
        ]
        + h_rows.scratch()
        + dy_rows.scratch(),
    )
    dims = ([p[1:] for p in gu], down_places, block, nb, D, ff)
    return pl.pallas_call(
        functools.partial(ffn_kernel, dims, h_rows, dy_rows),
        grid_spec=spec,
        out_shape=[
            jax.ShapeDtypeStruct((N, D), BF16),
            jax.ShapeDtypeStruct((N, ff), BF16),
            jax.ShapeDtypeStruct((N, 2 * ff), BF16),
            jax.ShapeDtypeStruct((N // 2, D), BF16),
            jax.ShapeDtypeStruct((N // 2, D), BF16),
        ],
        compiler_params=params(),
        cost_estimate=cost(30),
    )(sc, *h_rows.arrays, *dy_rows.arrays, *[p[0] for p in gu], *down)


def down_kernel(d_list, nb, ff, D, sc, act, *refs):
    n_d = len(d_list)
    d_refs, (keep, send, d_buf, sem) = refs[:n_d], refs[n_d:]
    i = pl.program_id(0)

    @pl.when(i == 0)
    def _():
        for c in load_down(sc, d_refs, d_list, d_buf, sem):
            c.wait()

    y = dot(act[...], d_buf[...].reshape(ff, D)).astype(BF16)
    side = lax.rem(i // nb, 2)
    m = y.shape[0] // 2
    for k, out in enumerate((keep, send)):
        for t in range(2):

            @pl.when((side == k) & (lax.rem(sc[3], 2) == t))
            def _():
                out[t * m : (t + 1) * m, :] = y[:m]
                out[(1 - t) * m : (2 - t) * m, :] = y[m:]


def down_product(sc, act, down, places):
    N, ff = act.shape
    D = down[0].shape[-1]
    block = 256
    nb = N // 4 // block
    d_shape = (2, 2, ff // 4, D) if len(down) > 1 else (ff, D)
    keep, send = sides(nb, by_index=True)
    spec = pltpu.PrefetchScalarGridSpec(
        num_scalar_prefetch=1,
        grid=(N // block,),
        in_specs=[pl.BlockSpec((block, ff), lambda i, sc: (i, 0))] + [ANY] * len(down),
        out_specs=[
            pl.BlockSpec((block, D), lambda i, sc: (keep(i, sc), 0)),
            pl.BlockSpec((block, D), lambda i, sc: (send(i, sc), 0)),
        ],
        scratch_shapes=[pltpu.VMEM(d_shape, BF16), pltpu.SemaphoreType.DMA((len(down),))],
    )
    return pl.pallas_call(
        functools.partial(down_kernel, places, nb, ff, D),
        grid_spec=spec,
        out_shape=[jax.ShapeDtypeStruct((N // 2, D), BF16)] * 2,
        compiler_params=params(),
        cost_estimate=cost(9),
    )(sc, act, *down)


def h_buf_rows(length):
    return 256 if length <= 1024 else 128


def attention_back_kernel(dims, d_rows, sc, tables, id_row, id_col, q, k, v, lse, w_out, h1, vectors, *refs):
    heads, length, N, D, w_list = dims
    block = h_buf_rows(length)
    d_refs, refs = refs[: len(d_rows.arrays)], refs[len(d_rows.arrays) :]
    w_refs, refs = refs[: len(w_list)], refs[len(w_list) :]
    d_lin, bias_grad, sums, keep, send, w, d_o, d_qk, sem_w, h_buf, sem_h, d_att, sem_d = refs
    wide = heads * HD
    copies = d_rows.load(sc, d_refs, d_att, sem_d)
    loads = load_groups(sc, w_refs, w_list, w, sem_w)
    h_loads = [
        pltpu.make_async_copy(h1.at[pl.ds(n * block, block)], h_buf.at[n % 2], sem_h.at[n % 2])
        for n in range(N // block)
    ]
    h_loads[0].start()
    for c in copies:
        c.wait()
    sums[...] = jnp.zeros_like(sums)
    step = min(length, (1 << 18) // length)
    scale = HD**-0.5
    bias_grad[...] = jnp.zeros_like(bias_grad)
    for s in range(2):
        start = s * length
        for r in range(length // step):
            at = pl.ds(start + r * step, step)
            d_o[pl.ds(r * step, step), :] = dot(d_att[at, :], w_out[...], NT).astype(BF16)
        d_qk[:, wide:] = jnp.zeros_like(d_qk[:, wide:])
        for hd in range(heads):
            lanes = slice(hd * HD, (hd + 1) * HD)
            k_lanes = slice(wide + hd * HD, wide + (hd + 1) * HD)
            v_lanes = slice(2 * wide + hd * HD, 2 * wide + (hd + 1) * HD)
            kh = k[pl.ds(start, length), lanes]
            vh = v[pl.ds(start, length), lanes]
            for r in range(length // step):
                part = pl.ds(start + r * step, step)
                local = pl.ds(r * step, step)
                allowed = id_col[part, 0:1] >= id_row[s : s + 1, :]
                qh = q[part, lanes]
                score = dot(qh, kh, NT) * scale
                p = jnp.where(allowed, jnp.exp(score - lse[part, hd : hd + 1]), 0.0)
                doh = d_o[local, lanes]
                dp = dot(doh, vh, NT)
                inner = jnp.sum(p * dp, axis=-1, keepdims=True)
                ds = (p * (dp - inner)).astype(BF16)
                d_qk[local, lanes] = dot(ds, kh) * scale
                dk = dot(ds, qh, TN) * scale
                dv = dot(p.astype(BF16), doh, TN)
                if length == step:
                    d_qk[:, k_lanes] = dk
                    d_qk[:, v_lanes] = dv
                else:
                    d_qk[:, k_lanes] += dk
                    d_qk[:, v_lanes] += dv
        if s == 0:
            for c in loads:
                c.wait()
        half = length // 2
        for b in range(length // block):
            local = pl.ds(b * block, block)
            at = pl.ds(start + b * block, block)
            qk = turn(d_qk[local, : 2 * wide], tables[0, local], tables[1, local], tables[2, local], -1.0)
            lin = jnp.concatenate([qk, d_qk[local, 2 * wide :]], axis=-1).astype(BF16)
            d_lin[at, :] = lin
            bias_grad[...] += jnp.sum(lin.astype(F32), axis=0, keepdims=True)
            d_h = dot(lin, w[...].reshape(D, 3 * wide), NT)
            n = (start + b * block) // block
            h_loads[n].wait()
            if n + 1 < N // block:
                h_loads[n + 1].start()
            sums[0:1, :] += jnp.sum(d_h * h_buf[n % 2].astype(F32), axis=0, keepdims=True)
            sums[1:2, :] += jnp.sum(d_h, axis=0, keepdims=True)
            d_h = d_h.astype(BF16)
            out = keep if b * block < half else send
            out[pl.ds(s * half + (b * block) % half, block), :] = d_h
    sums[0:1, :] = (sums[0:1, :] - vectors[1:2, :] * sums[1:2, :]) / vectors[0:1, :]


def attention_back(sc, tables, id_row, id_col, q, k, v, lse, w_out, h1, vectors, d_rows, weight):
    N, wide = q.shape
    D = w_out.shape[1]
    heads = wide // HD
    length = N // 2
    n_sr, _, _, f = weight[0][0].shape
    rows = D // (8 * n_sr)
    dims = (heads, length, N, D, [p[1:] for p in weight])
    return pl.pallas_call(
        functools.partial(attention_back_kernel, dims, d_rows),
        out_shape=[
            jax.ShapeDtypeStruct((N, 3 * wide), BF16),
            jax.ShapeDtypeStruct((1, 3 * wide), F32),
            jax.ShapeDtypeStruct((2, D), F32),
            jax.ShapeDtypeStruct((N // 2, D), BF16),
            jax.ShapeDtypeStruct((N // 2, D), BF16),
        ],
        in_specs=[SMEM] + [VMEM] * 8 + [ANY, VMEM] + [ANY] * (len(d_rows.arrays) + len(weight)),
        out_specs=[VMEM] * 5,
        scratch_shapes=[
            pltpu.VMEM((2, n_sr, 2, 2, rows, f), BF16),
            pltpu.VMEM((length, wide), BF16),
            pltpu.VMEM((length, 3 * wide), F32),
            pltpu.SemaphoreType.DMA((len(weight),)),
            pltpu.VMEM((2, h_buf_rows(length), D), BF16),
            pltpu.SemaphoreType.DMA((2,)),
        ]
        + d_rows.scratch(),
        compiler_params=params(),
        cost_estimate=cost(23),
    )(sc, tables, id_row, id_col, q, k, v, lse, w_out, h1, vectors, *d_rows.arrays, *[p[0] for p in weight])


def rows_kernel(dims, sc, h, d, *outs):
    n, two_rows = dims
    t = dot(h[...], d[...], TN).astype(BF16)
    i = pl.program_id(0)
    others, same = outs[:-1], outs[-1]
    for f in range(2):
        places = [(same, sc[1] == f)]
        for k, other in enumerate(others):
            places.append((other, (sc[1] != f) if len(others) == 1 else (sc[1] != f) & (i == k)))
        for out, here in places:

            @pl.when(here)
            def _():
                for j in range(n):
                    r = (2 * j + f) * two_rows
                    out[j * two_rows : (j + 1) * two_rows, :] = t[r : r + two_rows]


def grad_rows(sc, h, d, side, n_sr, rows, parts=2):
    N, D = h.shape
    f = d.shape[1]
    cut = D // 4
    n = n_sr // 2
    half, whole = pl.BlockSpec((cut // 2, f), lambda i, sc: (0, 0)), pl.BlockSpec((cut // 2, f), lambda i, sc: (i, 0))
    shape = lambda r: jax.ShapeDtypeStruct((r, f), BF16)
    spec = pltpu.PrefetchScalarGridSpec(
        num_scalar_prefetch=1,
        grid=(2,),
        in_specs=[
            pl.BlockSpec((N, cut), lambda i, sc: (0, (sc[0] ^ side) * 2 + i)),
            pl.BlockSpec((N, f), lambda i, sc: (0, 0)),
        ],
        out_specs=([half] * 2 if parts == 2 else [whole]) + [whole],
    )
    return pl.pallas_call(
        functools.partial(rows_kernel, (n, 2 * rows)),
        grid_spec=spec,
        out_shape=([shape(cut // 2)] * 2 if parts == 2 else [shape(cut)]) + [shape(cut)],
        compiler_params=params(),
        cost_estimate=cost(7),
    )(sc, h, d)


def slices_kernel(rows, cut, d_rows, sc, a, *refs):
    d_refs, refs = refs[: len(d_rows.arrays)], refs[len(d_rows.arrays) :]
    outs, (buf, sems) = refs[:4], refs[4:]
    i = pl.program_id(0)

    @pl.when(i == 0)
    def _():
        for c in d_rows.load(sc, d_refs, buf, sems):
            c.wait()

    d = buf[:, pl.ds(pl.multiple_of(i * cut, cut), cut)]
    t = dot(a[...], d, TN).astype(BF16)
    for n in range(4):
        for k in range(4):

            @pl.when((sc[0] == (n // 2) ^ (k // 2)) & (sc[1] == (n % 2) ^ (k % 2)))
            def _():
                outs[k][...] = t[n * rows : (n + 1) * rows]


def grad_slices(sc, a, d_rows):
    N, f = a.shape
    D = d_rows.D
    cut = D // 4
    spec = pltpu.PrefetchScalarGridSpec(
        num_scalar_prefetch=1,
        grid=(D // cut,),
        in_specs=[pl.BlockSpec((N, f), lambda i, sc: (0, 0))] + [ANY] * len(d_rows.arrays),
        out_specs=[pl.BlockSpec((f // 4, cut), lambda i, sc: (0, i))] * 4,
        scratch_shapes=d_rows.scratch(),
    )
    return pl.pallas_call(
        functools.partial(slices_kernel, f // 4, cut, d_rows),
        grid_spec=spec,
        out_shape=[jax.ShapeDtypeStruct((f // 4, D), BF16)] * 4,
        compiler_params=params(),
        cost_estimate=cost(9),
    )(sc, a, *d_rows.arrays)


def total_of(u0, u1, w0, w1):
    return jnp.concatenate([u0[...] + u1[...].astype(F32), w0[...] + w1[...].astype(F32)], axis=0)


def forward_kernel(u0, u1, w0, w1, x, vectors, x2, low):
    v = x[...].astype(F32) + total_of(u0, u1, w0, w1)
    x2[...] = v
    normed, _ = normalize(v)
    low[...] = (normed * vectors[2:3, :] + vectors[3:4, :]).astype(BF16)


def norm_step(terms, x, vectors):
    m, D = x.shape
    return pl.pallas_call(
        forward_kernel,
        out_shape=[jax.ShapeDtypeStruct((m, D), F32), jax.ShapeDtypeStruct((m, D), BF16)],
        in_specs=[VMEM] * 6,
        out_specs=[VMEM] * 2,
        compiler_params=params(),
        cost_estimate=cost(4),
    )(*terms, x, vectors)


def back_kernel(which, u0, u1, w0, w1, x, dy, vectors, grad, low, sums):
    d_h = total_of(u0, u1, w0, w1)
    normed, inv_std = normalize(x[...].astype(F32))
    total = dy[...].astype(F32) + normalize_back(d_h * vectors[which : which + 1, :], normed, inv_std)
    grad[...] = total
    low[...] = total.astype(BF16)
    sums[0:1, :] = jnp.sum(d_h * normed, axis=0, keepdims=True)
    sums[1:2, :] = jnp.sum(d_h, axis=0, keepdims=True)


def norm_step_back(terms, x, dy, vectors, which):
    m, D = x.shape
    return pl.pallas_call(
        functools.partial(back_kernel, which),
        out_shape=[
            jax.ShapeDtypeStruct((m, D), F32),
            jax.ShapeDtypeStruct((m, D), BF16),
            jax.ShapeDtypeStruct((2, D), F32),
        ],
        in_specs=[VMEM] * 7,
        out_specs=[VMEM] * 3,
        compiler_params=params(),
        cost_estimate=cost(4),
    )(*terms, x, dy, vectors)


def shards(
    inputs,
    cotangent,
    block_ids,
    ln1_gain,
    ln1_bias,
    qkv_weight,
    qkv_bias,
    out_weight,
    ln2_gain,
    ln2_bias,
    gate_weight,
    up_weight,
    down_weight,
):
    sb, sx, c, fh, fl = (lax.axis_index(a).astype(jnp.int32) for a in EVERY)
    n_sx = lax.axis_size("sx")
    sr, n_sr = sx * 2 + c, 2 * n_sx
    quad = 2 * n_sx
    n_dev = 8 * n_sr
    members = 2 * n_sr
    tok = inputs.shape[2]
    m = 2 * tok
    D = inputs.shape[3]
    length = block_ids.shape[2]
    N = 2 * length
    rows = qkv_weight.shape[0]
    ff_rows = down_weight.shape[0]
    ff = 4 * ff_rows
    heads = H // members
    wide = heads * HD
    natural = H % n_dev == 0
    sc = jnp.stack([sb, fh, fl, sx, sr])

    def pick(v, i):
        return lax.dynamic_index_in_dim(v, i, 0, keepdims=False)

    def device_of(t, a):
        return (((a // 2) * n_sr + t // 2) * 2 + a % 2) * 2 + t % 2

    def head_of(t, i):
        return device_of(t, i) if natural else t * heads + i

    qkv_plan = [
        [(0, (head_of(t, i) * 3 + part) * HD, HD) for part in range(3) for i in range(heads)]
        for t in range(members)
    ]
    gu_plan = [
        [(w, device_of(t, a) * ff_rows, ff_rows) for w in range(2) for a in range(4)]
        for t in range(members)
    ]
    head_place = {head_of(t, i): (t, i) for t in range(members) for i in range(heads)}
    qkv_back = [
        (head_place[h][0], part * wide + head_place[h][1] * HD, HD) for h in range(H) for part in range(3)
    ]
    ff_place = {device_of(t, a): (t, a) for t in range(members) for a in range(4)}
    gate_back = [(ff_place[d][0], ff_place[d][1] * ff_rows, ff_rows) for d in range(n_dev)]
    up_back = [(t, ff + b, n) for t, b, n in gate_back]

    def exchange(v):
        return lax.all_to_all(v, MEMBERS, split_axis=0, concat_axis=0, tiled=True)

    def of_rows(v):
        return v.reshape((n_sr, 2) + v.shape[1:])

    def both(bit, own, other):
        return jnp.stack([jnp.where(bit == 0, own, other), jnp.where(bit == 0, other, own)])

    my_ids = pick(block_ids, sb)
    c_of = (jnp.arange(2, dtype=jnp.int32) ^ c)[:, None, None, None]
    sx_of = (jnp.arange(n_sx, dtype=jnp.int32) ^ sx)[None, :, None, None]
    sb_of = (jnp.arange(2, dtype=jnp.int32) ^ sb)[None, None, :, None]
    pos = ((sb_of * n_sx + sx_of) * 2 + c_of) * tok + jnp.arange(tok, dtype=jnp.int32)[None, None, None, :]
    pos = pos.reshape(-1)
    half = ROT // 2
    lane = np.arange(2 * wide) % HD
    turned = lane < ROT
    frequency = np.where(turned, rope_base ** (-2.0 * (lane % half).astype(np.float32) / ROT), 0.0)
    angles = pos.astype(F32)[:, None] * jnp.asarray(frequency, F32)[None, :]
    sine = jnp.sin(angles)
    to_back = jnp.asarray(np.where(turned & (lane >= half), 1.0, 0.0), F32)
    to_front = jnp.asarray(np.where(lane < half, -1.0, 0.0), F32)
    tables = jnp.stack([jnp.cos(angles), sine * to_back, sine * to_front])

    rep = lambda v_: jnp.broadcast_to(v_[None], (quad,) + v_.shape)
    flat = lambda v_: v_.reshape(-1, v_.shape[-1])
    blocks = lambda v_: v_.reshape(2, n_sx, m, D)
    firsts = gather_rows(n_sx, m)

    def plus(a_, b_, kind=F32):
        return (a_.astype(F32) + b_.astype(F32)).astype(kind)

    vectors = [v_[None] for v_ in (ln1_gain, ln1_bias, ln2_gain, ln2_bias, qkv_bias)]
    live = Live(
        sc=sc,
        inputs=inputs,
        cotangent=cotangent,
        my_ids=my_ids,
        out_w=out_weight,
        gate_w=gate_weight,
        up_w=up_weight,
        down_w=down_weight,
    )
    half_rows = ff_rows // 32 * 16 if ff_rows % 16 == 0 else ff_rows // 2
    live.done(qkv_c=columns([qkv_weight], qkv_plan, vectors))
    give = jnp.concatenate([pick(live.inputs, 1 - sb)[0], pick(live.cotangent, 1 - sb)[0]], 0)
    live.done(
        w_qkv=of_rows(exchange(live.qkv_c)),
        got=swap_sb(give),
        out_1=swap_fh(live.out_w) if natural else live.out_w,
        out_2=swap_sb(live.out_w) if natural else live.out_w,
        ids_got=swap_fl(live.my_ids),
        gu_c=columns([live.gate_w, live.up_w], gu_plan),
        down_a=live.down_w[:half_rows],
        down_b=live.down_w[half_rows:],
        tables=tables,
    )

    own_x = jnp.concatenate([pick(live.inputs, sb)[0], live.got[:tok]], 0)
    own_dy = jnp.concatenate([pick(live.cotangent, sb)[0], live.got[tok:]], 0)
    ids = both(fl, live.my_ids, live.ids_got).reshape(2, 2, n_sx, 2, tok)
    ids = flip_if(fl, flip_if(c, flip_if(sb, ids, 1), 3), 0)
    ids = xor_order(ids, 2, sx, n_sx).transpose(0, 3, 2, 1, 4).reshape(2, length)
    live.drop("inputs", "cotangent", "got", "my_ids", "ids_got", "gate_w", "up_w", "qkv_c")
    live.done(
        qkv_1=swap_fh(live.w_qkv),
        qkv_2=swap_sb(live.w_qkv),
        w_gu=of_rows(exchange(live.gu_c)),
        own_x=own_x,
        own_dy=own_dy,
        x_first=gather_first(own_x),
        out_3=swap_sb(live.out_1) if natural else live.out_w,
        ids=ids,
        id_col=ids.reshape(N, 1),
        dy_rep=rep(own_dy),
    )

    cuts = [n_sr * n // 4 for n in (0, 1, 3, 4)]
    part = [live.w_gu[a_:b_] for a_, b_ in zip(cuts, cuts[1:])]
    if natural:
        out_own = in_order((live.out_w, live.out_1, live.out_2, live.out_3), sb, fh)
        out_own = out_own.reshape(wide, D)
    else:
        out_all = lax.all_gather(out_weight, EVERY, axis=0, tiled=True)
        out_own = lax.dynamic_slice_in_dim(out_all, (sr * 2 + fl) * wide, wide, 0)
    live.done(
        qkv_3=swap_sb(live.qkv_1),
        x_all=gather_second(live.x_first),
        gu_1=[swap_fh(part[0])],
        gu_part=part,
        out_own=out_own,
    )

    qkv = lambda: [(live.w_qkv, 0, 0), (live.qkv_1, 1, 0), (live.qkv_2, 2, 0), (live.qkv_3, 3, 0)]
    h1, q, k, v, o, lse, keep, send, vectors = attention(
        live.sc,
        Rows(live.x_all, firsts),
        live.tables,
        live.ids,
        live.id_col,
        live.out_own,
        qkv(),
        heads,
        rows,
    )
    live.drop("x_first", "x_all", "out_w", "out_1", "out_2", "out_3", "gu_c")
    live.done(
        h1=h1,
        q=q,
        k=k,
        v=v,
        o=o,
        lse=lse,
        keep=keep,
        send=send,
        vectors=vectors,
        gu_1=live.gu_1 + [swap_fh(live.gu_part[1])],
        gu_2=swap_sb(live.w_gu),
        dy_mine=flat(over_quad(live.dy_rep)),
    )
    live.drop("dy_rep")

    live.done(got=swap_c(live.send), dy_other=swap_c(live.dy_mine))
    send_x, send_l, keep_x, keep_l = add_first(blocks(live.keep), blocks(live.got))
    live.done(
        keep=(keep_x, keep_l),
        got=(swap_sx(send_x), swap_fl(send_l)),
        gu_1=live.gu_1 + [swap_fh(live.gu_part[2])],
        gu_3=[swap_sb(v_) for v_ in live.gu_1],
    )
    send_x, send_l, keep_x, keep_l = add_second(live.keep[0], live.got[0], live.keep[1], live.got[1])
    live.done(
        keep=(keep_x, keep_l),
        got=(swap_fl(send_x), swap_sx(send_l)),
        down_1b=swap_fh(live.down_b),
        down_2=swap_sb(live.down_w),
        gu_3=live.gu_3 + [swap_sb(live.gu_1[2])],
    )
    terms = (live.keep[0], live.got[0], live.keep[1], live.got[1])
    x2_own, h2_own = norm_step(terms, live.own_x, live.vectors)
    live.done(
        x2_own=x2_own,
        h2_first=gather_first(h2_own),
        down_3b=swap_sb(live.down_1b),
        down_1a=swap_fh(live.down_a),
    )
    live.done(h2_all=gather_second(live.h2_first), down_3a=swap_sb(live.down_1a))

    down = [live.down_w, live.down_1a, live.down_1b, live.down_2, live.down_3a, live.down_3b]
    down_places = [(0, 0), (1, 0), (1, half_rows), (2, 0), (3, 0), (3, half_rows)]
    if ff_rows % 16 != 0:
        down = [live.down_w, jnp.concatenate(down[1:3], 0), live.down_2, jnp.concatenate(down[4:6], 0)]
        down, down_places = [in_order(down, sb, fh).reshape(ff, D)], [(0, 0)]
    gu = [(live.w_gu, 0, 0), (live.gu_2, 2, 0)]
    gu += [(v_, 1, n) for n, v_ in zip(cuts, live.gu_1)] + [(v_, 3, n) for n, v_ in zip(cuts, live.gu_3)]
    h2, act, d_gu, keep, send = ffn(
        live.sc,
        Rows(live.h2_all, firsts),
        Quads(live.dy_mine, live.dy_other, m),
        gu,
        down,
        down_places,
        rows,
    )
    live.drop("w_gu", "gu_1", "gu_2", "gu_3", "gu_part", "down_a", "down_b", "down_w")
    live.drop("down_1a", "down_1b", "down_2", "down_3a", "down_3b")
    live.drop("h2_first", "h2_all")

    def give_back(v_):
        other = swap_sb(v_[tok:])
        first = jnp.where(sb == 0, v_[:tok], other)
        second = jnp.where(sb == 0, other, v_[:tok])
        return jnp.stack([first, second])[:, None]

    live.done(
        h2=h2,
        act=act,
        d_gu=d_gu,
        down=down,
        keep=keep,
        got=swap_c(send),
        gu_t=grad_rows(live.sc, h2, d_gu, 1, n_sr, rows),
    )
    send_x, send_l, keep_x, keep_l = add_first(blocks(live.keep), blocks(live.got))
    y_keep, y_send = down_product(live.sc, live.act, live.down, down_places)
    live.drop("down")
    live.done(
        keep=(keep_x, keep_l),
        got=(swap_sx(send_x), swap_fl(send_l)),
        gu_got1=swap_sb(live.gu_t[0]),
        gu_m=grad_rows(live.sc, live.h2, live.d_gu, 0, n_sr, rows),
        y_keep=y_keep,
        y_send=y_send,
    )
    live.drop("h2", "d_gu")
    send_x, send_l, keep_x, keep_l = add_second(live.keep[0], live.got[0], live.keep[1], live.got[1])
    halves = lambda v_: (v_[: v_.shape[0] // 2], v_[v_.shape[0] // 2 :])
    gu_give = [plus(a_, b_, BF16) for a_, b_ in zip(halves(live.gu_m[0]), halves(live.gu_got1))]
    live.done(
        keep=(keep_x, keep_l),
        got=(swap_fl(send_x), swap_sx(send_l)),
        gu_got1=swap_sb(live.gu_t[1]),
        gu_over=[swap_fh(gu_give[0])],
        gu_give=gu_give[1],
        down_t=grad_slices(live.sc, live.act, Quads(live.dy_mine, live.dy_other, m)),
        y_got=swap_c(live.y_send),
    )
    live.drop("dy_mine", "dy_other", "act", "y_send")
    terms = (live.keep[0], live.got[0], live.keep[1], live.got[1])
    d_x2, d_att, sums2 = norm_step_back(terms, live.x2_own, live.own_dy, live.vectors, 2)
    gu_give = [plus(a_, b_, BF16) for a_, b_ in zip(halves(live.gu_m[1]), halves(live.gu_got1))]
    live.done(
        d_x2=d_x2,
        sums2=sums2,
        att_first=gather_first(d_att),
        gu_over=live.gu_over + [swap_fh(live.gu_give)],
        gu_give=gu_give,
        down_got1=swap_sb(live.down_t[3]),
        y_sum=plus(live.y_keep, live.y_got, BF16),
    )
    live.drop("gu_got1", "y_keep", "y_got")
    down_cut = live.down_t[1].shape[0] // 32 * 16
    down_give = plus(live.down_t[1], live.down_got1, BF16)
    live.done(
        att_all=gather_second(live.att_first),
        gu_over=live.gu_over + [swap_fh(live.gu_give[0])],
        down_got0=swap_sb(live.down_t[2]),
        down_give=(down_give[:down_cut], down_give[down_cut:]),
    )
    live.drop("att_first")
    d_lin, bias_term, sums1, keep, send = attention_back(
        live.sc,
        live.tables,
        live.ids,
        live.id_col,
        live.q,
        live.k,
        live.v,
        live.lse,
        live.out_own,
        live.h1,
        live.vectors,
        Rows(live.att_all, firsts),
        qkv(),
    )
    live.drop("q", "k", "v", "lse", "out_own", "w_qkv", "qkv_1", "qkv_2", "qkv_3", "tables", "ids", "id_col")
    live.done(
        d_lin=d_lin,
        bias_term=bias_term,
        sums1=sums1,
        keep=keep,
        send=send,
        y_terms=over_quad(live.y_sum.reshape(quad, m, D)),
        gu_got0=swap_sb(live.gu_t[2]),
        gu_over=live.gu_over + [swap_fh(live.gu_give[1])],
    )
    live.drop("gu_give", "y_sum", "down_got1", "gu_t")
    live.done(
        got=swap_c(live.send),
        qkv_t=grad_rows(live.sc, live.h1, live.d_lin, 1, n_sr, rows, 1),
    )
    live.drop("send")

    def half_sum(v_, bit, swap):
        n = v_.shape[1] // 2
        take = lambda k: lax.dynamic_slice_in_dim(v_, k * n, n, 1)
        return take(bit) + swap(take(1 - bit))

    bias_term = live.bias_term.reshape(3, heads, HD).transpose(1, 0, 2)
    if natural:
        bias_term = bias_term.reshape(2, 1, 2, 1, -1)
        here = jnp.arange(n_sr)[None, :, None, None, None] == sr
        here = here & (jnp.arange(2)[None, None, None, :, None] == fl)
    else:
        bias_term = bias_term[None]
        here = jnp.arange(members)[:, None, None, None] == sr * 2 + fl
    bias_term = jnp.where(here, bias_term, 0.0).reshape(n_dev, 3, rows).transpose(1, 0, 2).reshape(3, D)
    gu_sum = plus(live.gu_m[2], live.gu_got0) + jnp.concatenate(live.gu_over, 0).astype(F32)
    send_x, send_l, keep_x, keep_l = add_first(blocks(live.keep), blocks(live.got))
    live.done(
        keep=(keep_x, keep_l),
        got=(swap_sx(send_x), swap_fl(send_l)),
        qkv_got1=swap_sb(live.qkv_t[0]),
        down_over=[swap_fh(live.down_give[1])],
        down_give=live.down_give[0],
        qkv_m=grad_rows(live.sc, live.h1, live.d_lin, 0, n_sr, rows, 1),
        gu_sum=gu_sum.astype(BF16),
        small=jnp.concatenate([live.sums1, live.sums2, bias_term], axis=0),
        out_t=grad_slices(live.sc, live.o, Rows(live.att_all, firsts)) if natural else (),
    )
    live.drop("h1", "d_lin", "gu_m", "gu_got0", "gu_over")
    send_x, send_l, keep_x, keep_l = add_second(live.keep[0], live.got[0], live.keep[1], live.got[1])
    qkv_give = [plus(a_, b_, BF16) for a_, b_ in zip(halves(live.qkv_m[0]), halves(live.qkv_got1))]
    live.done(
        keep=(keep_x, keep_l),
        got=(swap_fl(send_x), swap_sx(send_l)),
        qkv_got0=swap_sb(live.qkv_t[1]),
        qkv_over=[swap_fh(qkv_give[0])],
        qkv_give=qkv_give[1],
        small=half_sum(live.small, sb, swap_sb),
    )
    live.drop("qkv_t", "qkv_got1")
    terms = (live.keep[0], live.got[0], live.keep[1], live.got[1])
    _, input_low, _ = norm_step_back(terms, live.own_x, live.d_x2, live.vectors, 0)
    y = live.x2_own + jnp.sum(live.y_terms.astype(F32), axis=0)
    small = live.small
    bit = n_sx // 2
    while bit >= 1:
        small = half_sum(small, (sx // bit) % 2, functools.partial(swap_sx, bit=bit))
        bit //= 2
    live.done(
        input_low=input_low,
        small=half_sum(small, c, swap_c),
        qkv_over=live.qkv_over + [swap_fh(live.qkv_give)],
        out_got=[swap_sb(v_) for v_ in live.out_t[2:]],
        qkv_sum=plus(live.qkv_m[1], live.qkv_got0),
        layer_out=give_back(y.astype(BF16)),
        gu_done=exchange(live.gu_sum.reshape(members, rows, -1)),
    )
    live.drop("y_terms", "gu_sum")
    qkv_sum = live.qkv_sum + jnp.concatenate(live.qkv_over, 0).astype(F32)
    if natural:
        out_over = swap_fh(plus(live.out_t[1], live.out_got[1], BF16))
    else:
        d_att = jnp.zeros((N, D), BF16)
        for v_, r in zip(live.att_all, firsts):
            d_att = lax.dynamic_update_slice_in_dim(d_att, v_, r, 0)
        t = lax.dot_general(live.o, d_att, TN, preferred_element_type=F32)
        t = jnp.where(jnp.arange(members)[:, None, None] == sr * 2 + fl, t[None], 0.0)
        out_over = lax.psum_scatter(t.reshape(H * HD, D), EVERY, scatter_dimension=0, tiled=True)
    live.done(
        qkv_done=exchange(qkv_sum.astype(BF16).reshape(members, rows, -1)),
        out_over=out_over,
        small=half_sum(live.small, fh, swap_fh),
        down_over=[swap_fh(live.down_give)] + live.down_over,
        input_grad=give_back(live.input_low),
        gate_grad=uncolumns([live.gu_done], gate_back),
        up_grad=uncolumns([live.gu_done], up_back),
    )
    small = half_sum(live.small, fl, swap_fl)
    qkv_grad = uncolumns([live.qkv_done], qkv_back)
    out_grad = live.out_over
    if natural:
        out_grad = plus(live.out_t[0], live.out_got[0]) + out_grad.astype(F32)
    input_grad, layer_out = live.input_grad, live.layer_out
    down_grad = plus(live.down_t[0], live.down_got0) + jnp.concatenate(live.down_over, 0).astype(F32)
    gate_grad, up_grad = live.gate_grad, live.up_grad
    gain1_grad, bias1_grad, gain2_grad, bias2_grad = (small[n] for n in range(4))
    bias_grad = small[4:].reshape(-1)
    return (
        layer_out,
        input_grad,
        gain1_grad,
        bias1_grad,
        qkv_grad,
        bias_grad,
        out_grad,
        gain2_grad,
        bias2_grad,
        gate_grad,
        up_grad,
        down_grad,
    )


def solution(mesh):
    names = dict(mesh.shape)
    n_seq, n_fsdp = names["seq"], names["fsdp"]
    fine = Mesh(mesh.devices.reshape(2, n_seq // 4, 2, 2, n_fsdp // 2), EVERY)
    tokens = P(None, ("fh", "fl"), ("sb", "sx", "c"), None)
    vector = P(EVERY)
    matrix = P(EVERY, None)
    in_specs = (tokens, tokens, P(None, ("fh", "fl"), None), vector, vector, matrix, vector, matrix)
    in_specs += (vector, vector, matrix, matrix, matrix)
    out_specs = (tokens, tokens, vector, vector, matrix, vector, matrix, vector, vector)
    out_specs += (matrix, matrix, matrix)
    return jax.shard_map(shards, mesh=fine, in_specs=in_specs, out_specs=out_specs, check_vma=False)
```

```python
import functools

import jax
import jax.numpy as jnp
import numpy as np
from jax import lax
from jax.experimental import pallas as pl
from jax.experimental.pallas import tpu as pltpu
from jax.sharding import Mesh
from jax.sharding import PartitionSpec as P

H = 32
HD = 64
ROT = 16

eps_norm = 1e-05
rope_base = 10000.0
masked_score = -1e30

F32 = jnp.float32
BF16 = jnp.bfloat16

SWAP = [(0, 1), (1, 0)]
EVERY = ("sb", "sx", "c", "fh", "fl")
MEMBERS = ("sx", "c", "fl")
QUAD = ("fl", "sx")
ANY = pl.BlockSpec(memory_space=pl.ANY)
SMEM = pl.BlockSpec(memory_space=pltpu.SMEM)
VMEM = pl.BlockSpec(memory_space=pltpu.VMEM)
NT = (((1,), (1,)), ((), ()))
TN = (((0,), (0,)), ((), ()))
LIMIT = 60 * 1024 * 1024


def params():
    return pltpu.CompilerParams(vmem_limit_bytes=LIMIT)


def cost(microseconds):
    return pl.CostEstimate(flops=int(microseconds * 1e8), bytes_accessed=1024, transcendentals=0)


def dot(a, b, dims=(((1,), (0,)), ((), ()))):
    return lax.dot_general(a, b, dims, preferred_element_type=F32)


def swap_sb(v):
    return lax.ppermute(v, "sb", SWAP)


def swap_fh(v):
    return lax.ppermute(v, "fh", SWAP)


def swap_fl(v):
    return lax.ppermute(v, "fl", SWAP)


def swap_c(v):
    return lax.ppermute(v, "c", SWAP)


def swap_sx(v, bit=1):
    n = lax.axis_size("sx")
    return lax.ppermute(v, "sx", [(i, i ^ bit) for i in range(n)])


def over_quad(v):
    return lax.all_to_all(v, QUAD, split_axis=0, concat_axis=0, tiled=True)


class Live(dict):
    def __getattr__(self, name):
        return self[name]

    def done(self, **new):
        self.update(new)
        self.update(lax.optimization_barrier(dict(self)))

    def drop(self, *names):
        for name in names:
            del self[name]


def normalize(values):
    average = jnp.mean(values, axis=-1, keepdims=True)
    centered = values - average
    inv_std = lax.rsqrt(jnp.mean(centered * centered, axis=-1, keepdims=True) + eps_norm)
    return centered * inv_std, inv_std


def normalize_back(grad_normed, normed, inv_std):
    first_mean = jnp.mean(grad_normed, axis=-1, keepdims=True)
    second_mean = jnp.mean(grad_normed * normed, axis=-1, keepdims=True)
    return inv_std * (grad_normed - first_mean - normed * second_mean)


def gather_first(x):
    return (x, swap_sx(x), swap_fl(x), swap_c(x))


def gather_second(first):
    n_sx = lax.axis_size("sx")
    x, a, b, xo = first
    h = x.shape[0] // 2
    d1 = swap_fl(a[:h])
    d2 = swap_sx(b[h:])
    ao = swap_c(a)
    bo = swap_c(b)
    got = [x, a, b, d1, d2, xo, ao, bo, swap_c(d1), swap_c(d2)]
    bit = 2
    while bit < n_sx:
        got = got + [swap_sx(v, bit) for v in got]
        bit *= 2
    return got


def gather_rows(n_sx, m):
    h = m // 2
    got = []
    for c in range(2):
        at = c * n_sx * m
        over = 2 * n_sx * m + at
        got += [at, at + m, over, over + m, over + m + h]
    bit = 2
    while bit < n_sx:
        got = got + [r + bit * m for r in got]
        bit *= 2
    return got


def add_first_kernel(keep, got, send_x, send_l, keep_x, keep_l):
    h = keep.shape[2] // 2
    for f in range(2):
        for x in range(2):
            q = keep[f, x].astype(F32) + got[f, x].astype(F32)
            if x == 1:
                send_x[f] = q[:h].astype(BF16)
            else:
                keep_x[f] = q[:h]
            if f == 1:
                send_l[x] = q[h:].astype(BF16)
            else:
                keep_l[x] = q[h:]


def add_second_kernel(keep_x, got_x, keep_l, got_l, send_x, send_l, own_x, own_l):
    own_x[...] = keep_x[0] + got_x[0].astype(F32)
    own_l[...] = keep_l[0] + got_l[0].astype(F32)
    send_x[...] = (keep_x[1] + got_x[1].astype(F32)).astype(BF16)
    send_l[...] = (keep_l[1] + got_l[1].astype(F32)).astype(BF16)


def add_first(keep, got):
    bit = keep.shape[1] // 2
    while bit >= 2:
        q = keep.astype(F32) + got.astype(F32)
        keep = q[:, :bit].astype(BF16)
        got = swap_sx(q[:, bit:].astype(BF16), bit)
        bit //= 2
    m, D = keep.shape[2:]
    h = m // 2
    low = jax.ShapeDtypeStruct((2, h, D), BF16)
    high = jax.ShapeDtypeStruct((2, h, D), F32)
    return pl.pallas_call(
        add_first_kernel,
        out_shape=[low, low, high, high],
        in_specs=[VMEM] * 2,
        out_specs=[VMEM] * 4,
        compiler_params=params(),
        cost_estimate=cost(4),
    )(keep, got)


def add_second(keep_x, got_x, keep_l, got_l):
    _, h, D = keep_x.shape
    return pl.pallas_call(
        add_second_kernel,
        out_shape=[jax.ShapeDtypeStruct((h, D), BF16)] * 2 + [jax.ShapeDtypeStruct((h, D), F32)] * 2,
        in_specs=[VMEM] * 4,
        out_specs=[VMEM] * 4,
        compiler_params=params(),
        cost_estimate=cost(3),
    )(keep_x, got_x, keep_l, got_l)


def in_order(pieces, sb, fh):
    w, z, y, yz = pieces
    a, b = jnp.where(fh == 1, z, w), jnp.where(fh == 1, w, z)
    c, d = jnp.where(fh == 1, yz, y), jnp.where(fh == 1, y, yz)
    first = jnp.stack([jnp.where(sb == 1, c, a), jnp.where(sb == 1, d, b)])
    second = jnp.stack([jnp.where(sb == 1, a, c), jnp.where(sb == 1, b, d)])
    return jnp.stack([first, second])


def flip_if(bit, v, axis):
    return jnp.where(bit == 1, lax.rev(v, (axis,)), v)


def xor_order(v, axis, index, n):
    shape = v.shape
    bit = 1
    while bit < n:
        r = v.reshape(shape[:axis] + (n // (2 * bit), 2, bit) + shape[axis + 1 :])
        v = flip_if((index // bit) % 2, r, axis + 1).reshape(shape)
        bit *= 2
    return v


def load_groups(sc, pieces, places, buf, sems, first=0, start=True):
    copies = []
    rows = buf.shape[4]
    for n, (piece, (k, r)) in enumerate(zip(pieces, places)):
        where = buf.at[sc[0] ^ (k // 2), pl.ds(r, piece.shape[0]), sc[1] ^ (k % 2)]
        copies.append(pltpu.make_async_copy(piece.at[:, :, pl.ds(first, rows)], where, sems.at[n]))
    for c in copies if start else ():
        c.start()
    return copies


def load_down(sc, pieces, places, buf, sems, start=True):
    copies = []
    for n, (piece, (k, r)) in enumerate(zip(pieces, places)):
        where = buf
        if len(places) > 1:
            where = buf.at[sc[0] ^ (k // 2), sc[1] ^ (k % 2), pl.ds(r, piece.shape[0])]
        copies.append(pltpu.make_async_copy(piece, where, sems.at[n]))
    for c in copies if start else ():
        c.start()
    return copies


class Rows:
    def __init__(self, arrays, firsts):
        self.arrays, self.firsts = list(arrays), firsts
        self.N, self.D = sum(v.shape[0] for v in arrays), arrays[0].shape[1]

    def scratch(self):
        return [pltpu.VMEM((self.N, self.D), BF16), pltpu.SemaphoreType.DMA((len(self.arrays),))]

    def load(self, sc, refs, buf, sems, start=True):
        copies = [
            pltpu.make_async_copy(ref, buf.at[pl.ds(r, ref.shape[0])], sems.at[n])
            for n, (ref, r) in enumerate(zip(refs, self.firsts))
        ]
        for c in copies if start else ():
            c.start()
        return copies


class Quads:
    def __init__(self, mine, other, m):
        self.arrays, self.m = [mine, other], m
        self.N, self.D = 2 * mine.shape[0], mine.shape[1]
        self.n_sx = mine.shape[0] // (2 * m)

    def scratch(self):
        return [pltpu.VMEM((self.N, self.D), BF16), pltpu.SemaphoreType.DMA((4 * self.n_sx,))]

    def load(self, sc, refs, buf, sems, start=True):
        copies = []
        for k in range(2):
            for f in range(2):
                for x in range(self.n_sx):
                    to = ((2 * (f ^ sc[2]) + k) * self.n_sx + (x ^ sc[3])) * self.m
                    copies.append(
                        pltpu.make_async_copy(
                            refs[k].at[pl.ds((f * self.n_sx + x) * self.m, self.m)],
                            buf.at[pl.ds(pl.multiple_of(to, self.m), self.m)],
                            sems.at[len(copies)],
                        )
                    )
        for c in copies if start else ():
            c.start()
        return copies


def sides(nb, by_index=False):
    def place(f, b, sc):
        if by_index:
            f, b = f ^ sc[2], b ^ (sc[3] // 2)
        return f * nb + b

    def keep(i, sc=None):
        f, k, b = i // (2 * nb), lax.rem(i // nb, 2), lax.rem(i, nb)
        return place(f, jnp.where(k == 0, b, nb - 1), sc)

    def send(i, sc=None):
        f, k, b = i // (2 * nb), lax.rem(i // nb, 2), lax.rem(i, nb)
        return place(f, jnp.where(k == 0, 0, b), sc)

    return keep, send


def columns_kernel(plan, n_in, *refs):
    ins, vectors, out = refs[:n_in], refs[n_in:-1], refs[-1]
    rows = ins[0].shape[0]
    if vectors:
        row = jnp.concatenate([v[...] for v in vectors], axis=-1)
    for t, ranges in enumerate(plan):
        out[t, :rows] = jnp.concatenate([ins[i][:, a : a + n] for i, a, n in ranges], axis=-1)
        if vectors:
            out[t, rows : rows + 1, : row.shape[1]] = row


def columns(arrays, plan, vectors=()):
    width = sum(n for _, _, n in plan[0])
    rows = arrays[0].shape[0] + (8 if vectors else 0)
    return pl.pallas_call(
        functools.partial(columns_kernel, plan, len(arrays)),
        out_shape=jax.ShapeDtypeStruct((len(plan), rows, width), arrays[0].dtype),
        in_specs=[VMEM] * (len(arrays) + len(vectors)),
        out_specs=VMEM,
        compiler_params=params(),
        cost_estimate=cost(3),
    )(*arrays, *vectors)


def uncolumns_kernel(plan, *refs):
    ins, out = refs[:-1], refs[-1]
    width = ins[0].shape[2]
    if True:
        at, group, size = 0, [], 0
        for t, b, n in plan:
            group.append(ins[b // width][t, :, b % width : b % width + n].astype(F32))
            size += n
            if size % 128 == 0:
                out[:, at : at + size] = jnp.concatenate(group, axis=-1)
                at, group, size = at + size, [], 0
        if group:
            out[:, at : at + size] = jnp.concatenate(group, axis=-1)


def uncolumns(arrays, plan):
    rows = arrays[0].shape[1]
    return pl.pallas_call(
        functools.partial(uncolumns_kernel, plan),
        out_shape=jax.ShapeDtypeStruct((rows, sum(n for _, _, n in plan)), F32),
        in_specs=[VMEM] * len(arrays),
        out_specs=VMEM,
        compiler_params=params(),
        cost_estimate=cost(3),
    )(*arrays)


def turn(v, c_ref_value, sa, sb_, direction):
    width = v.shape[1]
    back = pltpu.roll(v, ROT // 2, 1)
    front = pltpu.roll(v, width - ROT // 2, 1)
    return v * c_ref_value + direction * (back * sa + front * sb_)


def attention_kernel(dims, places, x_rows, sc, tables, id_row, id_col, w_out, *refs):
    heads, length, block, D = dims
    x_refs, refs = refs[: len(x_rows.arrays)], refs[len(x_rows.arrays) :]
    w_refs, refs = refs[: len(places)], refs[len(places) :]
    h1, q, k, v, o, lse, keep, send, vectors, w, sems, small, small_sems, bias_q, x_buf, x_sems = refs
    wide = heads * HD
    per = length // block
    i = pl.program_id(0)

    @pl.when(i == 0)
    def _():
        n_sr, rows_ = w.shape[1], w.shape[4]
        copies = x_rows.load(sc, x_refs, x_buf, x_sems)
        copies += load_groups(sc, w_refs, places, small, small_sems, rows_)
        for c in load_groups(sc, w_refs, places, w, sems) + copies:
            c.wait()
        every = [(s, j, f, l) for s in range(2) for j in range(n_sr) for f in range(2) for l in range(2)]
        for n in range(4):
            row = [small[s, j, f, l, 0:1, n * rows_ : (n + 1) * rows_] for s, j, f, l in every]
            vectors[n : n + 1, :] = jnp.concatenate(row, axis=-1).astype(F32)
        first = 4 * rows_
        if 3 * rows_ == 3 * HD:
            row = [
                small[a // 2, sc[4], a % 2, sc[2], 0:1, first + p * HD : first + (p + 1) * HD]
                for p in range(3)
                for a in range(heads)
            ]
        else:
            count = 3 * HD // (3 * rows_)
            row = []
            for a in range(heads):
                for n in range(count):
                    d = ((sc[4] * 2 + sc[2]) * heads + a) * count + n
                    at = (d // (4 * n_sr), lax.rem(d // 4, n_sr), lax.rem(d // 2, 2), lax.rem(d, 2))
                    row.append(small[at[0], at[1], at[2], at[3], 0:1, first : first + 3 * rows_])
        bias_q[...] = jnp.concatenate(row, axis=-1).astype(F32)

    rows = pl.ds(pl.multiple_of(i * block, block), block)
    normed, _ = normalize(x_buf[rows, :].astype(F32))
    h = (normed * vectors[0:1, :] + vectors[1:2, :]).astype(BF16)
    h1[...] = h
    lin = dot(h, w[...].reshape(D, 3 * wide)) + bias_q[...]
    qk = turn(lin[:, : 2 * wide], tables[0], tables[1], tables[2], 1.0)
    q[rows, :] = qk[:, :wide].astype(BF16)
    k[rows, :] = qk[:, wide:].astype(BF16)
    v[rows, :] = lin[:, 2 * wide :].astype(BF16)

    @pl.when(lax.rem(i, per) == per - 1)
    def _():
        s = i // per
        start = pl.multiple_of(s * length, length)
        step = min(length, (1 << 18) // length)
        for r in range(length // step):
            part = pl.ds(pl.multiple_of(start + r * step, step), step)
            allowed = id_col[part, 0:1] >= id_row[pl.ds(s, 1), :]
            for hd in range(heads):
                lanes = slice(hd * HD, (hd + 1) * HD)
                kh = k[pl.ds(start, length), lanes]
                vh = v[pl.ds(start, length), lanes]
                score = dot(q[part, lanes], kh, NT) * (HD**-0.5)
                score = jnp.where(allowed, score, masked_score)
                peak = jnp.max(score, axis=-1, keepdims=True)
                e = jnp.exp(score - peak)
                total = jnp.sum(e, axis=-1, keepdims=True)
                p = (e * (1.0 / total)).astype(BF16)
                o[part, lanes] = dot(p, vh).astype(BF16)
                lse[part, hd : hd + 1] = peak + jnp.log(total)
        for side, out in enumerate((keep, send)):
            for b in range(per // 2):
                part = pl.ds(pl.multiple_of(start + (side * (per // 2) + b) * block, block), block)
                out[0, b * block : (b + 1) * block] = dot(o[part, :], w_out[...]).astype(BF16)


def attention(sc, x_rows, tables, id_row, id_col, w_out, weight, heads, rows):
    N, D = x_rows.N, x_rows.D
    length = N // 2
    block = 256
    per = length // block
    wide = heads * HD
    n_sr, _, _, f = weight[0][0].shape
    places = [p[1:] for p in weight]
    whole = lambda shape: pl.BlockSpec(shape, lambda i, sc: (0,) * len(shape))
    side = pl.BlockSpec((1, length // 2, D), lambda i, sc: (i // per, 0, 0))
    spec = pltpu.PrefetchScalarGridSpec(
        num_scalar_prefetch=1,
        grid=(N // block,),
        in_specs=[
            pl.BlockSpec((3, block, 2 * wide), lambda i, sc: (0, lax.rem(i, per), 0)),
            whole((2, length)),
            whole((N, 1)),
            whole((wide, D)),
        ]
        + [ANY] * (len(x_rows.arrays) + len(places)),
        out_specs=[pl.BlockSpec((block, D), lambda i, sc: (i, 0))]
        + [whole((N, wide))] * 4
        + [whole((N, heads)), side, side, whole((4, D))],
        scratch_shapes=[
            pltpu.VMEM((2, n_sr, 2, 2, rows, f), BF16),
            pltpu.SemaphoreType.DMA((len(places),)),
            pltpu.VMEM((2, n_sr, 2, 2, 8, f), BF16),
            pltpu.SemaphoreType.DMA((len(places),)),
            pltpu.VMEM((1, 3 * wide), F32),
        ]
        + x_rows.scratch(),
    )
    return pl.pallas_call(
        functools.partial(attention_kernel, (heads, length, block, D), places, x_rows),
        grid_spec=spec,
        out_shape=[jax.ShapeDtypeStruct((N, D), BF16)]
        + [jax.ShapeDtypeStruct((N, wide), BF16)] * 4
        + [jax.ShapeDtypeStruct((N, heads), F32)]
        + [jax.ShapeDtypeStruct((2, length // 2, D), BF16)] * 2
        + [jax.ShapeDtypeStruct((4, D), F32)],
        compiler_params=params(),
        cost_estimate=cost(25),
    )(sc, tables, id_row, id_col, w_out, *x_rows.arrays, *[p[0] for p in weight])


def ffn_kernel(dims, h_rows, dy_rows, sc, *refs):
    g_list, d_list, block, nb, D, ff = dims
    h_refs, refs = refs[: len(h_rows.arrays)], refs[len(h_rows.arrays) :]
    dy_refs, refs = refs[: len(dy_rows.arrays)], refs[len(dy_rows.arrays) :]
    g_refs, refs = refs[: len(g_list)], refs[len(g_list) :]
    d_refs, refs = refs[: len(d_list)], refs[len(d_list) :]
    h2, act, d_gu, keep, send, g_buf, d_buf, sem_g, sem_d, h_buf, h_sems, dy_buf, dy_sems = refs
    i = pl.program_id(0)
    rows = pl.ds(pl.multiple_of(i * block, block), block)

    @pl.when(i == 0)
    def _():
        first = h_rows.load(sc, h_refs, h_buf, h_sems) + load_groups(sc, g_refs, g_list, g_buf, sem_g)
        dy_rows.load(sc, dy_refs, dy_buf, dy_sems)
        load_down(sc, d_refs, d_list, d_buf, sem_d)
        for c in first:
            c.wait()

    h = h_buf[rows, :]
    h2[...] = h
    w_gu = g_buf[...].reshape(D, 2 * ff)
    gu = dot(h, w_gu)
    g, u = gu[:, :ff], gu[:, ff:]
    s = jax.nn.sigmoid(g)
    silu = g * s
    act[...] = (silu * u).astype(BF16)

    @pl.when(i == 0)
    def _():
        second = dy_rows.load(sc, dy_refs, dy_buf, dy_sems, False)
        for c in second + load_down(sc, d_refs, d_list, d_buf, sem_d, False):
            c.wait()

    d_act = dot(dy_buf[rows, :], d_buf[...].reshape(ff, D), NT)
    d_g = (d_act * u * s * (1.0 + g * (1.0 - s))).astype(BF16)
    d_u = (d_act * silu).astype(BF16)
    d = jnp.concatenate([d_g, d_u], axis=-1)
    d_gu[...] = d
    d_h = dot(d, w_gu, NT).astype(BF16)
    side = lax.rem(i // nb, 2)

    @pl.when(side == 0)
    def _():
        keep[...] = d_h

    @pl.when(side == 1)
    def _():
        send[...] = d_h


def ffn(sc, h_rows, dy_rows, gu, down, down_places, rows_):
    N, D = h_rows.N, h_rows.D
    block = 256
    nb = N // 4 // block
    n_sr, _, _, two_ff = gu[0][0].shape
    ff = two_ff // 2
    rows = lambda width: pl.BlockSpec((block, width), lambda i, sc: (i, 0))
    d_shape = (2, 2, ff // 4, D) if len(down) > 1 else (ff, D)
    keep, send = sides(nb)
    spec = pltpu.PrefetchScalarGridSpec(
        num_scalar_prefetch=1,
        grid=(N // block,),
        in_specs=[ANY] * (len(h_rows.arrays) + len(dy_rows.arrays) + len(gu) + len(down)),
        out_specs=[
            rows(D),
            rows(ff),
            rows(2 * ff),
            pl.BlockSpec((block, D), lambda i, sc: (keep(i), 0)),
            pl.BlockSpec((block, D), lambda i, sc: (send(i), 0)),
        ],
        scratch_shapes=[
            pltpu.VMEM((2, n_sr, 2, 2, rows_, two_ff), BF16),
            pltpu.VMEM(d_shape, BF16),
            pltpu.SemaphoreType.DMA((len(gu),)),
            pltpu.SemaphoreType.DMA((len(down),)),
        ]
        + h_rows.scratch()
        + dy_rows.scratch(),
    )
    dims = ([p[1:] for p in gu], down_places, block, nb, D, ff)
    return pl.pallas_call(
        functools.partial(ffn_kernel, dims, h_rows, dy_rows),
        grid_spec=spec,
        out_shape=[
            jax.ShapeDtypeStruct((N, D), BF16),
            jax.ShapeDtypeStruct((N, ff), BF16),
            jax.ShapeDtypeStruct((N, 2 * ff), BF16),
            jax.ShapeDtypeStruct((N // 2, D), BF16),
            jax.ShapeDtypeStruct((N // 2, D), BF16),
        ],
        compiler_params=params(),
        cost_estimate=cost(30),
    )(sc, *h_rows.arrays, *dy_rows.arrays, *[p[0] for p in gu], *down)


def down_kernel(d_list, nb, ff, D, sc, act, *refs):
    n_d = len(d_list)
    d_refs, (keep, send, d_buf, sem) = refs[:n_d], refs[n_d:]
    i = pl.program_id(0)

    @pl.when(i == 0)
    def _():
        for c in load_down(sc, d_refs, d_list, d_buf, sem):
            c.wait()

    y = dot(act[...], d_buf[...].reshape(ff, D)).astype(BF16)
    side = lax.rem(i // nb, 2)
    m = y.shape[0] // 2
    for k, out in enumerate((keep, send)):
        for t in range(2):

            @pl.when((side == k) & (lax.rem(sc[3], 2) == t))
            def _():
                out[t * m : (t + 1) * m, :] = y[:m]
                out[(1 - t) * m : (2 - t) * m, :] = y[m:]


def down_product(sc, act, down, places):
    N, ff = act.shape
    D = down[0].shape[-1]
    block = 256
    nb = N // 4 // block
    d_shape = (2, 2, ff // 4, D) if len(down) > 1 else (ff, D)
    keep, send = sides(nb, by_index=True)
    spec = pltpu.PrefetchScalarGridSpec(
        num_scalar_prefetch=1,
        grid=(N // block,),
        in_specs=[pl.BlockSpec((block, ff), lambda i, sc: (i, 0))] + [ANY] * len(down),
        out_specs=[
            pl.BlockSpec((block, D), lambda i, sc: (keep(i, sc), 0)),
            pl.BlockSpec((block, D), lambda i, sc: (send(i, sc), 0)),
        ],
        scratch_shapes=[pltpu.VMEM(d_shape, BF16), pltpu.SemaphoreType.DMA((len(down),))],
    )
    return pl.pallas_call(
        functools.partial(down_kernel, places, nb, ff, D),
        grid_spec=spec,
        out_shape=[jax.ShapeDtypeStruct((N // 2, D), BF16)] * 2,
        compiler_params=params(),
        cost_estimate=cost(9),
    )(sc, act, *down)


def h_buf_rows(length):
    return 256 if length <= 1024 else 128


def attention_back_kernel(dims, d_rows, sc, tables, id_row, id_col, q, k, v, lse, w_out, h1, vectors, *refs):
    heads, length, N, D, w_list = dims
    block = h_buf_rows(length)
    d_refs, refs = refs[: len(d_rows.arrays)], refs[len(d_rows.arrays) :]
    w_refs, refs = refs[: len(w_list)], refs[len(w_list) :]
    d_lin, bias_grad, sums, keep, send, w, d_o, d_qk, sem_w, h_buf, sem_h, d_att, sem_d = refs
    wide = heads * HD
    copies = d_rows.load(sc, d_refs, d_att, sem_d)
    loads = load_groups(sc, w_refs, w_list, w, sem_w)
    h_loads = [
        pltpu.make_async_copy(h1.at[pl.ds(n * block, block)], h_buf.at[n % 2], sem_h.at[n % 2])
        for n in range(N // block)
    ]
    h_loads[0].start()
    for c in copies:
        c.wait()
    sums[...] = jnp.zeros_like(sums)
    step = min(length, (1 << 18) // length)
    scale = HD**-0.5
    bias_grad[...] = jnp.zeros_like(bias_grad)
    for s in range(2):
        start = s * length
        for r in range(length // step):
            at = pl.ds(start + r * step, step)
            d_o[pl.ds(r * step, step), :] = dot(d_att[at, :], w_out[...], NT).astype(BF16)
        d_qk[:, wide:] = jnp.zeros_like(d_qk[:, wide:])
        for hd in range(heads):
            lanes = slice(hd * HD, (hd + 1) * HD)
            k_lanes = slice(wide + hd * HD, wide + (hd + 1) * HD)
            v_lanes = slice(2 * wide + hd * HD, 2 * wide + (hd + 1) * HD)
            kh = k[pl.ds(start, length), lanes]
            vh = v[pl.ds(start, length), lanes]
            for r in range(length // step):
                part = pl.ds(start + r * step, step)
                local = pl.ds(r * step, step)
                allowed = id_col[part, 0:1] >= id_row[s : s + 1, :]
                qh = q[part, lanes]
                score = dot(qh, kh, NT) * scale
                p = jnp.where(allowed, jnp.exp(score - lse[part, hd : hd + 1]), 0.0)
                doh = d_o[local, lanes]
                dp = dot(doh, vh, NT)
                inner = jnp.sum(p * dp, axis=-1, keepdims=True)
                ds = (p * (dp - inner)).astype(BF16)
                d_qk[local, lanes] = dot(ds, kh) * scale
                dk = dot(ds, qh, TN) * scale
                dv = dot(p.astype(BF16), doh, TN)
                if length == step:
                    d_qk[:, k_lanes] = dk
                    d_qk[:, v_lanes] = dv
                else:
                    d_qk[:, k_lanes] += dk
                    d_qk[:, v_lanes] += dv
        if s == 0:
            for c in loads:
                c.wait()
        half = length // 2
        for b in range(length // block):
            local = pl.ds(b * block, block)
            at = pl.ds(start + b * block, block)
            qk = turn(d_qk[local, : 2 * wide], tables[0, local], tables[1, local], tables[2, local], -1.0)
            lin = jnp.concatenate([qk, d_qk[local, 2 * wide :]], axis=-1).astype(BF16)
            d_lin[at, :] = lin
            bias_grad[...] += jnp.sum(lin.astype(F32), axis=0, keepdims=True)
            d_h = dot(lin, w[...].reshape(D, 3 * wide), NT)
            n = (start + b * block) // block
            h_loads[n].wait()
            if n + 1 < N // block:
                h_loads[n + 1].start()
            sums[0:1, :] += jnp.sum(d_h * h_buf[n % 2].astype(F32), axis=0, keepdims=True)
            sums[1:2, :] += jnp.sum(d_h, axis=0, keepdims=True)
            d_h = d_h.astype(BF16)
            out = keep if b * block < half else send
            out[pl.ds(s * half + (b * block) % half, block), :] = d_h
    sums[0:1, :] = (sums[0:1, :] - vectors[1:2, :] * sums[1:2, :]) / vectors[0:1, :]


def attention_back(sc, tables, id_row, id_col, q, k, v, lse, w_out, h1, vectors, d_rows, weight):
    N, wide = q.shape
    D = w_out.shape[1]
    heads = wide // HD
    length = N // 2
    n_sr, _, _, f = weight[0][0].shape
    rows = D // (8 * n_sr)
    dims = (heads, length, N, D, [p[1:] for p in weight])
    return pl.pallas_call(
        functools.partial(attention_back_kernel, dims, d_rows),
        out_shape=[
            jax.ShapeDtypeStruct((N, 3 * wide), BF16),
            jax.ShapeDtypeStruct((1, 3 * wide), F32),
            jax.ShapeDtypeStruct((2, D), F32),
            jax.ShapeDtypeStruct((N // 2, D), BF16),
            jax.ShapeDtypeStruct((N // 2, D), BF16),
        ],
        in_specs=[SMEM] + [VMEM] * 8 + [ANY, VMEM] + [ANY] * (len(d_rows.arrays) + len(weight)),
        out_specs=[VMEM] * 5,
        scratch_shapes=[
            pltpu.VMEM((2, n_sr, 2, 2, rows, f), BF16),
            pltpu.VMEM((length, wide), BF16),
            pltpu.VMEM((length, 3 * wide), F32),
            pltpu.SemaphoreType.DMA((len(weight),)),
            pltpu.VMEM((2, h_buf_rows(length), D), BF16),
            pltpu.SemaphoreType.DMA((2,)),
        ]
        + d_rows.scratch(),
        compiler_params=params(),
        cost_estimate=cost(23),
    )(sc, tables, id_row, id_col, q, k, v, lse, w_out, h1, vectors, *d_rows.arrays, *[p[0] for p in weight])


def rows_kernel(dims, sc, h, d, *outs):
    n, two_rows = dims
    t = dot(h[...], d[...], TN).astype(BF16)
    i = pl.program_id(0)
    others, same = outs[:-1], outs[-1]
    for f in range(2):
        places = [(same, sc[1] == f)]
        for k, other in enumerate(others):
            places.append((other, (sc[1] != f) if len(others) == 1 else (sc[1] != f) & (i == k)))
        for out, here in places:

            @pl.when(here)
            def _():
                for j in range(n):
                    r = (2 * j + f) * two_rows
                    out[j * two_rows : (j + 1) * two_rows, :] = t[r : r + two_rows]


def grad_rows(sc, h, d, side, n_sr, rows, parts=2):
    N, D = h.shape
    f = d.shape[1]
    cut = D // 4
    n = n_sr // 2
    half, whole = pl.BlockSpec((cut // 2, f), lambda i, sc: (0, 0)), pl.BlockSpec((cut // 2, f), lambda i, sc: (i, 0))
    shape = lambda r: jax.ShapeDtypeStruct((r, f), BF16)
    spec = pltpu.PrefetchScalarGridSpec(
        num_scalar_prefetch=1,
        grid=(2,),
        in_specs=[
            pl.BlockSpec((N, cut), lambda i, sc: (0, (sc[0] ^ side) * 2 + i)),
            pl.BlockSpec((N, f), lambda i, sc: (0, 0)),
        ],
        out_specs=([half] * 2 if parts == 2 else [whole]) + [whole],
    )
    return pl.pallas_call(
        functools.partial(rows_kernel, (n, 2 * rows)),
        grid_spec=spec,
        out_shape=([shape(cut // 2)] * 2 if parts == 2 else [shape(cut)]) + [shape(cut)],
        compiler_params=params(),
        cost_estimate=cost(7),
    )(sc, h, d)


def slices_kernel(rows, cut, d_rows, sc, a, *refs):
    d_refs, refs = refs[: len(d_rows.arrays)], refs[len(d_rows.arrays) :]
    outs, (buf, sems) = refs[:4], refs[4:]
    i = pl.program_id(0)

    @pl.when(i == 0)
    def _():
        for c in d_rows.load(sc, d_refs, buf, sems):
            c.wait()

    d = buf[:, pl.ds(pl.multiple_of(i * cut, cut), cut)]
    t = dot(a[...], d, TN).astype(BF16)
    for n in range(4):
        for k in range(4):

            @pl.when((sc[0] == (n // 2) ^ (k // 2)) & (sc[1] == (n % 2) ^ (k % 2)))
            def _():
                outs[k][...] = t[n * rows : (n + 1) * rows]


def grad_slices(sc, a, d_rows):
    N, f = a.shape
    D = d_rows.D
    cut = D // 4
    spec = pltpu.PrefetchScalarGridSpec(
        num_scalar_prefetch=1,
        grid=(D // cut,),
        in_specs=[pl.BlockSpec((N, f), lambda i, sc: (0, 0))] + [ANY] * len(d_rows.arrays),
        out_specs=[pl.BlockSpec((f // 4, cut), lambda i, sc: (0, i))] * 4,
        scratch_shapes=d_rows.scratch(),
    )
    return pl.pallas_call(
        functools.partial(slices_kernel, f // 4, cut, d_rows),
        grid_spec=spec,
        out_shape=[jax.ShapeDtypeStruct((f // 4, D), BF16)] * 4,
        compiler_params=params(),
        cost_estimate=cost(9),
    )(sc, a, *d_rows.arrays)


def total_of(u0, u1, w0, w1):
    return jnp.concatenate([u0[...] + u1[...].astype(F32), w0[...] + w1[...].astype(F32)], axis=0)


def forward_kernel(u0, u1, w0, w1, x, vectors, x2, low):
    v = x[...].astype(F32) + total_of(u0, u1, w0, w1)
    x2[...] = v
    normed, _ = normalize(v)
    low[...] = (normed * vectors[2:3, :] + vectors[3:4, :]).astype(BF16)


def norm_step(terms, x, vectors):
    m, D = x.shape
    return pl.pallas_call(
        forward_kernel,
        out_shape=[jax.ShapeDtypeStruct((m, D), F32), jax.ShapeDtypeStruct((m, D), BF16)],
        in_specs=[VMEM] * 6,
        out_specs=[VMEM] * 2,
        compiler_params=params(),
        cost_estimate=cost(4),
    )(*terms, x, vectors)


def back_kernel(which, u0, u1, w0, w1, x, dy, vectors, grad, low, sums):
    d_h = total_of(u0, u1, w0, w1)
    normed, inv_std = normalize(x[...].astype(F32))
    total = dy[...].astype(F32) + normalize_back(d_h * vectors[which : which + 1, :], normed, inv_std)
    grad[...] = total
    low[...] = total.astype(BF16)
    sums[0:1, :] = jnp.sum(d_h * normed, axis=0, keepdims=True)
    sums[1:2, :] = jnp.sum(d_h, axis=0, keepdims=True)


def norm_step_back(terms, x, dy, vectors, which):
    m, D = x.shape
    return pl.pallas_call(
        functools.partial(back_kernel, which),
        out_shape=[
            jax.ShapeDtypeStruct((m, D), F32),
            jax.ShapeDtypeStruct((m, D), BF16),
            jax.ShapeDtypeStruct((2, D), F32),
        ],
        in_specs=[VMEM] * 7,
        out_specs=[VMEM] * 3,
        compiler_params=params(),
        cost_estimate=cost(4),
    )(*terms, x, dy, vectors)


def shards(
    inputs,
    cotangent,
    block_ids,
    ln1_gain,
    ln1_bias,
    qkv_weight,
    qkv_bias,
    out_weight,
    ln2_gain,
    ln2_bias,
    gate_weight,
    up_weight,
    down_weight,
):
    sb, sx, c, fh, fl = (lax.axis_index(a).astype(jnp.int32) for a in EVERY)
    n_sx = lax.axis_size("sx")
    sr, n_sr = sx * 2 + c, 2 * n_sx
    quad = 2 * n_sx
    n_dev = 8 * n_sr
    members = 2 * n_sr
    tok = inputs.shape[2]
    m = 2 * tok
    D = inputs.shape[3]
    length = block_ids.shape[2]
    N = 2 * length
    rows = qkv_weight.shape[0]
    ff_rows = down_weight.shape[0]
    ff = 4 * ff_rows
    heads = H // members
    wide = heads * HD
    natural = H % n_dev == 0
    sc = jnp.stack([sb, fh, fl, sx, sr])

    def pick(v, i):
        return lax.dynamic_index_in_dim(v, i, 0, keepdims=False)

    def device_of(t, a):
        return (((a // 2) * n_sr + t // 2) * 2 + a % 2) * 2 + t % 2

    def head_of(t, i):
        return device_of(t, i) if natural else t * heads + i

    qkv_plan = [
        [(0, (head_of(t, i) * 3 + part) * HD, HD) for part in range(3) for i in range(heads)]
        for t in range(members)
    ]
    gu_plan = [
        [(w, device_of(t, a) * ff_rows, ff_rows) for w in range(2) for a in range(4)]
        for t in range(members)
    ]
    head_place = {head_of(t, i): (t, i) for t in range(members) for i in range(heads)}
    qkv_back = [
        (head_place[h][0], part * wide + head_place[h][1] * HD, HD) for h in range(H) for part in range(3)
    ]
    ff_place = {device_of(t, a): (t, a) for t in range(members) for a in range(4)}
    gate_back = [(ff_place[d][0], ff_place[d][1] * ff_rows, ff_rows) for d in range(n_dev)]
    up_back = [(t, ff + b, n) for t, b, n in gate_back]

    def exchange(v):
        return lax.all_to_all(v, MEMBERS, split_axis=0, concat_axis=0, tiled=True)

    def of_rows(v):
        return v.reshape((n_sr, 2) + v.shape[1:])

    def both(bit, own, other):
        return jnp.stack([jnp.where(bit == 0, own, other), jnp.where(bit == 0, other, own)])

    my_ids = pick(block_ids, sb)
    c_of = (jnp.arange(2, dtype=jnp.int32) ^ c)[:, None, None, None]
    sx_of = (jnp.arange(n_sx, dtype=jnp.int32) ^ sx)[None, :, None, None]
    sb_of = (jnp.arange(2, dtype=jnp.int32) ^ sb)[None, None, :, None]
    pos = ((sb_of * n_sx + sx_of) * 2 + c_of) * tok + jnp.arange(tok, dtype=jnp.int32)[None, None, None, :]
    pos = pos.reshape(-1)
    half = ROT // 2
    lane = np.arange(2 * wide) % HD
    turned = lane < ROT
    frequency = np.where(turned, rope_base ** (-2.0 * (lane % half).astype(np.float32) / ROT), 0.0)
    angles = pos.astype(F32)[:, None] * jnp.asarray(frequency, F32)[None, :]
    sine = jnp.sin(angles)
    to_back = jnp.asarray(np.where(turned & (lane >= half), 1.0, 0.0), F32)
    to_front = jnp.asarray(np.where(lane < half, -1.0, 0.0), F32)
    tables = jnp.stack([jnp.cos(angles), sine * to_back, sine * to_front])

    rep = lambda v_: jnp.broadcast_to(v_[None], (quad,) + v_.shape)
    flat = lambda v_: v_.reshape(-1, v_.shape[-1])
    blocks = lambda v_: v_.reshape(2, n_sx, m, D)
    firsts = gather_rows(n_sx, m)

    def plus(a_, b_, kind=F32):
        return (a_.astype(F32) + b_.astype(F32)).astype(kind)

    vectors = [v_[None] for v_ in (ln1_gain, ln1_bias, ln2_gain, ln2_bias, qkv_bias)]
    live = Live(
        sc=sc,
        inputs=inputs,
        cotangent=cotangent,
        my_ids=my_ids,
        out_w=out_weight,
        gate_w=gate_weight,
        up_w=up_weight,
        down_w=down_weight,
    )
    half_rows = ff_rows // 32 * 16 if ff_rows % 16 == 0 else ff_rows // 2
    live.done(qkv_c=columns([qkv_weight], qkv_plan, vectors))
    give = jnp.concatenate([pick(live.inputs, 1 - sb)[0], pick(live.cotangent, 1 - sb)[0]], 0)
    live.done(
        w_qkv=of_rows(exchange(live.qkv_c)),
        got=swap_sb(give),
        out_1=swap_fh(live.out_w) if natural else live.out_w,
        out_2=swap_sb(live.out_w) if natural else live.out_w,
        ids_got=swap_fl(live.my_ids),
        gu_c=columns([live.gate_w, live.up_w], gu_plan),
        down_a=live.down_w[:half_rows],
        down_b=live.down_w[half_rows:],
        tables=tables,
    )

    own_x = jnp.concatenate([pick(live.inputs, sb)[0], live.got[:tok]], 0)
    own_dy = jnp.concatenate([pick(live.cotangent, sb)[0], live.got[tok:]], 0)
    ids = both(fl, live.my_ids, live.ids_got).reshape(2, 2, n_sx, 2, tok)
    ids = flip_if(fl, flip_if(c, flip_if(sb, ids, 1), 3), 0)
    ids = xor_order(ids, 2, sx, n_sx).transpose(0, 3, 2, 1, 4).reshape(2, length)
    live.drop("inputs", "cotangent", "got", "my_ids", "ids_got", "gate_w", "up_w", "qkv_c")
    live.done(
        qkv_1=swap_fh(live.w_qkv),
        qkv_2=swap_sb(live.w_qkv),
        w_gu=of_rows(exchange(live.gu_c)),
        own_x=own_x,
        own_dy=own_dy,
        x_first=gather_first(own_x),
        out_3=swap_sb(live.out_1) if natural else live.out_w,
        ids=ids,
        id_col=ids.reshape(N, 1),
        dy_rep=rep(own_dy),
    )

    cuts = [n_sr * n // 4 for n in (0, 1, 3, 4)]
    part = [live.w_gu[a_:b_] for a_, b_ in zip(cuts, cuts[1:])]
    if natural:
        out_own = in_order((live.out_w, live.out_1, live.out_2, live.out_3), sb, fh)
        out_own = out_own.reshape(wide, D)
    else:
        out_all = lax.all_gather(out_weight, EVERY, axis=0, tiled=True)
        out_own = lax.dynamic_slice_in_dim(out_all, (sr * 2 + fl) * wide, wide, 0)
    live.done(
        qkv_3=swap_sb(live.qkv_1),
        x_all=gather_second(live.x_first),
        gu_1=[swap_fh(part[0])],
        gu_part=part,
        out_own=out_own,
    )

    qkv = lambda: [(live.w_qkv, 0, 0), (live.qkv_1, 1, 0), (live.qkv_2, 2, 0), (live.qkv_3, 3, 0)]
    h1, q, k, v, o, lse, keep, send, vectors = attention(
        live.sc,
        Rows(live.x_all, firsts),
        live.tables,
        live.ids,
        live.id_col,
        live.out_own,
        qkv(),
        heads,
        rows,
    )
    live.drop("x_first", "x_all", "out_w", "out_1", "out_2", "out_3", "gu_c")
    live.done(
        h1=h1,
        q=q,
        k=k,
        v=v,
        o=o,
        lse=lse,
        keep=keep,
        send=send,
        vectors=vectors,
        gu_1=live.gu_1 + [swap_fh(live.gu_part[1])],
        gu_2=swap_sb(live.w_gu),
        dy_mine=flat(over_quad(live.dy_rep)),
    )
    live.drop("dy_rep")

    live.done(got=swap_c(live.send), dy_other=swap_c(live.dy_mine))
    send_x, send_l, keep_x, keep_l = add_first(blocks(live.keep), blocks(live.got))
    live.done(
        keep=(keep_x, keep_l),
        got=(swap_sx(send_x), swap_fl(send_l)),
        gu_1=live.gu_1 + [swap_fh(live.gu_part[2])],
        gu_3=[swap_sb(v_) for v_ in live.gu_1],
    )
    send_x, send_l, keep_x, keep_l = add_second(live.keep[0], live.got[0], live.keep[1], live.got[1])
    live.done(
        keep=(keep_x, keep_l),
        got=(swap_fl(send_x), swap_sx(send_l)),
        down_1b=swap_fh(live.down_b),
        down_2=swap_sb(live.down_w),
        gu_3=live.gu_3 + [swap_sb(live.gu_1[2])],
    )
    terms = (live.keep[0], live.got[0], live.keep[1], live.got[1])
    x2_own, h2_own = norm_step(terms, live.own_x, live.vectors)
    live.done(
        x2_own=x2_own,
        h2_first=gather_first(h2_own),
        down_3b=swap_sb(live.down_1b),
        down_1a=swap_fh(live.down_a),
    )
    live.done(h2_all=gather_second(live.h2_first), down_3a=swap_sb(live.down_1a))

    down = [live.down_w, live.down_1a, live.down_1b, live.down_2, live.down_3a, live.down_3b]
    down_places = [(0, 0), (1, 0), (1, half_rows), (2, 0), (3, 0), (3, half_rows)]
    if ff_rows % 16 != 0:
        down = [live.down_w, jnp.concatenate(down[1:3], 0), live.down_2, jnp.concatenate(down[4:6], 0)]
        down, down_places = [in_order(down, sb, fh).reshape(ff, D)], [(0, 0)]
    gu = [(live.w_gu, 0, 0), (live.gu_2, 2, 0)]
    gu += [(v_, 1, n) for n, v_ in zip(cuts, live.gu_1)] + [(v_, 3, n) for n, v_ in zip(cuts, live.gu_3)]
    h2, act, d_gu, keep, send = ffn(
        live.sc,
        Rows(live.h2_all, firsts),
        Quads(live.dy_mine, live.dy_other, m),
        gu,
        down,
        down_places,
        rows,
    )
    live.drop("w_gu", "gu_1", "gu_2", "gu_3", "gu_part", "down_a", "down_b", "down_w")
    live.drop("down_1a", "down_1b", "down_2", "down_3a", "down_3b")
    live.drop("h2_first", "h2_all")

    def give_back(v_):
        other = swap_sb(v_[tok:])
        first = jnp.where(sb == 0, v_[:tok], other)
        second = jnp.where(sb == 0, other, v_[:tok])
        return jnp.stack([first, second])[:, None]

    live.done(
        h2=h2,
        act=act,
        d_gu=d_gu,
        down=down,
        keep=keep,
        got=swap_c(send),
        gu_t=grad_rows(live.sc, h2, d_gu, 1, n_sr, rows),
    )
    send_x, send_l, keep_x, keep_l = add_first(blocks(live.keep), blocks(live.got))
    y_keep, y_send = down_product(live.sc, live.act, live.down, down_places)
    live.drop("down")
    live.done(
        keep=(keep_x, keep_l),
        got=(swap_sx(send_x), swap_fl(send_l)),
        gu_got1=swap_sb(live.gu_t[0]),
        gu_m=grad_rows(live.sc, live.h2, live.d_gu, 0, n_sr, rows),
        y_keep=y_keep,
        y_send=y_send,
    )
    live.drop("h2", "d_gu")
    send_x, send_l, keep_x, keep_l = add_second(live.keep[0], live.got[0], live.keep[1], live.got[1])
    halves = lambda v_: (v_[: v_.shape[0] // 2], v_[v_.shape[0] // 2 :])
    gu_give = [plus(a_, b_, BF16) for a_, b_ in zip(halves(live.gu_m[0]), halves(live.gu_got1))]
    live.done(
        keep=(keep_x, keep_l),
        got=(swap_fl(send_x), swap_sx(send_l)),
        gu_got1=swap_sb(live.gu_t[1]),
        gu_over=[swap_fh(gu_give[0])],
        gu_give=gu_give[1],
        down_t=grad_slices(live.sc, live.act, Quads(live.dy_mine, live.dy_other, m)),
        y_got=swap_c(live.y_send),
    )
    live.drop("dy_mine", "dy_other", "act", "y_send")
    terms = (live.keep[0], live.got[0], live.keep[1], live.got[1])
    d_x2, d_att, sums2 = norm_step_back(terms, live.x2_own, live.own_dy, live.vectors, 2)
    gu_give = [plus(a_, b_, BF16) for a_, b_ in zip(halves(live.gu_m[1]), halves(live.gu_got1))]
    live.done(
        d_x2=d_x2,
        sums2=sums2,
        att_first=gather_first(d_att),
        gu_over=live.gu_over + [swap_fh(live.gu_give)],
        gu_give=gu_give,
        down_got1=swap_sb(live.down_t[3]),
        y_sum=plus(live.y_keep, live.y_got, BF16),
    )
    live.drop("gu_got1", "y_keep", "y_got")
    down_cut = live.down_t[1].shape[0] // 32 * 16
    down_give = plus(live.down_t[1], live.down_got1, BF16)
    live.done(
        att_all=gather_second(live.att_first),
        gu_over=live.gu_over + [swap_fh(live.gu_give[0])],
        down_got0=swap_sb(live.down_t[2]),
        down_give=(down_give[:down_cut], down_give[down_cut:]),
    )
    live.drop("att_first")
    d_lin, bias_term, sums1, keep, send = attention_back(
        live.sc,
        live.tables,
        live.ids,
        live.id_col,
        live.q,
        live.k,
        live.v,
        live.lse,
        live.out_own,
        live.h1,
        live.vectors,
        Rows(live.att_all, firsts),
        qkv(),
    )
    live.drop("q", "k", "v", "lse", "out_own", "w_qkv", "qkv_1", "qkv_2", "qkv_3", "tables", "ids", "id_col")
    live.done(
        d_lin=d_lin,
        bias_term=bias_term,
        sums1=sums1,
        keep=keep,
        send=send,
        y_terms=over_quad(live.y_sum.reshape(quad, m, D)),
        gu_got0=swap_sb(live.gu_t[2]),
        gu_over=live.gu_over + [swap_fh(live.gu_give[1])],
    )
    live.drop("gu_give", "y_sum", "down_got1", "gu_t")
    live.done(
        got=swap_c(live.send),
        qkv_t=grad_rows(live.sc, live.h1, live.d_lin, 1, n_sr, rows, 1),
    )
    live.drop("send")

    def half_sum(v_, bit, swap):
        n = v_.shape[1] // 2
        take = lambda k: lax.dynamic_slice_in_dim(v_, k * n, n, 1)
        return take(bit) + swap(take(1 - bit))

    bias_term = live.bias_term.reshape(3, heads, HD).transpose(1, 0, 2)
    if natural:
        bias_term = bias_term.reshape(2, 1, 2, 1, -1)
        here = jnp.arange(n_sr)[None, :, None, None, None] == sr
        here = here & (jnp.arange(2)[None, None, None, :, None] == fl)
    else:
        bias_term = bias_term[None]
        here = jnp.arange(members)[:, None, None, None] == sr * 2 + fl
    bias_term = jnp.where(here, bias_term, 0.0).reshape(n_dev, 3, rows).transpose(1, 0, 2).reshape(3, D)
    gu_sum = plus(live.gu_m[2], live.gu_got0) + jnp.concatenate(live.gu_over, 0).astype(F32)
    send_x, send_l, keep_x, keep_l = add_first(blocks(live.keep), blocks(live.got))
    live.done(
        keep=(keep_x, keep_l),
        got=(swap_sx(send_x), swap_fl(send_l)),
        qkv_got1=swap_sb(live.qkv_t[0]),
        down_over=[swap_fh(live.down_give[1])],
        down_give=live.down_give[0],
        qkv_m=grad_rows(live.sc, live.h1, live.d_lin, 0, n_sr, rows, 1),
        gu_sum=gu_sum.astype(BF16),
        small=jnp.concatenate([live.sums1, live.sums2, bias_term], axis=0),
        out_t=grad_slices(live.sc, live.o, Rows(live.att_all, firsts)) if natural else (),
    )
    live.drop("h1", "d_lin", "gu_m", "gu_got0", "gu_over")
    send_x, send_l, keep_x, keep_l = add_second(live.keep[0], live.got[0], live.keep[1], live.got[1])
    qkv_give = [plus(a_, b_, BF16) for a_, b_ in zip(halves(live.qkv_m[0]), halves(live.qkv_got1))]
    live.done(
        keep=(keep_x, keep_l),
        got=(swap_fl(send_x), swap_sx(send_l)),
        qkv_got0=swap_sb(live.qkv_t[1]),
        qkv_over=[swap_fh(qkv_give[0])],
        qkv_give=qkv_give[1],
        small=half_sum(live.small, sb, swap_sb),
    )
    live.drop("qkv_t", "qkv_got1")
    terms = (live.keep[0], live.got[0], live.keep[1], live.got[1])
    _, input_low, _ = norm_step_back(terms, live.own_x, live.d_x2, live.vectors, 0)
    y = live.x2_own + jnp.sum(live.y_terms.astype(F32), axis=0)
    small = live.small
    bit = n_sx // 2
    while bit >= 1:
        small = half_sum(small, (sx // bit) % 2, functools.partial(swap_sx, bit=bit))
        bit //= 2
    live.done(
        input_low=input_low,
        small=half_sum(small, c, swap_c),
        qkv_over=live.qkv_over + [swap_fh(live.qkv_give)],
        out_got=[swap_sb(v_) for v_ in live.out_t[2:]],
        qkv_sum=plus(live.qkv_m[1], live.qkv_got0),
        layer_out=give_back(y.astype(BF16)),
        gu_done=exchange(live.gu_sum.reshape(members, rows, -1)),
    )
    live.drop("y_terms", "gu_sum")
    live.done(qkv_sum=(live.qkv_sum + jnp.concatenate(live.qkv_over, 0).astype(F32)).astype(BF16))
    if natural:
        out_over = swap_fh(plus(live.out_t[1], live.out_got[1], BF16))
    else:
        d_att = jnp.zeros((N, D), BF16)
        for v_, r in zip(live.att_all, firsts):
            d_att = lax.dynamic_update_slice_in_dim(d_att, v_, r, 0)
        t = lax.dot_general(live.o, d_att, TN, preferred_element_type=F32)
        t = jnp.where(jnp.arange(members)[:, None, None] == sr * 2 + fl, t[None], 0.0)
        out_over = lax.psum_scatter(t.reshape(H * HD, D), EVERY, scatter_dimension=0, tiled=True)
    live.done(
        qkv_done=exchange(live.qkv_sum.reshape(members, rows, -1)),
        out_over=out_over,
        small=half_sum(live.small, fh, swap_fh),
        down_over=[swap_fh(live.down_give)] + live.down_over,
        input_grad=give_back(live.input_low),
        gate_grad=uncolumns([live.gu_done], gate_back),
        up_grad=uncolumns([live.gu_done], up_back),
    )
    small = half_sum(live.small, fl, swap_fl)
    qkv_grad = uncolumns([live.qkv_done], qkv_back)
    out_grad = live.out_over
    if natural:
        out_grad = plus(live.out_t[0], live.out_got[0]) + out_grad.astype(F32)
    input_grad, layer_out = live.input_grad, live.layer_out
    down_grad = plus(live.down_t[0], live.down_got0) + jnp.concatenate(live.down_over, 0).astype(F32)
    gate_grad, up_grad = live.gate_grad, live.up_grad
    gain1_grad, bias1_grad, gain2_grad, bias2_grad = (small[n] for n in range(4))
    bias_grad = small[4:].reshape(-1)
    return (
        layer_out,
        input_grad,
        gain1_grad,
        bias1_grad,
        qkv_grad,
        bias_grad,
        out_grad,
        gain2_grad,
        bias2_grad,
        gate_grad,
        up_grad,
        down_grad,
    )


def solution(mesh):
    names = dict(mesh.shape)
    n_seq, n_fsdp = names["seq"], names["fsdp"]
    fine = Mesh(mesh.devices.reshape(2, n_seq // 4, 2, 2, n_fsdp // 2), EVERY)
    tokens = P(None, ("fh", "fl"), ("sb", "sx", "c"), None)
    vector = P(EVERY)
    matrix = P(EVERY, None)
    in_specs = (tokens, tokens, P(None, ("fh", "fl"), None), vector, vector, matrix, vector, matrix)
    in_specs += (vector, vector, matrix, matrix, matrix)
    out_specs = (tokens, tokens, vector, vector, matrix, vector, matrix, vector, vector)
    out_specs += (matrix, matrix, matrix)
    return jax.shard_map(shards, mesh=fine, in_specs=in_specs, out_specs=out_specs, check_vma=False)
```

```python
import functools

import jax
import jax.numpy as jnp
import numpy as np
from jax import lax
from jax.experimental import pallas as pl
from jax.experimental.pallas import tpu as pltpu
from jax.sharding import Mesh
from jax.sharding import PartitionSpec as P

H = 32
HD = 64
ROT = 16

eps_norm = 1e-05
rope_base = 10000.0
masked_score = -1e30

F32 = jnp.float32
BF16 = jnp.bfloat16

SWAP = [(0, 1), (1, 0)]
EVERY = ("sb", "sx", "c", "fh", "fl")
MEMBERS = ("sx", "c", "fl")
QUAD = ("fl", "sx")
ANY = pl.BlockSpec(memory_space=pl.ANY)
SMEM = pl.BlockSpec(memory_space=pltpu.SMEM)
VMEM = pl.BlockSpec(memory_space=pltpu.VMEM)
NT = (((1,), (1,)), ((), ()))
TN = (((0,), (0,)), ((), ()))
LIMIT = 60 * 1024 * 1024


def params():
    return pltpu.CompilerParams(vmem_limit_bytes=LIMIT)


def cost(microseconds):
    return pl.CostEstimate(flops=int(microseconds * 2e8), bytes_accessed=1024, transcendentals=0)


def dot(a, b, dims=(((1,), (0,)), ((), ()))):
    return lax.dot_general(a, b, dims, preferred_element_type=F32)


def swap_sb(v):
    return lax.ppermute(v, "sb", SWAP)


def swap_fh(v):
    return lax.ppermute(v, "fh", SWAP)


def swap_fl(v):
    return lax.ppermute(v, "fl", SWAP)


def swap_c(v):
    return lax.ppermute(v, "c", SWAP)


def swap_sx(v, bit=1):
    n = lax.axis_size("sx")
    return lax.ppermute(v, "sx", [(i, i ^ bit) for i in range(n)])


def over_quad(v):
    return lax.all_to_all(v, QUAD, split_axis=0, concat_axis=0, tiled=True)


class Live(dict):
    def __getattr__(self, name):
        return self[name]

    def done(self, **new):
        self.update(new)
        self.update(lax.optimization_barrier(dict(self)))

    def drop(self, *names):
        for name in names:
            del self[name]


def normalize(values):
    average = jnp.mean(values, axis=-1, keepdims=True)
    centered = values - average
    inv_std = lax.rsqrt(jnp.mean(centered * centered, axis=-1, keepdims=True) + eps_norm)
    return centered * inv_std, inv_std


def normalize_back(grad_normed, normed, inv_std):
    first_mean = jnp.mean(grad_normed, axis=-1, keepdims=True)
    second_mean = jnp.mean(grad_normed * normed, axis=-1, keepdims=True)
    return inv_std * (grad_normed - first_mean - normed * second_mean)


def gather_first(x):
    return (x, swap_sx(x), swap_fl(x), swap_c(x))


def gather_second(first):
    n_sx = lax.axis_size("sx")
    x, a, b, xo = first
    h = x.shape[0] // 2
    d1 = swap_fl(a[:h])
    d2 = swap_sx(b[h:])
    ao = swap_c(a)
    bo = swap_c(b)
    got = [x, a, b, d1, d2, xo, ao, bo, swap_c(d1), swap_c(d2)]
    bit = 2
    while bit < n_sx:
        got = got + [swap_sx(v, bit) for v in got]
        bit *= 2
    return got


def gather_rows(n_sx, m):
    h = m // 2
    got = []
    for c in range(2):
        at = c * n_sx * m
        over = 2 * n_sx * m + at
        got += [at, at + m, over, over + m, over + m + h]
    bit = 2
    while bit < n_sx:
        got = got + [r + bit * m for r in got]
        bit *= 2
    return got


def add_first_kernel(keep, got, send_x, send_l, keep_x, keep_l):
    h = keep.shape[2] // 2
    for f in range(2):
        for x in range(2):
            q = keep[f, x].astype(F32) + got[f, x].astype(F32)
            if x == 1:
                send_x[f] = q[:h].astype(BF16)
            else:
                keep_x[f] = q[:h]
            if f == 1:
                send_l[x] = q[h:].astype(BF16)
            else:
                keep_l[x] = q[h:]


def add_second_kernel(keep_x, got_x, keep_l, got_l, send_x, send_l, own_x, own_l):
    own_x[...] = keep_x[0] + got_x[0].astype(F32)
    own_l[...] = keep_l[0] + got_l[0].astype(F32)
    send_x[...] = (keep_x[1] + got_x[1].astype(F32)).astype(BF16)
    send_l[...] = (keep_l[1] + got_l[1].astype(F32)).astype(BF16)


def add_first(keep, got):
    bit = keep.shape[1] // 2
    while bit >= 2:
        q = keep.astype(F32) + got.astype(F32)
        keep = q[:, :bit].astype(BF16)
        got = swap_sx(q[:, bit:].astype(BF16), bit)
        bit //= 2
    m, D = keep.shape[2:]
    h = m // 2
    low = jax.ShapeDtypeStruct((2, h, D), BF16)
    high = jax.ShapeDtypeStruct((2, h, D), F32)
    return pl.pallas_call(
        add_first_kernel,
        out_shape=[low, low, high, high],
        in_specs=[VMEM] * 2,
        out_specs=[VMEM] * 4,
        compiler_params=params(),
        cost_estimate=cost(4),
    )(keep, got)


def add_second(keep_x, got_x, keep_l, got_l):
    _, h, D = keep_x.shape
    return pl.pallas_call(
        add_second_kernel,
        out_shape=[jax.ShapeDtypeStruct((h, D), BF16)] * 2 + [jax.ShapeDtypeStruct((h, D), F32)] * 2,
        in_specs=[VMEM] * 4,
        out_specs=[VMEM] * 4,
        compiler_params=params(),
        cost_estimate=cost(3),
    )(keep_x, got_x, keep_l, got_l)


def in_order(pieces, sb, fh):
    w, z, y, yz = pieces
    a, b = jnp.where(fh == 1, z, w), jnp.where(fh == 1, w, z)
    c, d = jnp.where(fh == 1, yz, y), jnp.where(fh == 1, y, yz)
    first = jnp.stack([jnp.where(sb == 1, c, a), jnp.where(sb == 1, d, b)])
    second = jnp.stack([jnp.where(sb == 1, a, c), jnp.where(sb == 1, b, d)])
    return jnp.stack([first, second])


def flip_if(bit, v, axis):
    return jnp.where(bit == 1, lax.rev(v, (axis,)), v)


def xor_order(v, axis, index, n):
    shape = v.shape
    bit = 1
    while bit < n:
        r = v.reshape(shape[:axis] + (n // (2 * bit), 2, bit) + shape[axis + 1 :])
        v = flip_if((index // bit) % 2, r, axis + 1).reshape(shape)
        bit *= 2
    return v


def load_groups(sc, pieces, places, buf, sems, first=0, start=True):
    copies = []
    rows = buf.shape[4]
    for n, (piece, (k, r)) in enumerate(zip(pieces, places)):
        where = buf.at[sc[0] ^ (k // 2), pl.ds(r, piece.shape[0]), sc[1] ^ (k % 2)]
        copies.append(pltpu.make_async_copy(piece.at[:, :, pl.ds(first, rows)], where, sems.at[n]))
    for c in copies if start else ():
        c.start()
    return copies


def load_down(sc, pieces, places, buf, sems, start=True):
    copies = []
    for n, (piece, (k, r)) in enumerate(zip(pieces, places)):
        where = buf
        if len(places) > 1:
            where = buf.at[sc[0] ^ (k // 2), sc[1] ^ (k % 2), pl.ds(r, piece.shape[0])]
        copies.append(pltpu.make_async_copy(piece, where, sems.at[n]))
    for c in copies if start else ():
        c.start()
    return copies


class Rows:
    def __init__(self, arrays, firsts):
        self.arrays, self.firsts = list(arrays), firsts
        self.N, self.D = sum(v.shape[0] for v in arrays), arrays[0].shape[1]

    def scratch(self):
        return [pltpu.VMEM((self.N, self.D), BF16), pltpu.SemaphoreType.DMA((len(self.arrays),))]

    def load(self, sc, refs, buf, sems, start=True):
        copies = [
            pltpu.make_async_copy(ref, buf.at[pl.ds(r, ref.shape[0])], sems.at[n])
            for n, (ref, r) in enumerate(zip(refs, self.firsts))
        ]
        for c in copies if start else ():
            c.start()
        return copies


class Quads:
    def __init__(self, mine, other, m):
        self.arrays, self.m = [mine, other], m
        self.N, self.D = 2 * mine.shape[0], mine.shape[1]
        self.n_sx = mine.shape[0] // (2 * m)

    def scratch(self):
        return [pltpu.VMEM((self.N, self.D), BF16), pltpu.SemaphoreType.DMA((4 * self.n_sx,))]

    def load(self, sc, refs, buf, sems, start=True):
        copies = []
        for k in range(2):
            for f in range(2):
                for x in range(self.n_sx):
                    to = ((2 * (f ^ sc[2]) + k) * self.n_sx + (x ^ sc[3])) * self.m
                    copies.append(
                        pltpu.make_async_copy(
                            refs[k].at[pl.ds((f * self.n_sx + x) * self.m, self.m)],
                            buf.at[pl.ds(pl.multiple_of(to, self.m), self.m)],
                            sems.at[len(copies)],
                        )
                    )
        for c in copies if start else ():
            c.start()
        return copies


def sides(nb, by_index=False):
    def place(f, b, sc):
        if by_index:
            f, b = f ^ sc[2], b ^ (sc[3] // 2)
        return f * nb + b

    def keep(i, sc=None):
        f, k, b = i // (2 * nb), lax.rem(i // nb, 2), lax.rem(i, nb)
        return place(f, jnp.where(k == 0, b, nb - 1), sc)

    def send(i, sc=None):
        f, k, b = i // (2 * nb), lax.rem(i // nb, 2), lax.rem(i, nb)
        return place(f, jnp.where(k == 0, 0, b), sc)

    return keep, send


def columns_kernel(plan, n_in, *refs):
    ins, vectors, out = refs[:n_in], refs[n_in:-1], refs[-1]
    rows = ins[0].shape[0]
    if vectors:
        row = jnp.concatenate([v[...] for v in vectors], axis=-1)
    for t, ranges in enumerate(plan):
        out[t, :rows] = jnp.concatenate([ins[i][:, a : a + n] for i, a, n in ranges], axis=-1)
        if vectors:
            out[t, rows : rows + 1, : row.shape[1]] = row


def columns(arrays, plan, vectors=()):
    width = sum(n for _, _, n in plan[0])
    rows = arrays[0].shape[0] + (8 if vectors else 0)
    return pl.pallas_call(
        functools.partial(columns_kernel, plan, len(arrays)),
        out_shape=jax.ShapeDtypeStruct((len(plan), rows, width), arrays[0].dtype),
        in_specs=[VMEM] * (len(arrays) + len(vectors)),
        out_specs=VMEM,
        compiler_params=params(),
        cost_estimate=cost(3),
    )(*arrays, *vectors)


def uncolumns_kernel(plan, *refs):
    ins, out = refs[:-1], refs[-1]
    width = ins[0].shape[2]
    if True:
        at, group, size = 0, [], 0
        for t, b, n in plan:
            group.append(ins[b // width][t, :, b % width : b % width + n].astype(F32))
            size += n
            if size % 128 == 0:
                out[:, at : at + size] = jnp.concatenate(group, axis=-1)
                at, group, size = at + size, [], 0
        if group:
            out[:, at : at + size] = jnp.concatenate(group, axis=-1)


def uncolumns(arrays, plan):
    rows = arrays[0].shape[1]
    return pl.pallas_call(
        functools.partial(uncolumns_kernel, plan),
        out_shape=jax.ShapeDtypeStruct((rows, sum(n for _, _, n in plan)), F32),
        in_specs=[VMEM] * len(arrays),
        out_specs=VMEM,
        compiler_params=params(),
        cost_estimate=cost(3),
    )(*arrays)


def turn(v, c_ref_value, sa, sb_, direction):
    width = v.shape[1]
    back = pltpu.roll(v, ROT // 2, 1)
    front = pltpu.roll(v, width - ROT // 2, 1)
    return v * c_ref_value + direction * (back * sa + front * sb_)


def attention_kernel(dims, places, x_rows, sc, tables, id_row, id_col, w_out, *refs):
    heads, length, block, D = dims
    x_refs, refs = refs[: len(x_rows.arrays)], refs[len(x_rows.arrays) :]
    w_refs, refs = refs[: len(places)], refs[len(places) :]
    h1, q, k, v, o, lse, keep, send, vectors, w, sems, small, small_sems, bias_q, x_buf, x_sems = refs
    wide = heads * HD
    per = length // block
    i = pl.program_id(0)

    @pl.when(i == 0)
    def _():
        n_sr, rows_ = w.shape[1], w.shape[4]
        copies = x_rows.load(sc, x_refs, x_buf, x_sems)
        copies += load_groups(sc, w_refs, places, small, small_sems, rows_)
        for c in load_groups(sc, w_refs, places, w, sems) + copies:
            c.wait()
        every = [(s, j, f, l) for s in range(2) for j in range(n_sr) for f in range(2) for l in range(2)]
        for n in range(4):
            row = [small[s, j, f, l, 0:1, n * rows_ : (n + 1) * rows_] for s, j, f, l in every]
            vectors[n : n + 1, :] = jnp.concatenate(row, axis=-1).astype(F32)
        first = 4 * rows_
        if 3 * rows_ == 3 * HD:
            row = [
                small[a // 2, sc[4], a % 2, sc[2], 0:1, first + p * HD : first + (p + 1) * HD]
                for p in range(3)
                for a in range(heads)
            ]
        else:
            count = 3 * HD // (3 * rows_)
            row = []
            for a in range(heads):
                for n in range(count):
                    d = ((sc[4] * 2 + sc[2]) * heads + a) * count + n
                    at = (d // (4 * n_sr), lax.rem(d // 4, n_sr), lax.rem(d // 2, 2), lax.rem(d, 2))
                    row.append(small[at[0], at[1], at[2], at[3], 0:1, first : first + 3 * rows_])
        bias_q[...] = jnp.concatenate(row, axis=-1).astype(F32)

    rows = pl.ds(pl.multiple_of(i * block, block), block)
    normed, _ = normalize(x_buf[rows, :].astype(F32))
    h = (normed * vectors[0:1, :] + vectors[1:2, :]).astype(BF16)
    h1[...] = h
    lin = dot(h, w[...].reshape(D, 3 * wide)) + bias_q[...]
    qk = turn(lin[:, : 2 * wide], tables[0], tables[1], tables[2], 1.0)
    q[rows, :] = (qk[:, :wide] * (HD**-0.5)).astype(BF16)
    k[rows, :] = qk[:, wide:].astype(BF16)
    v[rows, :] = lin[:, 2 * wide :].astype(BF16)

    @pl.when(lax.rem(i, per) == per - 1)
    def _():
        s = i // per
        start = pl.multiple_of(s * length, length)
        step = min(length, (1 << 18) // length)
        for r in range(length // step):
            part = pl.ds(pl.multiple_of(start + r * step, step), step)
            allowed = id_col[part, 0:1] >= id_row[pl.ds(s, 1), :]
            for hd in range(heads):
                lanes = slice(hd * HD, (hd + 1) * HD)
                kh = k[pl.ds(start, length), lanes]
                vh = v[pl.ds(start, length), lanes]
                score = dot(q[part, lanes], kh, NT)
                score = jnp.where(allowed, score, masked_score)
                peak = jnp.max(score, axis=-1, keepdims=True)
                e = jnp.exp(score - peak)
                total = jnp.sum(e, axis=-1, keepdims=True)
                p = (e * (1.0 / total)).astype(BF16)
                o[part, lanes] = dot(p, vh).astype(BF16)
                lse[part, hd : hd + 1] = peak + jnp.log(total)
        for side, out in enumerate((keep, send)):
            for b in range(per // 2):
                part = pl.ds(pl.multiple_of(start + (side * (per // 2) + b) * block, block), block)
                out[0, b * block : (b + 1) * block] = dot(o[part, :], w_out[...]).astype(BF16)


def attention(sc, x_rows, tables, id_row, id_col, w_out, weight, heads, rows):
    N, D = x_rows.N, x_rows.D
    length = N // 2
    block = 256
    per = length // block
    wide = heads * HD
    n_sr, _, _, f = weight[0][0].shape
    places = [p[1:] for p in weight]
    whole = lambda shape: pl.BlockSpec(shape, lambda i, sc: (0,) * len(shape))
    side = pl.BlockSpec((1, length // 2, D), lambda i, sc: (i // per, 0, 0))
    spec = pltpu.PrefetchScalarGridSpec(
        num_scalar_prefetch=1,
        grid=(N // block,),
        in_specs=[
            pl.BlockSpec((3, block, 2 * wide), lambda i, sc: (0, lax.rem(i, per), 0)),
            whole((2, length)),
            whole((N, 1)),
            whole((wide, D)),
        ]
        + [ANY] * (len(x_rows.arrays) + len(places)),
        out_specs=[pl.BlockSpec((block, D), lambda i, sc: (i, 0))]
        + [whole((N, wide))] * 4
        + [whole((N, heads)), side, side, whole((4, D))],
        scratch_shapes=[
            pltpu.VMEM((2, n_sr, 2, 2, rows, f), BF16),
            pltpu.SemaphoreType.DMA((len(places),)),
            pltpu.VMEM((2, n_sr, 2, 2, 8, f), BF16),
            pltpu.SemaphoreType.DMA((len(places),)),
            pltpu.VMEM((1, 3 * wide), F32),
        ]
        + x_rows.scratch(),
    )
    return pl.pallas_call(
        functools.partial(attention_kernel, (heads, length, block, D), places, x_rows),
        grid_spec=spec,
        out_shape=[jax.ShapeDtypeStruct((N, D), BF16)]
        + [jax.ShapeDtypeStruct((N, wide), BF16)] * 4
        + [jax.ShapeDtypeStruct((N, heads), F32)]
        + [jax.ShapeDtypeStruct((2, length // 2, D), BF16)] * 2
        + [jax.ShapeDtypeStruct((4, D), F32)],
        compiler_params=params(),
        cost_estimate=cost(25),
    )(sc, tables, id_row, id_col, w_out, *x_rows.arrays, *[p[0] for p in weight])


def ffn_kernel(dims, h_rows, dy_rows, sc, *refs):
    g_list, d_list, block, nb, D, ff = dims
    h_refs, refs = refs[: len(h_rows.arrays)], refs[len(h_rows.arrays) :]
    dy_refs, refs = refs[: len(dy_rows.arrays)], refs[len(dy_rows.arrays) :]
    g_refs, refs = refs[: len(g_list)], refs[len(g_list) :]
    d_refs, refs = refs[: len(d_list)], refs[len(d_list) :]
    h2, act, d_gu, keep, send, g_buf, d_buf, sem_g, sem_d, h_buf, h_sems, dy_buf, dy_sems = refs
    i = pl.program_id(0)
    rows = pl.ds(pl.multiple_of(i * block, block), block)

    @pl.when(i == 0)
    def _():
        first = h_rows.load(sc, h_refs, h_buf, h_sems) + load_groups(sc, g_refs, g_list, g_buf, sem_g)
        dy_rows.load(sc, dy_refs, dy_buf, dy_sems)
        load_down(sc, d_refs, d_list, d_buf, sem_d)
        for c in first:
            c.wait()

    h = h_buf[rows, :]
    h2[...] = h
    w_gu = g_buf[...].reshape(D, 2 * ff)
    gu = dot(h, w_gu)
    g, u = gu[:, :ff], gu[:, ff:]
    s = jax.nn.sigmoid(g)
    silu = g * s
    act[...] = (silu * u).astype(BF16)

    @pl.when(i == 0)
    def _():
        second = dy_rows.load(sc, dy_refs, dy_buf, dy_sems, False)
        for c in second + load_down(sc, d_refs, d_list, d_buf, sem_d, False):
            c.wait()

    d_act = dot(dy_buf[rows, :], d_buf[...].reshape(ff, D), NT)
    d_g = (d_act * u * s * (1.0 + g * (1.0 - s))).astype(BF16)
    d_u = (d_act * silu).astype(BF16)
    d = jnp.concatenate([d_g, d_u], axis=-1)
    d_gu[...] = d
    d_h = dot(d, w_gu, NT).astype(BF16)
    side = lax.rem(i // nb, 2)

    @pl.when(side == 0)
    def _():
        keep[...] = d_h

    @pl.when(side == 1)
    def _():
        send[...] = d_h


def ffn(sc, h_rows, dy_rows, gu, down, down_places, rows_):
    N, D = h_rows.N, h_rows.D
    block = 256
    nb = N // 4 // block
    n_sr, _, _, two_ff = gu[0][0].shape
    ff = two_ff // 2
    rows = lambda width: pl.BlockSpec((block, width), lambda i, sc: (i, 0))
    d_shape = (2, 2, ff // 4, D) if len(down) > 1 else (ff, D)
    keep, send = sides(nb)
    spec = pltpu.PrefetchScalarGridSpec(
        num_scalar_prefetch=1,
        grid=(N // block,),
        in_specs=[ANY] * (len(h_rows.arrays) + len(dy_rows.arrays) + len(gu) + len(down)),
        out_specs=[
            rows(D),
            rows(ff),
            rows(2 * ff),
            pl.BlockSpec((block, D), lambda i, sc: (keep(i), 0)),
            pl.BlockSpec((block, D), lambda i, sc: (send(i), 0)),
        ],
        scratch_shapes=[
            pltpu.VMEM((2, n_sr, 2, 2, rows_, two_ff), BF16),
            pltpu.VMEM(d_shape, BF16),
            pltpu.SemaphoreType.DMA((len(gu),)),
            pltpu.SemaphoreType.DMA((len(down),)),
        ]
        + h_rows.scratch()
        + dy_rows.scratch(),
    )
    dims = ([p[1:] for p in gu], down_places, block, nb, D, ff)
    return pl.pallas_call(
        functools.partial(ffn_kernel, dims, h_rows, dy_rows),
        grid_spec=spec,
        out_shape=[
            jax.ShapeDtypeStruct((N, D), BF16),
            jax.ShapeDtypeStruct((N, ff), BF16),
            jax.ShapeDtypeStruct((N, 2 * ff), BF16),
            jax.ShapeDtypeStruct((N // 2, D), BF16),
            jax.ShapeDtypeStruct((N // 2, D), BF16),
        ],
        compiler_params=params(),
        cost_estimate=cost(30),
    )(sc, *h_rows.arrays, *dy_rows.arrays, *[p[0] for p in gu], *down)


def down_kernel(d_list, nb, ff, D, sc, act, *refs):
    n_d = len(d_list)
    d_refs, (keep, send, d_buf, sem) = refs[:n_d], refs[n_d:]
    i = pl.program_id(0)

    @pl.when(i == 0)
    def _():
        for c in load_down(sc, d_refs, d_list, d_buf, sem):
            c.wait()

    y = dot(act[...], d_buf[...].reshape(ff, D)).astype(BF16)
    side = lax.rem(i // nb, 2)
    m = y.shape[0] // 2
    for k, out in enumerate((keep, send)):
        for t in range(2):

            @pl.when((side == k) & (lax.rem(sc[3], 2) == t))
            def _():
                out[t * m : (t + 1) * m, :] = y[:m]
                out[(1 - t) * m : (2 - t) * m, :] = y[m:]


def down_product(sc, act, down, places):
    N, ff = act.shape
    D = down[0].shape[-1]
    block = 256
    nb = N // 4 // block
    d_shape = (2, 2, ff // 4, D) if len(down) > 1 else (ff, D)
    keep, send = sides(nb, by_index=True)
    spec = pltpu.PrefetchScalarGridSpec(
        num_scalar_prefetch=1,
        grid=(N // block,),
        in_specs=[pl.BlockSpec((block, ff), lambda i, sc: (i, 0))] + [ANY] * len(down),
        out_specs=[
            pl.BlockSpec((block, D), lambda i, sc: (keep(i, sc), 0)),
            pl.BlockSpec((block, D), lambda i, sc: (send(i, sc), 0)),
        ],
        scratch_shapes=[pltpu.VMEM(d_shape, BF16), pltpu.SemaphoreType.DMA((len(down),))],
    )
    return pl.pallas_call(
        functools.partial(down_kernel, places, nb, ff, D),
        grid_spec=spec,
        out_shape=[jax.ShapeDtypeStruct((N // 2, D), BF16)] * 2,
        compiler_params=params(),
        cost_estimate=cost(9),
    )(sc, act, *down)


def h_buf_rows(length):
    return 256 if length <= 1024 else 128


def attention_back_kernel(dims, d_rows, sc, tables, id_row, id_col, q, k, v, lse, w_out, h1, vectors, *refs):
    heads, length, N, D, w_list = dims
    block = h_buf_rows(length)
    d_refs, refs = refs[: len(d_rows.arrays)], refs[len(d_rows.arrays) :]
    w_refs, refs = refs[: len(w_list)], refs[len(w_list) :]
    d_lin, bias_grad, sums, keep, send, w, d_o, d_qk, sem_w, h_buf, sem_h, d_att, sem_d = refs
    wide = heads * HD
    copies = d_rows.load(sc, d_refs, d_att, sem_d)
    loads = load_groups(sc, w_refs, w_list, w, sem_w)
    h_loads = [
        pltpu.make_async_copy(h1.at[pl.ds(n * block, block)], h_buf.at[n % 2], sem_h.at[n % 2])
        for n in range(N // block)
    ]
    h_loads[0].start()
    for c in copies:
        c.wait()
    sums[...] = jnp.zeros_like(sums)
    step = min(length, (1 << 18) // length)
    scale = HD**-0.5
    bias_grad[...] = jnp.zeros_like(bias_grad)
    for s in range(2):
        start = s * length
        for r in range(length // step):
            at = pl.ds(start + r * step, step)
            d_o[pl.ds(r * step, step), :] = dot(d_att[at, :], w_out[...], NT).astype(BF16)
        d_qk[:, wide:] = jnp.zeros_like(d_qk[:, wide:])
        for hd in range(heads):
            lanes = slice(hd * HD, (hd + 1) * HD)
            k_lanes = slice(wide + hd * HD, wide + (hd + 1) * HD)
            v_lanes = slice(2 * wide + hd * HD, 2 * wide + (hd + 1) * HD)
            kh = k[pl.ds(start, length), lanes]
            vh = v[pl.ds(start, length), lanes]
            for r in range(length // step):
                part = pl.ds(start + r * step, step)
                local = pl.ds(r * step, step)
                allowed = id_col[part, 0:1] >= id_row[s : s + 1, :]
                qh = q[part, lanes]
                score = dot(qh, kh, NT)
                p = jnp.where(allowed, jnp.exp(score - lse[part, hd : hd + 1]), 0.0)
                doh = d_o[local, lanes]
                dp = dot(doh, vh, NT)
                inner = jnp.sum(p * dp, axis=-1, keepdims=True)
                ds = (p * (dp - inner)).astype(BF16)
                d_qk[local, lanes] = dot(ds, kh) * scale
                dk = dot(ds, qh, TN)
                dv = dot(p.astype(BF16), doh, TN)
                if length == step:
                    d_qk[:, k_lanes] = dk
                    d_qk[:, v_lanes] = dv
                else:
                    d_qk[:, k_lanes] += dk
                    d_qk[:, v_lanes] += dv
        if s == 0:
            for c in loads:
                c.wait()
        half = length // 2
        for b in range(length // block):
            local = pl.ds(b * block, block)
            at = pl.ds(start + b * block, block)
            qk = turn(d_qk[local, : 2 * wide], tables[0, local], tables[1, local], tables[2, local], -1.0)
            lin = jnp.concatenate([qk, d_qk[local, 2 * wide :]], axis=-1).astype(BF16)
            d_lin[at, :] = lin
            bias_grad[...] += jnp.sum(lin.astype(F32), axis=0, keepdims=True)
            d_h = dot(lin, w[...].reshape(D, 3 * wide), NT)
            n = (start + b * block) // block
            h_loads[n].wait()
            if n + 1 < N // block:
                h_loads[n + 1].start()
            sums[0:1, :] += jnp.sum(d_h * h_buf[n % 2].astype(F32), axis=0, keepdims=True)
            sums[1:2, :] += jnp.sum(d_h, axis=0, keepdims=True)
            d_h = d_h.astype(BF16)
            out = keep if b * block < half else send
            out[pl.ds(s * half + (b * block) % half, block), :] = d_h
    sums[0:1, :] = (sums[0:1, :] - vectors[1:2, :] * sums[1:2, :]) / vectors[0:1, :]


def attention_back(sc, tables, id_row, id_col, q, k, v, lse, w_out, h1, vectors, d_rows, weight):
    N, wide = q.shape
    D = w_out.shape[1]
    heads = wide // HD
    length = N // 2
    n_sr, _, _, f = weight[0][0].shape
    rows = D // (8 * n_sr)
    dims = (heads, length, N, D, [p[1:] for p in weight])
    return pl.pallas_call(
        functools.partial(attention_back_kernel, dims, d_rows),
        out_shape=[
            jax.ShapeDtypeStruct((N, 3 * wide), BF16),
            jax.ShapeDtypeStruct((1, 3 * wide), F32),
            jax.ShapeDtypeStruct((2, D), F32),
            jax.ShapeDtypeStruct((N // 2, D), BF16),
            jax.ShapeDtypeStruct((N // 2, D), BF16),
        ],
        in_specs=[SMEM] + [VMEM] * 8 + [ANY, VMEM] + [ANY] * (len(d_rows.arrays) + len(weight)),
        out_specs=[VMEM] * 5,
        scratch_shapes=[
            pltpu.VMEM((2, n_sr, 2, 2, rows, f), BF16),
            pltpu.VMEM((length, wide), BF16),
            pltpu.VMEM((length, 3 * wide), F32),
            pltpu.SemaphoreType.DMA((len(weight),)),
            pltpu.VMEM((2, h_buf_rows(length), D), BF16),
            pltpu.SemaphoreType.DMA((2,)),
        ]
        + d_rows.scratch(),
        compiler_params=params(),
        cost_estimate=cost(23),
    )(sc, tables, id_row, id_col, q, k, v, lse, w_out, h1, vectors, *d_rows.arrays, *[p[0] for p in weight])


def rows_kernel(dims, sc, h, d, *outs):
    n, two_rows = dims
    t = dot(h[...], d[...], TN).astype(BF16)
    i = pl.program_id(0)
    others, same = outs[:-1], outs[-1]
    for f in range(2):
        places = [(same, sc[1] == f)]
        for k, other in enumerate(others):
            places.append((other, (sc[1] != f) if len(others) == 1 else (sc[1] != f) & (i == k)))
        for out, here in places:

            @pl.when(here)
            def _():
                for j in range(n):
                    r = (2 * j + f) * two_rows
                    out[j * two_rows : (j + 1) * two_rows, :] = t[r : r + two_rows]


def grad_rows(sc, h, d, side, n_sr, rows, parts=2):
    N, D = h.shape
    f = d.shape[1]
    cut = D // 4
    n = n_sr // 2
    half, whole = pl.BlockSpec((cut // 2, f), lambda i, sc: (0, 0)), pl.BlockSpec((cut // 2, f), lambda i, sc: (i, 0))
    shape = lambda r: jax.ShapeDtypeStruct((r, f), BF16)
    spec = pltpu.PrefetchScalarGridSpec(
        num_scalar_prefetch=1,
        grid=(2,),
        in_specs=[
            pl.BlockSpec((N, cut), lambda i, sc: (0, (sc[0] ^ side) * 2 + i)),
            pl.BlockSpec((N, f), lambda i, sc: (0, 0)),
        ],
        out_specs=([half] * 2 if parts == 2 else [whole]) + [whole],
    )
    return pl.pallas_call(
        functools.partial(rows_kernel, (n, 2 * rows)),
        grid_spec=spec,
        out_shape=([shape(cut // 2)] * 2 if parts == 2 else [shape(cut)]) + [shape(cut)],
        compiler_params=params(),
        cost_estimate=cost(7),
    )(sc, h, d)


def slices_kernel(rows, cut, d_rows, sc, a, *refs):
    d_refs, refs = refs[: len(d_rows.arrays)], refs[len(d_rows.arrays) :]
    outs, (buf, sems) = refs[:4], refs[4:]
    i = pl.program_id(0)

    @pl.when(i == 0)
    def _():
        for c in d_rows.load(sc, d_refs, buf, sems):
            c.wait()

    d = buf[:, pl.ds(pl.multiple_of(i * cut, cut), cut)]
    t = dot(a[...], d, TN).astype(BF16)
    for n in range(4):
        for k in range(4):

            @pl.when((sc[0] == (n // 2) ^ (k // 2)) & (sc[1] == (n % 2) ^ (k % 2)))
            def _():
                outs[k][...] = t[n * rows : (n + 1) * rows]


def grad_slices(sc, a, d_rows):
    N, f = a.shape
    D = d_rows.D
    cut = D // 4
    spec = pltpu.PrefetchScalarGridSpec(
        num_scalar_prefetch=1,
        grid=(D // cut,),
        in_specs=[pl.BlockSpec((N, f), lambda i, sc: (0, 0))] + [ANY] * len(d_rows.arrays),
        out_specs=[pl.BlockSpec((f // 4, cut), lambda i, sc: (0, i))] * 4,
        scratch_shapes=d_rows.scratch(),
    )
    return pl.pallas_call(
        functools.partial(slices_kernel, f // 4, cut, d_rows),
        grid_spec=spec,
        out_shape=[jax.ShapeDtypeStruct((f // 4, D), BF16)] * 4,
        compiler_params=params(),
        cost_estimate=cost(9),
    )(sc, a, *d_rows.arrays)


def total_of(u0, u1, w0, w1):
    return jnp.concatenate([u0[...] + u1[...].astype(F32), w0[...] + w1[...].astype(F32)], axis=0)


def forward_kernel(u0, u1, w0, w1, x, vectors, x2, low):
    v = x[...].astype(F32) + total_of(u0, u1, w0, w1)
    x2[...] = v
    normed, _ = normalize(v)
    low[...] = (normed * vectors[2:3, :] + vectors[3:4, :]).astype(BF16)


def norm_step(terms, x, vectors):
    m, D = x.shape
    return pl.pallas_call(
        forward_kernel,
        out_shape=[jax.ShapeDtypeStruct((m, D), F32), jax.ShapeDtypeStruct((m, D), BF16)],
        in_specs=[VMEM] * 6,
        out_specs=[VMEM] * 2,
        compiler_params=params(),
        cost_estimate=cost(4),
    )(*terms, x, vectors)


def back_kernel(which, u0, u1, w0, w1, x, dy, vectors, grad, low, sums):
    d_h = total_of(u0, u1, w0, w1)
    normed, inv_std = normalize(x[...].astype(F32))
    total = dy[...].astype(F32) + normalize_back(d_h * vectors[which : which + 1, :], normed, inv_std)
    grad[...] = total
    low[...] = total.astype(BF16)
    sums[0:1, :] = jnp.sum(d_h * normed, axis=0, keepdims=True)
    sums[1:2, :] = jnp.sum(d_h, axis=0, keepdims=True)


def norm_step_back(terms, x, dy, vectors, which):
    m, D = x.shape
    return pl.pallas_call(
        functools.partial(back_kernel, which),
        out_shape=[
            jax.ShapeDtypeStruct((m, D), F32),
            jax.ShapeDtypeStruct((m, D), BF16),
            jax.ShapeDtypeStruct((2, D), F32),
        ],
        in_specs=[VMEM] * 7,
        out_specs=[VMEM] * 3,
        compiler_params=params(),
        cost_estimate=cost(4),
    )(*terms, x, dy, vectors)


def shards(
    inputs,
    cotangent,
    block_ids,
    ln1_gain,
    ln1_bias,
    qkv_weight,
    qkv_bias,
    out_weight,
    ln2_gain,
    ln2_bias,
    gate_weight,
    up_weight,
    down_weight,
):
    sb, sx, c, fh, fl = (lax.axis_index(a).astype(jnp.int32) for a in EVERY)
    n_sx = lax.axis_size("sx")
    sr, n_sr = sx * 2 + c, 2 * n_sx
    quad = 2 * n_sx
    n_dev = 8 * n_sr
    members = 2 * n_sr
    tok = inputs.shape[2]
    m = 2 * tok
    D = inputs.shape[3]
    length = block_ids.shape[2]
    N = 2 * length
    rows = qkv_weight.shape[0]
    ff_rows = down_weight.shape[0]
    ff = 4 * ff_rows
    heads = H // members
    wide = heads * HD
    natural = H % n_dev == 0
    sc = jnp.stack([sb, fh, fl, sx, sr])

    def pick(v, i):
        return lax.dynamic_index_in_dim(v, i, 0, keepdims=False)

    def device_of(t, a):
        return (((a // 2) * n_sr + t // 2) * 2 + a % 2) * 2 + t % 2

    def head_of(t, i):
        return device_of(t, i) if natural else t * heads + i

    qkv_plan = [
        [(0, (head_of(t, i) * 3 + part) * HD, HD) for part in range(3) for i in range(heads)]
        for t in range(members)
    ]
    gu_plan = [
        [(w, device_of(t, a) * ff_rows, ff_rows) for w in range(2) for a in range(4)]
        for t in range(members)
    ]
    head_place = {head_of(t, i): (t, i) for t in range(members) for i in range(heads)}
    qkv_back = [
        (head_place[h][0], part * wide + head_place[h][1] * HD, HD) for h in range(H) for part in range(3)
    ]
    ff_place = {device_of(t, a): (t, a) for t in range(members) for a in range(4)}
    gate_back = [(ff_place[d][0], ff_place[d][1] * ff_rows, ff_rows) for d in range(n_dev)]
    up_back = [(t, ff + b, n) for t, b, n in gate_back]

    def exchange(v):
        return lax.all_to_all(v, MEMBERS, split_axis=0, concat_axis=0, tiled=True)

    def of_rows(v):
        return v.reshape((n_sr, 2) + v.shape[1:])

    def both(bit, own, other):
        return jnp.stack([jnp.where(bit == 0, own, other), jnp.where(bit == 0, other, own)])

    my_ids = pick(block_ids, sb)
    c_of = (jnp.arange(2, dtype=jnp.int32) ^ c)[:, None, None, None]
    sx_of = (jnp.arange(n_sx, dtype=jnp.int32) ^ sx)[None, :, None, None]
    sb_of = (jnp.arange(2, dtype=jnp.int32) ^ sb)[None, None, :, None]
    pos = ((sb_of * n_sx + sx_of) * 2 + c_of) * tok + jnp.arange(tok, dtype=jnp.int32)[None, None, None, :]
    pos = pos.reshape(-1)
    half = ROT // 2
    lane = np.arange(2 * wide) % HD
    turned = lane < ROT
    frequency = np.where(turned, rope_base ** (-2.0 * (lane % half).astype(np.float32) / ROT), 0.0)
    angles = pos.astype(F32)[:, None] * jnp.asarray(frequency, F32)[None, :]
    sine = jnp.sin(angles)
    to_back = jnp.asarray(np.where(turned & (lane >= half), 1.0, 0.0), F32)
    to_front = jnp.asarray(np.where(lane < half, -1.0, 0.0), F32)
    tables = jnp.stack([jnp.cos(angles), sine * to_back, sine * to_front])

    rep = lambda v_: jnp.broadcast_to(v_[None], (quad,) + v_.shape)
    flat = lambda v_: v_.reshape(-1, v_.shape[-1])
    blocks = lambda v_: v_.reshape(2, n_sx, m, D)
    firsts = gather_rows(n_sx, m)

    def plus(a_, b_, kind=F32):
        return (a_.astype(F32) + b_.astype(F32)).astype(kind)

    vectors = [v_[None] for v_ in (ln1_gain, ln1_bias, ln2_gain, ln2_bias, qkv_bias)]
    live = Live(
        sc=sc,
        inputs=inputs,
        cotangent=cotangent,
        my_ids=my_ids,
        out_w=out_weight,
        gate_w=gate_weight,
        up_w=up_weight,
        down_w=down_weight,
    )
    half_rows = ff_rows // 32 * 16 if ff_rows % 16 == 0 else ff_rows // 2
    live.done(qkv_c=columns([qkv_weight], qkv_plan, vectors))
    give = jnp.concatenate([pick(live.inputs, 1 - sb)[0], pick(live.cotangent, 1 - sb)[0]], 0)
    live.done(
        w_qkv=of_rows(exchange(live.qkv_c)),
        got=swap_sb(give),
        out_1=swap_fh(live.out_w) if natural else live.out_w,
        out_2=swap_sb(live.out_w) if natural else live.out_w,
        ids_got=swap_fl(live.my_ids),
        gu_c=columns([live.gate_w, live.up_w], gu_plan),
        down_a=live.down_w[:half_rows],
        down_b=live.down_w[half_rows:],
        tables=tables,
    )

    own_x = jnp.concatenate([pick(live.inputs, sb)[0], live.got[:tok]], 0)
    own_dy = jnp.concatenate([pick(live.cotangent, sb)[0], live.got[tok:]], 0)
    ids = both(fl, live.my_ids, live.ids_got).reshape(2, 2, n_sx, 2, tok)
    ids = flip_if(fl, flip_if(c, flip_if(sb, ids, 1), 3), 0)
    ids = xor_order(ids, 2, sx, n_sx).transpose(0, 3, 2, 1, 4).reshape(2, length)
    live.drop("inputs", "cotangent", "got", "my_ids", "ids_got", "gate_w", "up_w", "qkv_c")
    live.done(
        qkv_1=swap_fh(live.w_qkv),
        qkv_2=swap_sb(live.w_qkv),
        w_gu=of_rows(exchange(live.gu_c)),
        own_x=own_x,
        own_dy=own_dy,
        x_first=gather_first(own_x),
        out_3=swap_sb(live.out_1) if natural else live.out_w,
        ids=ids,
        id_col=ids.reshape(N, 1),
        dy_rep=rep(own_dy),
    )

    cuts = [n_sr * n // 4 for n in (0, 1, 3, 4)]
    part = [live.w_gu[a_:b_] for a_, b_ in zip(cuts, cuts[1:])]
    if natural:
        out_own = in_order((live.out_w, live.out_1, live.out_2, live.out_3), sb, fh)
        out_own = out_own.reshape(wide, D)
    else:
        out_all = lax.all_gather(out_weight, EVERY, axis=0, tiled=True)
        out_own = lax.dynamic_slice_in_dim(out_all, (sr * 2 + fl) * wide, wide, 0)
    live.done(
        qkv_3=swap_sb(live.qkv_1),
        x_all=gather_second(live.x_first),
        gu_1=[swap_fh(part[0])],
        gu_part=part,
        out_own=out_own,
    )

    qkv = lambda: [(live.w_qkv, 0, 0), (live.qkv_1, 1, 0), (live.qkv_2, 2, 0), (live.qkv_3, 3, 0)]
    h1, q, k, v, o, lse, keep, send, vectors = attention(
        live.sc,
        Rows(live.x_all, firsts),
        live.tables,
        live.ids,
        live.id_col,
        live.out_own,
        qkv(),
        heads,
        rows,
    )
    live.drop("x_first", "x_all", "out_w", "out_1", "out_2", "out_3", "gu_c")
    live.done(
        h1=h1,
        q=q,
        k=k,
        v=v,
        o=o,
        lse=lse,
        keep=keep,
        send=send,
        vectors=vectors,
        gu_1=live.gu_1 + [swap_fh(live.gu_part[1])],
        gu_2=swap_sb(live.w_gu),
        dy_mine=flat(over_quad(live.dy_rep)),
    )
    live.drop("dy_rep")

    live.done(got=swap_c(live.send), dy_other=swap_c(live.dy_mine))
    send_x, send_l, keep_x, keep_l = add_first(blocks(live.keep), blocks(live.got))
    live.done(
        keep=(keep_x, keep_l),
        got=(swap_sx(send_x), swap_fl(send_l)),
        gu_1=live.gu_1 + [swap_fh(live.gu_part[2])],
        gu_3=[swap_sb(v_) for v_ in live.gu_1],
    )
    send_x, send_l, keep_x, keep_l = add_second(live.keep[0], live.got[0], live.keep[1], live.got[1])
    live.done(
        keep=(keep_x, keep_l),
        got=(swap_fl(send_x), swap_sx(send_l)),
        down_1b=swap_fh(live.down_b),
        down_2=swap_sb(live.down_w),
        gu_3=live.gu_3 + [swap_sb(live.gu_1[2])],
    )
    terms = (live.keep[0], live.got[0], live.keep[1], live.got[1])
    x2_own, h2_own = norm_step(terms, live.own_x, live.vectors)
    live.done(
        x2_own=x2_own,
        h2_first=gather_first(h2_own),
        down_3b=swap_sb(live.down_1b),
        down_1a=swap_fh(live.down_a),
    )
    live.done(h2_all=gather_second(live.h2_first), down_3a=swap_sb(live.down_1a))

    down = [live.down_w, live.down_1a, live.down_1b, live.down_2, live.down_3a, live.down_3b]
    down_places = [(0, 0), (1, 0), (1, half_rows), (2, 0), (3, 0), (3, half_rows)]
    if ff_rows % 16 != 0:
        down = [live.down_w, jnp.concatenate(down[1:3], 0), live.down_2, jnp.concatenate(down[4:6], 0)]
        down, down_places = [in_order(down, sb, fh).reshape(ff, D)], [(0, 0)]
    gu = [(live.w_gu, 0, 0), (live.gu_2, 2, 0)]
    gu += [(v_, 1, n) for n, v_ in zip(cuts, live.gu_1)] + [(v_, 3, n) for n, v_ in zip(cuts, live.gu_3)]
    h2, act, d_gu, keep, send = ffn(
        live.sc,
        Rows(live.h2_all, firsts),
        Quads(live.dy_mine, live.dy_other, m),
        gu,
        down,
        down_places,
        rows,
    )
    live.drop("w_gu", "gu_1", "gu_2", "gu_3", "gu_part", "down_a", "down_b", "down_w")
    live.drop("down_1a", "down_1b", "down_2", "down_3a", "down_3b")
    live.drop("h2_first", "h2_all")

    def give_back(v_):
        other = swap_sb(v_[tok:])
        first = jnp.where(sb == 0, v_[:tok], other)
        second = jnp.where(sb == 0, other, v_[:tok])
        return jnp.stack([first, second])[:, None]

    live.done(
        h2=h2,
        act=act,
        d_gu=d_gu,
        down=down,
        keep=keep,
        got=swap_c(send),
        gu_t=grad_rows(live.sc, h2, d_gu, 1, n_sr, rows),
    )
    send_x, send_l, keep_x, keep_l = add_first(blocks(live.keep), blocks(live.got))
    y_keep, y_send = down_product(live.sc, live.act, live.down, down_places)
    live.drop("down")
    live.done(
        keep=(keep_x, keep_l),
        got=(swap_sx(send_x), swap_fl(send_l)),
        gu_got1=swap_sb(live.gu_t[0]),
        gu_m=grad_rows(live.sc, live.h2, live.d_gu, 0, n_sr, rows),
        y_keep=y_keep,
        y_send=y_send,
    )
    live.drop("h2", "d_gu")
    send_x, send_l, keep_x, keep_l = add_second(live.keep[0], live.got[0], live.keep[1], live.got[1])
    halves = lambda v_: (v_[: v_.shape[0] // 2], v_[v_.shape[0] // 2 :])
    gu_give = [plus(a_, b_, BF16) for a_, b_ in zip(halves(live.gu_m[0]), halves(live.gu_got1))]
    live.done(
        keep=(keep_x, keep_l),
        got=(swap_fl(send_x), swap_sx(send_l)),
        gu_got1=swap_sb(live.gu_t[1]),
        gu_over=[swap_fh(gu_give[0])],
        gu_give=gu_give[1],
        down_t=grad_slices(live.sc, live.act, Quads(live.dy_mine, live.dy_other, m)),
        y_got=swap_c(live.y_send),
    )
    live.drop("dy_mine", "dy_other", "act", "y_send")
    terms = (live.keep[0], live.got[0], live.keep[1], live.got[1])
    d_x2, d_att, sums2 = norm_step_back(terms, live.x2_own, live.own_dy, live.vectors, 2)
    gu_give = [plus(a_, b_, BF16) for a_, b_ in zip(halves(live.gu_m[1]), halves(live.gu_got1))]
    live.done(
        d_x2=d_x2,
        sums2=sums2,
        att_first=gather_first(d_att),
        gu_over=live.gu_over + [swap_fh(live.gu_give)],
        gu_give=gu_give,
        down_got1=swap_sb(live.down_t[3]),
        y_sum=plus(live.y_keep, live.y_got, BF16),
    )
    live.drop("gu_got1", "y_keep", "y_got")
    down_cut = live.down_t[1].shape[0] // 32 * 16
    down_give = plus(live.down_t[1], live.down_got1, BF16)
    live.done(
        att_all=gather_second(live.att_first),
        gu_over=live.gu_over + [swap_fh(live.gu_give[0])],
        down_got0=swap_sb(live.down_t[2]),
        down_give=(down_give[:down_cut], down_give[down_cut:]),
    )
    live.drop("att_first")
    d_lin, bias_term, sums1, keep, send = attention_back(
        live.sc,
        live.tables,
        live.ids,
        live.id_col,
        live.q,
        live.k,
        live.v,
        live.lse,
        live.out_own,
        live.h1,
        live.vectors,
        Rows(live.att_all, firsts),
        qkv(),
    )
    live.drop("q", "k", "v", "lse", "out_own", "w_qkv", "qkv_1", "qkv_2", "qkv_3", "tables", "ids", "id_col")
    live.done(
        d_lin=d_lin,
        bias_term=bias_term,
        sums1=sums1,
        keep=keep,
        send=send,
        y_terms=over_quad(live.y_sum.reshape(quad, m, D)),
        gu_got0=swap_sb(live.gu_t[2]),
        gu_over=live.gu_over + [swap_fh(live.gu_give[1])],
    )
    live.drop("gu_give", "y_sum", "down_got1", "gu_t")
    live.done(
        got=swap_c(live.send),
        qkv_t=grad_rows(live.sc, live.h1, live.d_lin, 1, n_sr, rows, 1),
    )
    live.drop("send")

    def half_sum(v_, bit, swap):
        n = v_.shape[1] // 2
        take = lambda k: lax.dynamic_slice_in_dim(v_, k * n, n, 1)
        return take(bit) + swap(take(1 - bit))

    bias_term = live.bias_term.reshape(3, heads, HD).transpose(1, 0, 2)
    if natural:
        bias_term = bias_term.reshape(2, 1, 2, 1, -1)
        here = jnp.arange(n_sr)[None, :, None, None, None] == sr
        here = here & (jnp.arange(2)[None, None, None, :, None] == fl)
    else:
        bias_term = bias_term[None]
        here = jnp.arange(members)[:, None, None, None] == sr * 2 + fl
    bias_term = jnp.where(here, bias_term, 0.0).reshape(n_dev, 3, rows).transpose(1, 0, 2).reshape(3, D)
    gu_sum = plus(live.gu_m[2], live.gu_got0) + jnp.concatenate(live.gu_over, 0).astype(F32)
    send_x, send_l, keep_x, keep_l = add_first(blocks(live.keep), blocks(live.got))
    live.done(
        keep=(keep_x, keep_l),
        got=(swap_sx(send_x), swap_fl(send_l)),
        qkv_got1=swap_sb(live.qkv_t[0]),
        down_over=[swap_fh(live.down_give[1])],
        down_give=live.down_give[0],
        qkv_m=grad_rows(live.sc, live.h1, live.d_lin, 0, n_sr, rows, 1),
        gu_sum=gu_sum.astype(BF16),
        small=jnp.concatenate([live.sums1, live.sums2, bias_term], axis=0),
        out_t=grad_slices(live.sc, live.o, Rows(live.att_all, firsts)) if natural else (),
    )
    live.drop("h1", "d_lin", "gu_m", "gu_got0", "gu_over")
    send_x, send_l, keep_x, keep_l = add_second(live.keep[0], live.got[0], live.keep[1], live.got[1])
    qkv_give = [plus(a_, b_, BF16) for a_, b_ in zip(halves(live.qkv_m[0]), halves(live.qkv_got1))]
    live.done(
        keep=(keep_x, keep_l),
        got=(swap_fl(send_x), swap_sx(send_l)),
        qkv_got0=swap_sb(live.qkv_t[1]),
        qkv_over=[swap_fh(qkv_give[0])],
        qkv_give=qkv_give[1],
        small=half_sum(live.small, sb, swap_sb),
    )
    live.drop("qkv_t", "qkv_got1")
    terms = (live.keep[0], live.got[0], live.keep[1], live.got[1])
    _, input_low, _ = norm_step_back(terms, live.own_x, live.d_x2, live.vectors, 0)
    y = live.x2_own + jnp.sum(live.y_terms.astype(F32), axis=0)
    small = live.small
    bit = n_sx // 2
    while bit >= 1:
        small = half_sum(small, (sx // bit) % 2, functools.partial(swap_sx, bit=bit))
        bit //= 2
    live.done(
        input_low=input_low,
        small=half_sum(small, c, swap_c),
        qkv_over=live.qkv_over + [swap_fh(live.qkv_give)],
        out_got=[swap_sb(v_) for v_ in live.out_t[2:]],
        qkv_sum=plus(live.qkv_m[1], live.qkv_got0),
        layer_out=give_back(y.astype(BF16)),
        gu_done=exchange(live.gu_sum.reshape(members, rows, -1)),
    )
    live.drop("y_terms", "gu_sum")
    live.done(qkv_sum=(live.qkv_sum + jnp.concatenate(live.qkv_over, 0).astype(F32)).astype(BF16))
    if natural:
        out_over = swap_fh(plus(live.out_t[1], live.out_got[1], BF16))
    else:
        d_att = jnp.zeros((N, D), BF16)
        for v_, r in zip(live.att_all, firsts):
            d_att = lax.dynamic_update_slice_in_dim(d_att, v_, r, 0)
        t = lax.dot_general(live.o, d_att, TN, preferred_element_type=F32)
        t = jnp.where(jnp.arange(members)[:, None, None] == sr * 2 + fl, t[None], 0.0)
        out_over = lax.psum_scatter(t.reshape(H * HD, D), EVERY, scatter_dimension=0, tiled=True)
    live.done(
        qkv_done=exchange(live.qkv_sum.reshape(members, rows, -1)),
        out_over=out_over,
        small=half_sum(live.small, fh, swap_fh),
        down_over=[swap_fh(live.down_give)] + live.down_over,
        input_grad=give_back(live.input_low),
        gate_grad=uncolumns([live.gu_done], gate_back),
        up_grad=uncolumns([live.gu_done], up_back),
    )
    small = half_sum(live.small, fl, swap_fl)
    qkv_grad = uncolumns([live.qkv_done], qkv_back)
    out_grad = live.out_over
    if natural:
        out_grad = plus(live.out_t[0], live.out_got[0]) + out_grad.astype(F32)
    input_grad, layer_out = live.input_grad, live.layer_out
    down_grad = plus(live.down_t[0], live.down_got0) + jnp.concatenate(live.down_over, 0).astype(F32)
    gate_grad, up_grad = live.gate_grad, live.up_grad
    gain1_grad, bias1_grad, gain2_grad, bias2_grad = (small[n] for n in range(4))
    bias_grad = small[4:].reshape(-1)
    return (
        layer_out,
        input_grad,
        gain1_grad,
        bias1_grad,
        qkv_grad,
        bias_grad,
        out_grad,
        gain2_grad,
        bias2_grad,
        gate_grad,
        up_grad,
        down_grad,
    )


def solution(mesh):
    names = dict(mesh.shape)
    n_seq, n_fsdp = names["seq"], names["fsdp"]
    fine = Mesh(mesh.devices.reshape(2, n_seq // 4, 2, 2, n_fsdp // 2), EVERY)
    tokens = P(None, ("fh", "fl"), ("sb", "sx", "c"), None)
    vector = P(EVERY)
    matrix = P(EVERY, None)
    in_specs = (tokens, tokens, P(None, ("fh", "fl"), None), vector, vector, matrix, vector, matrix)
    in_specs += (vector, vector, matrix, matrix, matrix)
    out_specs = (tokens, tokens, vector, vector, matrix, vector, matrix, vector, vector)
    out_specs += (matrix, matrix, matrix)
    return jax.shard_map(shards, mesh=fine, in_specs=in_specs, out_specs=out_specs, check_vma=False)
```
